256 devices in a mesh: group: 32 (over z, x), member: 8 (over y, core).
Axes of the slice: x: 4, y: 4, z: 8, core: 2. Of those that a mesh axis runs over, the one named last changes fastest.
Arguments:
- node_latent: bfloat16 [131072, 128], P(('group', 'member')), may hold values from -6 to 6
- edge_latent: bfloat16 [786432, 128], P(('group', 'member')), may hold values from -6 to 6
- edge_src: int32 [786432], P(('group', 'member')), may hold values from 0 to 767
- edge_dst: int32 [786432], P(('group', 'member')), may hold values from 0 to 511
- edge_count: int32 [256], P(('group', 'member')), may hold values from 1536 to 3072, as said below
- halo_send: int32 [256, 2, 128], P(('group', 'member')), may hold values from 0 to 511
- halo_count: int32 [256, 2], P(('group', 'member')), may hold values from 64 to 128, as said below
- pool_index: int32 [131072], P(('group', 'member')), may hold values from 0 to 255, as said below
- coarse_src: int32 [49152], P('group'), may hold values from 0 to 511
- coarse_dst: int32 [49152], P('group'), may hold values from 0 to 255
- coarse_count: int32 [32], P('group'), may hold values from 768 to 1536, as said below
- coarse_send: int32 [32, 2, 128], P('group'), may hold values from 0 to 255
- coarse_halo_count: int32 [32, 2], P('group'), may hold values from 64 to 128, as said below
- w_edge_in: bfloat16 [384, 128], replicated, may hold values from -0.3125 to 0.3125
- w_node_in: bfloat16 [256, 128], replicated, may hold values from -0.375 to 0.375
- w_cedge_in: bfloat16 [256, 128], replicated, may hold values from -0.375 to 0.375
- w_cnode_in: bfloat16 [256, 128], replicated, may hold values from -0.375 to 0.375
- w_outs: bfloat16 [5, 128, 128], replicated, may hold values from -0.5 to 0.5
- cot_nodes: bfloat16 [131072, 128], P(('group', 'member')), may hold values from -24 to 24
- cot_edges: bfloat16 [786432, 128], P(('group', 'member')), may hold values from -6 to 6
Outputs:
- new_nodes: bfloat16 [131072, 128], P(('group', 'member'))
- new_edges: bfloat16 [786432, 128], P(('group', 'member'))
- grad_nodes: bfloat16 [131072, 128], P(('group', 'member'))
- grad_edges: bfloat16 [786432, 128], P(('group', 'member'))
- grad_edge_in: float32 [384, 128], replicated
- grad_node_in: float32 [256, 128], replicated
- grad_cedge_in: float32 [256, 128], replicated
- grad_cnode_in: float32 [256, 128], replicated
- grad_outs: float32 [5, 128, 128], replicated
The draws below stay inside these ranges and needn't reach their ends.
Inputs may be any that keep to these rules, and one draw needn't show every extreme that they name: `edge_count`: in every draw some fine partition has all 3072 edge rows live. `halo_count`: in every draw some send list is full. `pool_index`: every coarse node of a coarse partition receives at least one fine node of that partition. `coarse_count`: in every draw some coarse partition has all 1536 edge rows live. `coarse_halo_count`: in every draw some coarse send list is full.
All inputs are finite; a program needn't handle non-finite values.
Results may differ from the reference program's by a relative error of at most 0.022.
Values may be sent and summed in bfloat16 or wider, within the bound.
No kernel may reach another device: no remote copies, remote signals or barrier semaphores. Data moves between devices by JAX's collectives and lax.ppermute only.
A program may use at most 64 MiB of HBM per device.

```python
import jax
import jax.numpy as jnp
from jax import lax

L = 128
NF_DEV = 512
HALO_F = 128
HALO_C = 128
EF_DEV = 3072
NC_GRP = 256
CE_GRP = 1536
NF = 131072
EF = 786432
CE = 49152
N_GROUP = 32
N_MEMBER = 8


def ragged_counts(key, shape, most):
    values = jax.random.randint(key, shape, most // 2, most + 1).reshape(-1)
    where_full = jax.random.randint(jax.random.fold_in(key, 5), (), 0, values.shape[0])
    return values.at[where_full].set(most).reshape(shape).astype(jnp.int32)


def draw_edge_count(key, part):
    key = jax.random.fold_in(key, 11)
    return ragged_counts(key, (N_GROUP * N_MEMBER,), EF_DEV)


def draw_halo_count(key, part):
    key = jax.random.fold_in(key, 12)
    return ragged_counts(key, (N_GROUP * N_MEMBER, 2), HALO_F)


def draw_coarse_count(key, part):
    key = jax.random.fold_in(key, 13)
    return ragged_counts(key, (N_GROUP,), CE_GRP)


def draw_coarse_halo_count(key, part):
    key = jax.random.fold_in(key, 14)
    return ragged_counts(key, (N_GROUP, 2), HALO_C)


def draw_pool_index(key, part):
    key = jax.random.fold_in(key, 15)
    group_rows = N_MEMBER * NF_DEV
    random_base = jax.random.randint(key, (N_GROUP, group_rows), 0, NC_GRP)
    cover_keys = jax.random.split(jax.random.fold_in(key, 1), N_GROUP)
    covering = jax.vmap(lambda subkey: jax.random.permutation(subkey, NC_GRP))(cover_keys)
    filled = random_base.at[:, :NC_GRP].set(covering)
    order_keys = jax.random.split(jax.random.fold_in(key, 2), N_GROUP)
    shuffle_order = jax.vmap(lambda subkey: jax.random.permutation(subkey, group_rows))(order_keys)
    mixed_rows = jnp.take_along_axis(filled, shuffle_order, axis=1)
    return mixed_rows.reshape(N_GROUP * group_rows).astype(jnp.int32)


def with_ends(result, stream_key, least, high):
    longest = result.shape.index(max(result.shape))
    spots = []
    for shift in (0, 1):
        where = [jax.random.randint(jax.random.fold_in(stream_key, axis), (), 0, length) for axis, length in enumerate(result.shape)]
        where[longest] = (where[longest] + shift) % result.shape[longest]
        spots.append(tuple(where))
    return result.at[spots[0]].set(least).at[spots[1]].set(high)


def with_spikes(entries, key, source, target, parts, factor):
    def block_of(position):
        return (jnp.arange(entries.shape[position]) // (entries.shape[position] // parts)).reshape((-1,) + (1,) * (entries.ndim - 1 - position))

    first = jax.random.permutation(key, parts)[block_of(target)]
    second = (block_of(target) + parts // 2) % parts
    return jnp.where((block_of(source) == first) | (block_of(source) == second), factor * entries, entries)


def shard_levels(rng, extent, cuts, low, high):
    loudness = 1.0
    for axis_at, parts in cuts:
        steps = jax.random.uniform(jax.random.fold_in(jax.random.fold_in(rng, 6), axis_at), (parts,), jnp.float32, low / len(cuts), high / len(cuts))
        loudness = loudness * jnp.repeat(jnp.exp(steps), extent[axis_at] // parts).reshape((-1,) + (1,) * (len(extent) - 1 - axis_at))
    return loudness


def noise(rng, shape, scale, limit, cuts=(), kind=jnp.bfloat16):
    result = jax.random.normal(rng, shape, jnp.float32) * scale
    if len(cuts) > 0:
        result = shard_levels(rng, shape, cuts, -0.22, 0.18) * result
    return jnp.clip(result, min=-limit, max=limit).astype(kind)


def gaussian_with(own_key, shape, scale, reach, cuts, heavy, held_as=jnp.bfloat16):
    entries = scale * jax.random.normal(own_key, shape, jnp.float32)
    if cuts:
        entries = entries * shard_levels(own_key, shape, cuts, -0.22, 0.18)
    return jnp.clip(with_spikes(entries, jax.random.fold_in(own_key, 3), *heavy), -reach, reach).astype(held_as)


def setup_inputs(seed: int = 0) -> dict:
    splits = jax.random.split(jax.random.key(seed), 21)
    return {
        "node_latent": noise(splits[0], (NF, L), 1.0, 6.0, ((0, 256),)),
        "edge_latent": noise(splits[1], (EF, L), 1.0, 6.0, ((0, 256),)),
        "edge_src": with_ends(jax.random.randint(splits[2], (EF,), 0, NF_DEV + 2 * HALO_F), jax.random.fold_in(splits[2], 1), 0, (NF_DEV + 2 * HALO_F) - 1).astype(jnp.int32),
        "edge_dst": with_ends(jax.random.randint(splits[3], (EF,), 0, NF_DEV), jax.random.fold_in(splits[3], 1), 0, NF_DEV - 1).astype(jnp.int32),
        "edge_count": draw_edge_count(jax.random.fold_in(splits[20], 71), 0),
        "halo_send": with_ends(jax.random.randint(splits[5], (NF // NF_DEV, 2, HALO_F), 0, NF_DEV), jax.random.fold_in(splits[5], 1), 0, NF_DEV - 1).astype(jnp.int32),
        "halo_count": draw_halo_count(jax.random.fold_in(splits[20], 71), 0),
        "pool_index": draw_pool_index(jax.random.fold_in(splits[20], 71), 0),
        "coarse_src": with_ends(jax.random.randint(splits[8], (CE,), 0, NC_GRP + 2 * HALO_C), jax.random.fold_in(splits[8], 1), 0, (NC_GRP + 2 * HALO_C) - 1).astype(jnp.int32),
        "coarse_dst": with_ends(jax.random.randint(splits[9], (CE,), 0, NC_GRP), jax.random.fold_in(splits[9], 1), 0, NC_GRP - 1).astype(jnp.int32),
        "coarse_count": draw_coarse_count(jax.random.fold_in(splits[20], 71), 0),
        "coarse_send": with_ends(jax.random.randint(splits[11], (N_GROUP, 2, HALO_C), 0, NC_GRP), jax.random.fold_in(splits[11], 1), 0, NC_GRP - 1).astype(jnp.int32),
        "coarse_halo_count": draw_coarse_halo_count(jax.random.fold_in(splits[20], 71), 0),
        "w_edge_in": noise(splits[13], (3 * L, L), (3 * L) ** -0.5, 0.3125),
        "w_node_in": noise(splits[14], (2 * L, L), (2 * L) ** -0.5, 0.375),
        "w_cedge_in": noise(splits[15], (2 * L, L), (2 * L) ** -0.5, 0.375),
        "w_cnode_in": noise(splits[16], (2 * L, L), (2 * L) ** -0.5, 0.375),
        "w_outs": noise(splits[17], (5, L, L), L ** -0.5, 0.5),
        "cot_nodes": gaussian_with(splits[18], (NF, L), 1.0, 24.0, ((0, 256),), (0, 1, 128, 5.5)),
        "cot_edges": noise(splits[19], (EF, L), 1.0, 6.0, ((0, 256),)),
    }


eps = 1e-05

def widen(values):
    return lax.optimization_barrier(values).astype(jnp.float32)

def rounded(values):
    return widen(values.astype(jnp.bfloat16))

def segment_total(values, indices, row_count):
    return jax.ops.segment_sum(values, indices, num_segments=row_count)

def silu_slope(pre_act):
    sigmoid = jax.nn.sigmoid(pre_act)
    return sigmoid * (1.0 + pre_act * (1.0 - sigmoid))

def mlp_forward(inputs, w_first, w_second):
    pre_act = jnp.dot(inputs, w_first, preferred_element_type=jnp.float32)
    hidden = (pre_act * jax.nn.sigmoid(pre_act)).astype(jnp.bfloat16)
    outcome = jnp.dot(hidden, w_second, preferred_element_type=jnp.float32)
    centred = outcome - lax.optimization_barrier(jnp.mean(outcome, axis=-1, keepdims=True))
    inv_scale = lax.rsqrt(lax.optimization_barrier(jnp.mean(centred * centred, axis=-1, keepdims=True)) + eps)
    normed = centred * inv_scale
    return (normed, (pre_act, hidden, normed, inv_scale))

def mlp_backward(grad_out, inputs, w_first, w_second, stored):
    pre_act, hidden, normed, inv_scale = stored
    grad_raw = inv_scale * (grad_out - lax.optimization_barrier(jnp.mean(grad_out, axis=-1, keepdims=True)) - normed * lax.optimization_barrier(jnp.mean(grad_out * normed, axis=-1, keepdims=True)))
    grad_raw = grad_raw.astype(jnp.bfloat16)
    grad_second = jnp.dot(hidden.T, grad_raw, preferred_element_type=jnp.float32)
    grad_hidden = jnp.dot(grad_raw, w_second.T, preferred_element_type=jnp.float32)
    grad_pre = (grad_hidden * silu_slope(pre_act)).astype(jnp.bfloat16)
    grad_first = jnp.dot(inputs.T, grad_pre, preferred_element_type=jnp.float32)
    grad_inputs = jnp.dot(grad_pre, w_first.T, preferred_element_type=jnp.float32)
    return (grad_inputs, grad_first, grad_second)

def pick_rows(source_rows, send_rows, live_count):
    slot_mask = (jnp.arange(send_rows.shape[-1])[None, :] < live_count[:, None]).astype(source_rows.dtype)
    return source_rows[send_rows] * slot_mask[:, :, None]

def extend_all(source_rows, send_rows, live_count):
    sent = jax.vmap(pick_rows)(source_rows, send_rows, live_count)
    empty_rows = jnp.zeros((1,) + sent.shape[2:], source_rows.dtype)
    from_prev = jnp.concatenate([empty_rows, sent[:-1, 1]], 0)
    from_next = jnp.concatenate([sent[1:, 0], empty_rows], 0)
    return jnp.concatenate([source_rows, from_prev, from_next], 1)

def return_all(grad_ext, send_rows, live_count, row_count):
    slot_width = send_rows.shape[-1]
    prev_slots = grad_ext[:, row_count:row_count + slot_width]
    next_slots = grad_ext[:, row_count + slot_width:]
    empty_rows = jnp.zeros((1,) + prev_slots.shape[1:], jnp.float32)
    first_back = jnp.concatenate([empty_rows, next_slots[:-1]], 0)
    second_back = jnp.concatenate([prev_slots[1:], empty_rows], 0)
    slot_mask = (jnp.arange(slot_width)[None, None, :] < live_count[:, :, None]).astype(jnp.float32)
    returned = jnp.stack([first_back, second_back], 1) * slot_mask[..., None]

    def scatter_back(values, indices):
        return segment_total(values.reshape(2 * slot_width, -1), indices.reshape(2 * slot_width), row_count)
    return jax.vmap(scatter_back)(returned, send_rows)

def edge_section(extended, node_rows, edge_rows, sources, targets, live_count, w_first, w_second):
    inputs = jnp.concatenate([edge_rows, extended[sources], node_rows[targets]], 1)
    message, stored = mlp_forward(inputs, w_first, w_second)
    valid_rows = (jnp.arange(edge_rows.shape[0]) < live_count).astype(jnp.float32)[:, None]
    new_rows = (edge_rows.astype(jnp.float32) + valid_rows * message).astype(jnp.bfloat16)
    aggregate = segment_total(widen(new_rows) * valid_rows, targets, node_rows.shape[0]).astype(jnp.bfloat16)
    return (inputs, stored, valid_rows, new_rows, aggregate)

def coarse_section(extended, latents, sources, targets, valid_rows, w_first, w_second, row_count):
    inputs = jnp.concatenate([extended[sources], latents[targets]], 1)
    message, stored = mlp_forward(inputs, w_first, w_second)
    partial_value = segment_total(message * valid_rows, targets, row_count)
    return (inputs, stored, partial_value)

def reference(node_latent, edge_latent, edge_src, edge_dst, edge_count, halo_send, halo_count, pool_index, coarse_src, coarse_dst, coarse_count, coarse_send, coarse_halo_count, w_edge_in, w_node_in, w_cedge_in, w_cnode_in, w_outs, cot_nodes, cot_edges):
    partitions = N_GROUP * N_MEMBER
    node_parts = node_latent.reshape(partitions, NF_DEV, L)
    edge_parts = edge_latent.reshape(partitions, EF_DEV, L)
    src_parts = edge_src.reshape(partitions, EF_DEV)
    dst_parts = edge_dst.reshape(partitions, EF_DEV)
    cot_parts = cot_edges.reshape(partitions, EF_DEV, L)
    extended = extend_all(node_parts, halo_send, halo_count)

    def forward_part(pieces):
        ext_p, node_p, edge_p, src_p, dst_p, count_p = pieces
        outcome = edge_section(ext_p, node_p, edge_p, src_p, dst_p, count_p, w_edge_in, w_outs[0])
        return (outcome[3], outcome[4])
    new_edge_parts, aggregate = lax.map(forward_part, (extended, node_parts, edge_parts, src_parts, dst_parts, edge_count))
    node_in = jnp.concatenate([node_parts, aggregate], 2)
    update, stored_node = jax.vmap(mlp_forward, (0, None, None))(node_in, w_node_in, w_outs[1])
    refined = (node_parts.astype(jnp.float32) + update).astype(jnp.bfloat16)
    refined_groups = widen(refined).reshape(N_GROUP, N_MEMBER * NF_DEV, L)
    pool_groups = pool_index.reshape(N_GROUP, N_MEMBER * NF_DEV)
    totals = jax.vmap(lambda values, indices: segment_total(values, indices, NC_GRP))(refined_groups, pool_groups)
    counts = jax.vmap(lambda indices: segment_total(jnp.ones(indices.shape, jnp.float32), indices, NC_GRP))(pool_groups)
    restricted = (totals / counts[..., None]).astype(jnp.bfloat16)
    coarse_ext = extend_all(restricted, coarse_send, coarse_halo_count)
    csrc_groups = coarse_src.reshape(N_GROUP, CE_GRP)
    cdst_groups = coarse_dst.reshape(N_GROUP, CE_GRP)
    coarse_valid = (jnp.arange(CE_GRP)[None, :] < coarse_count[:, None]).astype(jnp.float32)[..., None]

    def coarse_group(ext_g, latent_g, src_g, dst_g, valid_g):
        return coarse_section(ext_g, latent_g, src_g, dst_g, valid_g, w_cedge_in, w_outs[2], NC_GRP)
    coarse_in, stored_coarse, partial_value = jax.vmap(coarse_group)(coarse_ext, restricted, csrc_groups, cdst_groups, coarse_valid)
    coarse_agg = partial_value.astype(jnp.bfloat16)
    coarse_node_in = jnp.concatenate([restricted, coarse_agg], 2)
    coarse_update, stored_cnode = jax.vmap(mlp_forward, (0, None, None))(coarse_node_in, w_cnode_in, w_outs[3])
    coarse_latent = (restricted.astype(jnp.float32) + coarse_update).astype(jnp.bfloat16)
    lifted = jax.vmap(lambda latents, indices: latents[indices])(coarse_latent, pool_groups).reshape(NF, L)
    refined_flat = refined_groups.reshape(NF, L)
    new_nodes = (refined_flat + jnp.dot(lifted, w_outs[4], preferred_element_type=jnp.float32)).astype(jnp.bfloat16)
    grad_lift_w = jnp.dot(lifted.T, cot_nodes, preferred_element_type=jnp.float32)
    grad_lifted = jnp.dot(cot_nodes, w_outs[4].T, preferred_element_type=jnp.float32).reshape(N_GROUP, N_MEMBER * NF_DEV, L)
    grad_coarse = rounded(jax.vmap(lambda values, indices: segment_total(values, indices, NC_GRP))(grad_lifted, pool_groups))
    grad_cnode_x, grad_cnode_first, grad_cnode_second = jax.vmap(mlp_backward, (0, 0, None, None, 0))(grad_coarse, coarse_node_in, w_cnode_in, w_outs[3], stored_cnode)
    grad_agg = rounded(grad_cnode_x[..., L:])
    grad_message = jax.vmap(lambda values, indices: values[indices])(grad_agg, cdst_groups) * coarse_valid
    grad_cin, grad_cedge_first, grad_cedge_second = jax.vmap(mlp_backward, (0, 0, None, None, 0))(grad_message, coarse_in, w_cedge_in, w_outs[2], stored_coarse)
    grad_cext = jax.vmap(lambda values, indices: segment_total(values, indices, NC_GRP + 2 * HALO_C))(grad_cin[..., :L], csrc_groups)
    grad_targets = jax.vmap(lambda values, indices: segment_total(values, indices, NC_GRP))(grad_cin[..., L:], cdst_groups)
    grad_latent = grad_coarse + grad_cnode_x[..., :L] + grad_targets + grad_cext[:, :NC_GRP] + return_all(grad_cext, coarse_send, coarse_halo_count, NC_GRP)
    grad_pool = rounded(grad_latent) / counts[..., None]
    grad_pooled = jax.vmap(lambda values, indices: values[indices])(grad_pool, pool_groups)
    grad_refined = rounded(cot_nodes.astype(jnp.float32).reshape(N_GROUP, N_MEMBER * NF_DEV, L) + grad_pooled)
    grad_refined = grad_refined.reshape(partitions, NF_DEV, L)
    grad_node_x, grad_node_first, grad_node_second = jax.vmap(mlp_backward, (0, 0, None, None, 0))(grad_refined, node_in, w_node_in, w_outs[1], stored_node)
    grad_aggregate = rounded(grad_node_x[..., L:])

    def backward_part(pieces):
        ext_p, node_p, edge_p, src_p, dst_p, count_p, cot_p, agg_p = pieces
        inputs, stored, valid_rows, _, _ = edge_section(ext_p, node_p, edge_p, src_p, dst_p, count_p, w_edge_in, w_outs[0])
        grad_new = rounded(cot_p.astype(jnp.float32) + valid_rows * agg_p[dst_p])
        grad_inputs, grad_first, grad_second = mlp_backward(grad_new * valid_rows, inputs, w_edge_in, w_outs[0], stored)
        grad_edge_p = (grad_new + grad_inputs[:, :L]).astype(jnp.bfloat16)
        grad_ext_p = segment_total(grad_inputs[:, L:2 * L], src_p, NF_DEV + 2 * HALO_F)
        grad_dst_p = segment_total(grad_inputs[:, 2 * L:], dst_p, NF_DEV)
        return (grad_edge_p, grad_ext_p, grad_dst_p, grad_first, grad_second)
    grad_edge_parts, grad_ext, grad_dst, grad_edge_first, grad_edge_second = lax.map(backward_part, (extended, node_parts, edge_parts, src_parts, dst_parts, edge_count, cot_parts, grad_aggregate))
    grad_total = grad_refined + grad_node_x[..., :L] + grad_dst + grad_ext[:, :NF_DEV] + return_all(grad_ext, halo_send, halo_count, NF_DEV)
    grad_outs = jnp.stack([lax.optimization_barrier(jnp.sum(grad_edge_second, 0)), lax.optimization_barrier(jnp.sum(grad_node_second, 0)), lax.optimization_barrier(jnp.sum(grad_cedge_second, 0)), lax.optimization_barrier(jnp.sum(grad_cnode_second, 0)), grad_lift_w])
    return (new_nodes, new_edge_parts.reshape(EF, L), grad_total.astype(jnp.bfloat16).reshape(NF, L), grad_edge_parts.reshape(EF, L), lax.optimization_barrier(jnp.sum(grad_edge_first, 0)), lax.optimization_barrier(jnp.sum(grad_node_first, 0)), lax.optimization_barrier(jnp.sum(grad_cedge_first, 0)), lax.optimization_barrier(jnp.sum(grad_cnode_first, 0)), grad_outs)
```

```python
import functools

import jax
import jax.numpy as jnp
from jax import lax
from jax.experimental import pallas as pl
from jax.experimental.pallas import tpu as pltpu
from jax.sharding import Mesh
from jax.sharding import PartitionSpec as P

F32 = jnp.float32
BF = jnp.bfloat16
I32 = jnp.int32
EPS = 1e-05

L = 128
NF = 512
EF = 3072
NC = 256
EC = 1536
SLOT = 128
BLK = 4
CNT = 16
GRADS = 1792
ROWS_EDGE, ROWS_NODE, ROWS_CEDGE, ROWS_CNODE, ROWS_OUTS = 0, 384, 640, 896, 1152

EVERY = ("z", "x", "y", "c")
GROUP = ("z", "x")
PLANE = ("x", "y", "c")

VMEM = pl.BlockSpec(memory_space=pltpu.VMEM)
SMEM = pl.BlockSpec(memory_space=pltpu.SMEM)


def call(kernel, name, out_shape, ins, specs, flops=10**9):
    size = sum(a.size * a.dtype.itemsize for a in ins)
    return pl.pallas_call(
        kernel,
        name=name,
        out_shape=out_shape,
        in_specs=specs,
        out_specs=jax.tree.map(lambda _: VMEM, out_shape),
        cost_estimate=pl.CostEstimate(flops=flops, bytes_accessed=size, transcendentals=0),
        compiler_params=pltpu.CompilerParams(vmem_limit_bytes=48 * 2**20),
    )(*ins)


def shape(*dims, dtype=BF):
    return jax.ShapeDtypeStruct(dims, dtype)


def dot(a, b):
    return jnp.dot(a, b, preferred_element_type=F32)


def dot_nt(a, b):
    return lax.dot_general(a, b, (((1,), (1,)), ((), ())), preferred_element_type=F32)


def dot_tn(a, b):
    return lax.dot_general(a, b, (((0,), (0,)), ((), ())), preferred_element_type=F32)


def mean(v):
    return jnp.mean(v, axis=-1, keepdims=True)


def columns(rows):
    pad = -rows.shape[0] % 8
    rows = rows.astype(F32)
    if pad:
        rows = jnp.concatenate([rows, jnp.zeros((pad, 128), F32)], 0)
    return rows.T.astype(I32)


def pick(cols, blocks, n):
    lane = lax.broadcasted_iota(I32, (128, n), 1)
    return jnp.concatenate(
        [jnp.where(lane == cols[:, j : j + 1], 1.0, 0.0).astype(BF) for j in blocks], 0
    )


def put(rows, blocks, n):
    line = lax.broadcasted_iota(I32, (n, 128), 0)
    return jnp.concatenate(
        [jnp.where(line == rows[j : j + 1, :], 1.0, 0.0).astype(BF) for j in blocks], 1
    )


def live_rows(rows, count):
    at = lax.broadcasted_iota(I32, rows.shape, 0) * 128 + lax.broadcasted_iota(I32, rows.shape, 1)
    return jnp.where(at < count, rows, -1)


def live_slots(send, counts):
    lane = lax.broadcasted_iota(I32, (1, SLOT), 1)
    return jnp.concatenate(
        [jnp.where(lane < counts[0, s], send[s : s + 1, :], -1) for s in (0, 1)], 0
    )


def sigmoid(a):
    return 1.0 / (1.0 + jnp.exp(-a))


def normed_of(hidden, w_second):
    outcome = dot(hidden, w_second)
    centred = outcome - mean(outcome)
    inv = lax.rsqrt(mean(centred * centred) + EPS)
    return centred * inv, inv


def forward(a, w_second):
    hidden = (a * sigmoid(a)).astype(BF)
    return normed_of(hidden, w_second)[0]


def backward(grad, a, w_second):
    sig = sigmoid(a)
    hidden = (a * sig).astype(BF)
    normed, inv = normed_of(hidden, w_second)
    go = (inv * (grad - mean(grad) - normed * mean(grad * normed))).astype(BF)
    gu = dot_nt(go, w_second)
    ga = (gu * (sig * (1.0 + a * (1.0 - sig)))).astype(BF)
    return go, hidden, ga


def send_kernel(node, send, counts, to_prev, to_next):
    cols = columns(live_slots(send[...], counts))
    rows = node[...]
    to_prev[...] = dot(pick(cols, (0,), NF), rows).astype(BF)
    to_next[...] = dot(pick(cols, (1,), NF), rows).astype(BF)


def pre_kernel(edge, node, src, dst, w_in, pool, cot, pre, side):
    w = w_in[...]
    rows = node[...]
    table = jnp.concatenate([dot(rows, w[256:384]), dot(rows, w[128:256])], 0).astype(BF)
    src_cols, dst_cols = columns(src[...]), columns(dst[...])
    for c in range(EF // 128 // BLK):
        blocks = range(c * BLK, (c + 1) * BLK)
        at = pl.ds(c * BLK * 128, BLK * 128)
        hot = jnp.concatenate([pick(dst_cols, blocks, NF), pick(src_cols, blocks, NF)], 1)
        pre[at, :] = dot(edge[at, :], w[:128]) + dot(hot, table)
    pool_hot = put(pool[...], range(NF // 128), NC)
    side[0:NC, :] = dot(pool_hot, cot[...]).astype(BF)
    count = dot_nt(jnp.ones((8, NF), BF), pool_hot)
    high = jnp.floor(count * (1.0 / 16.0))
    low = count - 16.0 * high
    at = lax.broadcasted_iota(I32, (CNT, 128), 0)
    lines = jnp.zeros((CNT, 128), F32)
    for k, v in enumerate((high[0:1, :128], high[0:1, 128:], low[0:1, :128], low[0:1, 128:])):
        lines = jnp.where(at == k, v, lines)
    side[NC : NC + CNT, :] = lines.astype(BF)


def fine_kernel(
    live, pre, edge, node, from_prev, from_next, src, dst, w_in, w_node, w_outs, pool, side,
    new_edges, act, agg_out, act_node, refined, payload,
):
    halo = jnp.concatenate([from_prev[...], from_next[...]], 0)
    table = dot(halo, w_in[128:256, :]).astype(BF)
    src_cols = columns(src[...] - NF)
    dst_rows = live_rows(dst[...], live[0])
    w_second = w_outs[0]
    total = jnp.zeros((NF, L), F32)
    for c in range(EF // 128 // BLK):
        blocks = range(c * BLK, (c + 1) * BLK)
        at = pl.ds(c * BLK * 128, BLK * 128)
        a = pre[at, :] + dot(pick(src_cols, blocks, 2 * SLOT), table)
        act[at, :] = a
        message = forward(a, w_second)
        here = lax.broadcasted_iota(I32, message.shape, 0) + c * BLK * 128 < live[0]
        rows = (edge[at, :].astype(F32) + jnp.where(here, message, 0.0)).astype(BF)
        new_edges[at, :] = rows
        total += dot(put(dst_rows, blocks, NF), rows)
    agg = total.astype(BF)
    agg_out[...] = agg
    a = dot(node[...], w_node[:128, :]) + dot(agg, w_node[128:, :])
    act_node[...] = a
    rows = (node[...].astype(F32) + forward(a, w_outs[1])).astype(BF)
    refined[...] = rows
    payload[0:NC, :] = dot(put(pool[...], range(NF // 128), NC), rows).astype(BF)
    payload[NC:, :] = side[...]


def pair_kernel(pair, out):
    total = (pair[0].astype(F32) + pair[1].astype(F32)).astype(BF)
    for k in range(out.shape[0]):
        out[k] = total


def pool_kernel(parts, send, counts, own_out, cot_out, divisor, to_prev, to_next):
    total = parts[0].astype(F32)
    for k in range(1, parts.shape[0]):
        total += parts[k].astype(F32)
    lines = total[2 * NC :, :]
    count = 16.0 * lines[0:2, :] + lines[2:4, :]
    cols = jnp.concatenate([count, jnp.ones((6, 128), F32)], 0).T
    count = jnp.concatenate(
        [jnp.broadcast_to(cols[:, k : k + 1], (128, L)) for k in (0, 1)], 0
    )
    own = (total[:NC, :] / count).astype(BF)
    own_out[...] = own
    cot_out[...] = total[NC : 2 * NC, :].astype(BF)
    divisor[...] = count
    cols = columns(live_slots(send[...], counts))
    to_prev[...] = dot(pick(cols, (0,), NC), own).astype(BF)
    to_next[...] = dot(pick(cols, (1,), NC), own).astype(BF)


def coarse_pre_kernel(own, cot, src, dst, w_in, w_node, w_outs, pre, pre_node, grad_coarse):
    rows = own[...]
    table = jnp.concatenate([dot(rows, w_in[128:, :]), dot(rows, w_in[:128, :])], 0).astype(BF)
    src_cols, dst_cols = columns(src[...]), columns(dst[...])
    for c in range(EC // 128 // BLK):
        blocks = range(c * BLK, (c + 1) * BLK)
        hot = jnp.concatenate([pick(dst_cols, blocks, NC), pick(src_cols, blocks, NC)], 1)
        pre[pl.ds(c * BLK * 128, BLK * 128), :] = dot(hot, table)
    pre_node[...] = dot(rows, w_node[:128, :])
    grad_coarse[...] = dot_nt(cot[...], w_outs[4]).astype(BF)


def coarse_kernel(
    live, own, pre, pre_node, grad_coarse, from_prev, from_next, src, dst, w_in, w_node, w_outs,
    coarse_out, grad_own, back_prev, back_next, sums_out, seconds, ga_out, agg_out, act,
):
    halo = jnp.concatenate([from_prev[...], from_next[...]], 0)
    table = dot(halo, w_in[:128, :]).astype(BF)
    src_rows = src[...]
    src_cols = columns(src_rows - NC)
    dst_rows = live_rows(dst[...], live[0])
    dst_cols = columns(dst_rows)
    w_second = w_outs[2]
    total = jnp.zeros((NC, L), F32)
    for c in range(EC // 128 // BLK):
        blocks = range(c * BLK, (c + 1) * BLK)
        at = pl.ds(c * BLK * 128, BLK * 128)
        a = pre[at, :] + dot(pick(src_cols, blocks, 2 * SLOT), table)
        act[at, :] = a
        total += dot(put(dst_rows, blocks, NC), forward(a, w_second).astype(BF))
    agg = total.astype(BF)
    agg_out[...] = agg
    a = pre_node[...] + dot(agg, w_node[128:, :])
    rows = own[...]
    coarse_out[...] = (rows.astype(F32) + forward(a, w_outs[3])).astype(BF)
    grad = grad_coarse[...].astype(F32)
    go, hidden, ga = backward(grad, a, w_outs[3])
    ga_out[...] = ga
    seconds[1] = dot_tn(hidden, go)
    grad_total = grad + dot_nt(ga, w_node[:128, :])
    grad_agg = dot_nt(ga, w_node[128:, :]).astype(BF)
    second = jnp.zeros((L, L), F32)
    sums = jnp.zeros((NC + 2 * SLOT + NC, L), F32)
    for c in range(EC // 128 // BLK):
        blocks = range(c * BLK, (c + 1) * BLK)
        at = pl.ds(c * BLK * 128, BLK * 128)
        grad = dot(pick(dst_cols, blocks, NC), grad_agg)
        go, hidden, ga = backward(grad, act[at, :], w_second)
        second += dot_tn(hidden, go)
        hot = jnp.concatenate(
            [put(src_rows, blocks, NC + 2 * SLOT), put(dst_rows, blocks, NC)], 0
        )
        sums += dot(hot, ga)
    seconds[0] = second
    sums = sums.astype(BF)
    sums_out[...] = sums
    grad_ext = dot_nt(sums[: NC + 2 * SLOT], w_in[:128, :])
    grad_own[...] = grad_total + grad_ext[:NC] + dot_nt(sums[NC + 2 * SLOT :], w_in[128:, :])
    back_prev[...] = grad_ext[NC : NC + SLOT].astype(BF)
    back_next[...] = grad_ext[NC + SLOT :].astype(BF)


def lift_kernel(
    own, cot, from_prev, from_next, coarse, sums, seconds, ga, agg, refined, pool, w_outs,
    new_nodes, grads,
):
    part = 1.0 / 8.0
    rows = own[...]
    ext = jnp.concatenate([rows, from_prev[...], from_next[...]], 0)
    both = sums[...]
    lifted = dot(pick(columns(pool[...]), range(NF // 128), NC), coarse[...]).astype(BF)
    new_nodes[...] = (refined[...].astype(F32) + dot(lifted, w_outs[4])).astype(BF)
    grads[0:128, :] = (part * dot_tn(ext, both[: NC + 2 * SLOT])).astype(BF)
    grads[128:256, :] = (part * dot_tn(rows, both[NC + 2 * SLOT :])).astype(BF)
    grads[256:384, :] = (part * dot_tn(rows, ga[...])).astype(BF)
    grads[384:512, :] = (part * dot_tn(agg[...], ga[...])).astype(BF)
    grads[512:640, :] = (part * seconds[0]).astype(BF)
    grads[640:768, :] = (part * seconds[1]).astype(BF)
    grads[768:896, :] = (part * dot_tn(coarse[...], cot[...])).astype(BF)


def fine_back_kernel(
    live, counts, grad_own, divisor, ret_prev, ret_next, send, cot, pool, node, from_prev,
    from_next, act_node, agg, act, edge, cot_edges, src, dst, w_in, w_node, w_outs, coarse_grads,
    grad_edges, grad_node, back_prev, back_next, grads,
):
    back = jnp.concatenate([ret_prev[...], ret_next[...]], 0)
    hot = put(live_slots(send[...], counts), (0, 1), NC)
    grad_pool = (grad_own[...] + dot(hot, back)).astype(BF).astype(F32) / divisor[...]
    pooled = dot(pick(columns(pool[...]), range(NF // 128), NC), grad_pool.astype(BF))
    grad_refined = (cot[...].astype(F32) + pooled).astype(BF).astype(F32)
    go, hidden, ga = backward(grad_refined, act_node[...], w_outs[1])
    rows = node[...]
    node_first = (dot_tn(rows, ga), dot_tn(agg[...], ga))
    node_second = dot_tn(hidden, go)
    grad_total = grad_refined + dot_nt(ga, w_node[:128, :])
    grad_agg = dot_nt(ga, w_node[128:, :]).astype(BF)
    src_rows = src[...]
    dst_rows = live_rows(dst[...], live[0])
    dst_cols = columns(dst_rows)
    w_second = w_outs[0]
    first = jnp.zeros((L, L), F32)
    second = jnp.zeros((L, L), F32)
    sums = jnp.zeros((NF + 2 * SLOT + NF, L), F32)
    for c in range(EF // 128 // BLK):
        blocks = range(c * BLK, (c + 1) * BLK)
        at = pl.ds(c * BLK * 128, BLK * 128)
        gathered = dot(pick(dst_cols, blocks, NF), grad_agg)
        grad_new = (cot_edges[at, :].astype(F32) + gathered).astype(BF).astype(F32)
        here = lax.broadcasted_iota(I32, grad_new.shape, 0) + c * BLK * 128 < live[0]
        go, hidden, ga = backward(jnp.where(here, grad_new, 0.0), act[at, :], w_second)
        grad_edges[at, :] = (grad_new + dot_nt(ga, w_in[:128, :])).astype(BF)
        first += dot_tn(edge[at, :], ga)
        second += dot_tn(hidden, go)
        hot = jnp.concatenate(
            [put(src_rows, blocks, NF + 2 * SLOT), put(dst_rows, blocks, NF)], 0
        )
        sums += dot(hot, ga)
    sums = sums.astype(BF)
    grad_ext = dot_nt(sums[: NF + 2 * SLOT], w_in[128:256, :])
    grad_node[...] = grad_total + grad_ext[:NF] + dot_nt(sums[NF + 2 * SLOT :], w_in[256:, :])
    back_prev[...] = grad_ext[NF : NF + SLOT].astype(BF)
    back_next[...] = grad_ext[NF + SLOT :].astype(BF)
    ext = jnp.concatenate([rows, from_prev[...], from_next[...]], 0)
    grads[0:128, :] = first.astype(BF)
    grads[128:256, :] = dot_tn(ext, sums[: NF + 2 * SLOT]).astype(BF)
    grads[256:384, :] = dot_tn(rows, sums[NF + 2 * SLOT :]).astype(BF)
    grads[384:512, :] = node_first[0].astype(BF)
    grads[512:640, :] = node_first[1].astype(BF)
    grads[640:1152, :] = coarse_grads[0:512, :]
    grads[1152:1280, :] = second.astype(BF)
    grads[1280:1408, :] = node_second.astype(BF)
    grads[1408:1792, :] = coarse_grads[512:896, :]


def node_end_kernel(counts, grad_node, ret_prev, ret_next, send, out):
    back = jnp.concatenate([ret_prev[...], ret_next[...]], 0)
    hot = put(live_slots(send[...], counts), (0, 1), NF)
    out[...] = (grad_node[...] + dot(hot, back)).astype(BF)


def spread_kernel(parts, out):
    total = parts[0].astype(F32)
    for k in range(1, parts.shape[0]):
        total += parts[k].astype(F32)
    total = total.astype(BF)
    for k in range(out.shape[0]):
        out[k] = total


def end_kernel(rows, edge_in, node_in, cedge_in, cnode_in, outs):
    edge_in[...] = rows[ROWS_EDGE:ROWS_NODE, :].astype(F32)
    node_in[...] = rows[ROWS_NODE:ROWS_CEDGE, :].astype(F32)
    cedge_in[...] = rows[ROWS_CEDGE:ROWS_CNODE, :].astype(F32)
    cnode_in[...] = rows[ROWS_CNODE:ROWS_OUTS, :].astype(F32)
    for k in range(5):
        outs[k] = rows[ROWS_OUTS + k * 128 : ROWS_OUTS + (k + 1) * 128, :].astype(F32)


def shift(value, axes, step):
    count = lax.axis_size(axes)
    return lax.ppermute(
        value, axes, [(i, i + step) for i in range(count) if 0 <= i + step < count]
    )


def exchange(value, axes):
    return lax.all_to_all(value, axes, 0, 0)


def on_device(
    node, edge, src, dst, live, send, counts, pool, csrc, cdst, clive, csend, ccounts,
    w_edge, w_node, w_cedge, w_cnode, w_outs, cot, cot_edges,
):
    f32 = functools.partial(shape, dtype=F32)
    slots = (shape(SLOT, L), shape(SLOT, L))
    src, dst = src.reshape(EF // 128, 128), dst.reshape(EF // 128, 128)
    csrc, cdst = csrc.reshape(EC // 128, 128), cdst.reshape(EC // 128, 128)
    pool = pool.reshape(NF // 128, 128)
    send, csend = send.reshape(2, SLOT), csend.reshape(2, SLOT)

    to_prev, to_next = call(
        send_kernel, "send", slots, (node, send, counts), [VMEM, VMEM, SMEM], 10**7
    )
    from_prev, from_next = shift(to_next, EVERY, 1), shift(to_prev, EVERY, -1)
    pre, side = call(
        pre_kernel, "pre", (f32(EF, L), shape(NC + CNT, L)),
        (edge, node, src, dst, w_edge, pool, cot), [VMEM] * 7,
    )
    new_edges, act, agg, act_node, refined, payload = call(
        fine_kernel, "fine",
        (shape(EF, L), f32(EF, L), shape(NF, L), f32(NF, L), shape(NF, L), shape(2 * NC + CNT, L)),
        (live, pre, edge, node, from_prev, from_next, src, dst, w_edge, w_node, w_outs, pool, side),
        [SMEM] + [VMEM] * 12,
    )
    pair = lax.all_gather(payload, "c", axis=0, tiled=False)
    spread = call(pair_kernel, "pair", shape(4, 2 * NC + CNT, L), (pair,), [VMEM], 10**6)
    parts = exchange(spread, "y")
    own, pooled_cot, divisor, to_prev, to_next = call(
        pool_kernel, "pool", (shape(NC, L), shape(NC, L), f32(NC, L)) + slots,
        (parts, csend, ccounts), [VMEM, VMEM, SMEM], 10**7,
    )
    cfrom_prev, cfrom_next = shift(to_next, GROUP, 1), shift(to_prev, GROUP, -1)
    cpre, cpre_node, grad_coarse = call(
        coarse_pre_kernel, "coarse_pre", (f32(EC, L), f32(NC, L), shape(NC, L)),
        (own, pooled_cot, csrc, cdst, w_cedge, w_cnode, w_outs), [VMEM] * 7,
    )
    coarse, grad_own, back_prev, back_next, sums, seconds, cga, cagg, _ = call(
        coarse_kernel, "coarse",
        (shape(NC, L), f32(NC, L)) + slots
        + (shape(2 * NC + 2 * SLOT, L), f32(2, L, L), shape(NC, L), shape(NC, L), f32(EC, L)),
        (clive, own, cpre, cpre_node, grad_coarse, cfrom_prev, cfrom_next, csrc, cdst,
         w_cedge, w_cnode, w_outs),
        [SMEM] + [VMEM] * 11,
    )
    cret_prev, cret_next = shift(back_next, GROUP, 1), shift(back_prev, GROUP, -1)
    new_nodes, coarse_grads = call(
        lift_kernel, "lift", (shape(NF, L), shape(896, L)),
        (own, pooled_cot, cfrom_prev, cfrom_next, coarse, sums, seconds, cga, cagg, refined, pool,
         w_outs),
        [VMEM] * 12,
    )
    grad_edges, grad_node, back_prev, back_next, grads = call(
        fine_back_kernel, "fine_back",
        (shape(EF, L), f32(NF, L)) + slots + (shape(GRADS, L),),
        (live, ccounts, grad_own, divisor, cret_prev, cret_next, csend, cot, pool, node,
         from_prev, from_next, act_node, agg, act, edge, cot_edges, src, dst, w_edge, w_node,
         w_outs, coarse_grads),
        [SMEM, SMEM] + [VMEM] * 21,
    )
    ret_prev, ret_next = shift(back_next, EVERY, 1), shift(back_prev, EVERY, -1)
    parts = exchange(grads.reshape(32, GRADS // 32, L), PLANE)
    spread = call(spread_kernel, "sum_plane", shape(8, GRADS // 32, L), (parts,), [VMEM], 10**6)
    parts = exchange(spread, "z")
    spread = call(spread_kernel, "sum_z", shape(32, GRADS // 32, L), (parts,), [VMEM], 10**6)
    grad_nodes = call(
        node_end_kernel, "node_end", shape(NF, L),
        (counts, grad_node, ret_prev, ret_next, send), [SMEM] + [VMEM] * 4, 10**7,
    )
    rows = exchange(spread, PLANE).reshape(GRADS, L)
    weights = call(
        end_kernel, "end",
        (f32(384, L), f32(256, L), f32(256, L), f32(256, L), f32(5, L, L)),
        (rows,), [VMEM], 10**6,
    )
    return (new_nodes, new_edges, grad_nodes, grad_edges) + tuple(weights)


def solution(mesh):
    cube = Mesh(mesh.devices.reshape(8, 4, 4, 2), EVERY)
    fine, coarse = P(EVERY), P(GROUP)
    in_specs = (fine,) * 8 + (coarse,) * 5 + (P(),) * 5 + (fine,) * 2
    out_specs = (fine,) * 4 + (P(),) * 5
    return jax.shard_map(
        on_device, mesh=cube, in_specs=in_specs, out_specs=out_specs, check_vma=False
    )
```

```python
import functools

import jax
import jax.numpy as jnp
from jax import lax
from jax.experimental import pallas as pl
from jax.experimental.pallas import tpu as pltpu
from jax.sharding import Mesh
from jax.sharding import PartitionSpec as P

F32 = jnp.float32
BF = jnp.bfloat16
I32 = jnp.int32
EPS = 1e-05

L = 128
NF = 512
EF = 3072
NC = 256
EC = 1536
SLOT = 128
FINE_BLK = 8
COARSE_BLK = 12
CNT = 16
GRADS = 1792
ROWS_EDGE, ROWS_NODE, ROWS_CEDGE, ROWS_CNODE, ROWS_OUTS = 0, 384, 640, 896, 1152

EVERY = ("z", "x", "y", "c")
GROUP = ("z", "x")
PLANE = ("x", "y", "c")

VMEM = pl.BlockSpec(memory_space=pltpu.VMEM)
HBM = pl.BlockSpec(memory_space=pltpu.HBM)


def call(kernel, name, out_shape, ins, flops=10**9, hbm_in=False, hbm_out=(), scratch=()):
    size = sum(a.size * a.dtype.itemsize for a in ins)
    outs = out_shape if isinstance(out_shape, tuple) else (out_shape,)
    specs = tuple(HBM if k in hbm_out else VMEM for k in range(len(outs)))
    return pl.pallas_call(
        kernel,
        name=name,
        out_shape=out_shape,
        in_specs=[HBM if hbm_in else VMEM] * len(ins),
        out_specs=specs if isinstance(out_shape, tuple) else specs[0],
        scratch_shapes=scratch,
        cost_estimate=pl.CostEstimate(flops=flops, bytes_accessed=size, transcendentals=0),
        compiler_params=pltpu.CompilerParams(vmem_limit_bytes=32 * 2**20),
    )(*ins)


def landing(ins):
    return tuple(pltpu.VMEM(a.shape, a.dtype) for a in ins) + (pltpu.SemaphoreType.DMA((len(ins),)),)


def fetch(sources, places, sems):
    copies = [
        pltpu.make_async_copy(a, b, sems.at[k]) for k, (a, b) in enumerate(zip(sources, places))
    ]
    for copy in copies:
        copy.start()
    return copies


def shape(*dims, dtype=BF):
    return jax.ShapeDtypeStruct(dims, dtype)


def dot(a, b):
    return jnp.dot(a, b, preferred_element_type=F32)


def dot_nt(a, b):
    return lax.dot_general(a, b, (((1,), (1,)), ((), ())), preferred_element_type=F32)


def dot_tn(a, b):
    return lax.dot_general(a, b, (((0,), (0,)), ((), ())), preferred_element_type=F32)


def mean(v):
    return jnp.mean(v, axis=-1, keepdims=True)


def columns(rows):
    pad = -rows.shape[0] % 8
    rows = rows.astype(F32)
    if pad:
        rows = jnp.concatenate([rows, jnp.zeros((pad, 128), F32)], 0)
    return rows.T.astype(I32)


def pick(cols, blocks, n):
    lane = lax.broadcasted_iota(I32, (128, n), 1)
    return jnp.concatenate(
        [jnp.where(lane == cols[:, j : j + 1], 1.0, 0.0).astype(BF) for j in blocks], 0
    )


def put(rows, blocks, n):
    line = lax.broadcasted_iota(I32, (n, 128), 0)
    return jnp.concatenate(
        [jnp.where(line == rows[j : j + 1, :], 1.0, 0.0).astype(BF) for j in blocks], 1
    )


def live_rows(rows, count):
    at = lax.broadcasted_iota(I32, rows.shape, 0) * 128 + lax.broadcasted_iota(I32, rows.shape, 1)
    return jnp.where(at < jnp.broadcast_to(count, rows.shape), rows, -1)


def live_slots(send, counts):
    lane = lax.broadcasted_iota(I32, (1, SLOT), 1)
    return jnp.concatenate(
        [
            jnp.where(
                lane < jnp.broadcast_to(counts[0:1, s : s + 1], (1, SLOT)), send[s : s + 1, :], -1
            )
            for s in (0, 1)
        ],
        0,
    )


def sigmoid(a):
    return 1.0 / (1.0 + jnp.exp(-a))


def normed_of(hidden, w_second):
    outcome = dot(hidden, w_second)
    centred = outcome - mean(outcome)
    inv = lax.rsqrt(mean(centred * centred) + EPS)
    return centred * inv, inv


def activation(a):
    sig = sigmoid(a)
    return (a * sig).astype(BF), sig * (1.0 + a * (1.0 - sig))


def norm_back(grad, normed, inv):
    return (inv * (grad - mean(grad) - normed * mean(grad * normed))).astype(BF)


def forward(a, w_second):
    return normed_of((a * sigmoid(a)).astype(BF), w_second)[0]


def send_kernel(node_hbm, send_hbm, counts_hbm, to_prev, to_next, node, send, counts, sems):
    copies = fetch((node_hbm, send_hbm, counts_hbm), (node, send, counts), sems)
    for copy in copies:
        copy.wait()
    cols = columns(live_slots(send[...], counts))
    rows = node[...]
    to_prev[...] = dot(pick(cols, (0,), NF), rows).astype(BF)
    to_next[...] = dot(pick(cols, (1,), NF), rows).astype(BF)


def pre_kernel(*refs):
    sources, (pre, side), places, sems = refs[:7], refs[7:9], refs[9:16], refs[16]
    node, w_in, src, dst, edge, pool, cot = places
    copies = fetch(sources, places, sems)
    for copy in copies[:4]:
        copy.wait()
    w = w_in[...]
    rows = node[...]
    table = jnp.concatenate([dot(rows, w[256:384]), dot(rows, w[128:256])], 0).astype(BF)
    src_cols, dst_cols = columns(src[...]), columns(dst[...])
    for copy in copies[4:]:
        copy.wait()
    for c in range(EF // 128 // FINE_BLK):
        blocks = range(c * FINE_BLK, (c + 1) * FINE_BLK)
        at = pl.ds(c * FINE_BLK * 128, FINE_BLK * 128)
        hot = jnp.concatenate([pick(dst_cols, blocks, NF), pick(src_cols, blocks, NF)], 1)
        pre[at, :] = dot(edge[at, :], w[:128]) + dot(hot, table)
    pool_hot = put(pool[...], range(NF // 128), NC)
    side[0:NC, :] = dot(pool_hot, cot[...]).astype(BF)
    count = dot_nt(jnp.ones((8, NF), BF), pool_hot)
    high = jnp.floor(count * (1.0 / 16.0))
    low = count - 16.0 * high
    at = lax.broadcasted_iota(I32, (CNT, 128), 0)
    lines = jnp.zeros((CNT, 128), F32)
    for k, v in enumerate((high[0:1, :128], high[0:1, 128:], low[0:1, :128], low[0:1, 128:])):
        lines = jnp.where(at == k, v, lines)
    side[NC : NC + CNT, :] = lines.astype(BF)


def fine_kernel(
    live, pre, edge, node, from_prev, from_next, src, dst, w_in, w_node, w_outs, pool, side,
    new_edges_hbm, act, agg_out, act_node, refined, payload, new_edges, sems,
):
    halo = jnp.concatenate([from_prev[...], from_next[...]], 0)
    table = dot(halo, w_in[128:256, :]).astype(BF)
    src_cols = columns(src[...] - NF)
    dst_rows = live_rows(dst[...], live[...])
    w_second = w_outs[0]
    total = jnp.zeros((NF, L), F32)
    copies = []
    for c in range(EF // 128 // FINE_BLK):
        blocks = range(c * FINE_BLK, (c + 1) * FINE_BLK)
        at = pl.ds(c * FINE_BLK * 128, FINE_BLK * 128)
        a = pre[at, :] + dot(pick(src_cols, blocks, 2 * SLOT), table)
        act[at, :] = a
        message = forward(a, w_second)
        here = lax.broadcasted_iota(I32, message.shape, 0) + c * FINE_BLK * 128
        here = here < jnp.broadcast_to(live[...], message.shape)
        rows = (edge[at, :].astype(F32) + jnp.where(here, message, 0.0)).astype(BF)
        new_edges[at, :] = rows
        copies.append(pltpu.make_async_copy(new_edges.at[at], new_edges_hbm.at[at], sems.at[c]))
        copies[-1].start()
        total += dot(put(dst_rows, blocks, NF), rows)
    agg = total.astype(BF)
    agg_out[...] = agg
    a = dot(node[...], w_node[:128, :]) + dot(agg, w_node[128:, :])
    act_node[...] = a
    rows = (node[...].astype(F32) + forward(a, w_outs[1])).astype(BF)
    refined[...] = rows
    payload[0:NC, :] = dot(put(pool[...], range(NF // 128), NC), rows).astype(BF)
    payload[NC:, :] = side[...]
    for copy in copies:
        copy.wait()


def pair_kernel(pair, out):
    out[...] = (pair[0].astype(F32) + pair[1].astype(F32)).astype(BF)


def pool_kernel(a, b, c, d, send, counts, own_out, cot_out, divisor, to_prev, to_next):
    total = a[...].astype(F32) + b[...].astype(F32) + c[...].astype(F32) + d[...].astype(F32)
    lines = total[2 * NC :, :]
    count = 16.0 * lines[0:2, :] + lines[2:4, :]
    cols = jnp.concatenate([count, jnp.ones((6, 128), F32)], 0).T
    count = jnp.concatenate(
        [jnp.broadcast_to(cols[:, k : k + 1], (128, L)) for k in (0, 1)], 0
    )
    own = (total[:NC, :] / count).astype(BF)
    own_out[...] = own
    cot_out[...] = total[NC : 2 * NC, :].astype(BF)
    divisor[...] = count
    cols = columns(live_slots(send[...], counts))
    to_prev[...] = dot(pick(cols, (0,), NC), own).astype(BF)
    to_next[...] = dot(pick(cols, (1,), NC), own).astype(BF)


def coarse_pre_kernel(own, cot, src, dst, w_in, w_node, w_outs, pre, pre_node, grad_coarse):
    rows = own[...]
    table = jnp.concatenate([dot(rows, w_in[128:, :]), dot(rows, w_in[:128, :])], 0).astype(BF)
    src_cols, dst_cols = columns(src[...]), columns(dst[...])
    for c in range(EC // 128 // COARSE_BLK):
        blocks = range(c * COARSE_BLK, (c + 1) * COARSE_BLK)
        hot = jnp.concatenate([pick(dst_cols, blocks, NC), pick(src_cols, blocks, NC)], 1)
        pre[pl.ds(c * COARSE_BLK * 128, COARSE_BLK * 128), :] = dot(hot, table)
    pre_node[...] = dot(rows, w_node[:128, :])
    grad_coarse[...] = dot_nt(cot[...], w_outs[4]).astype(BF)


def coarse_kernel(
    live, own, pre, pre_node, grad_coarse, from_prev, from_next, src, dst, w_in, w_node, w_outs,
    coarse_out, grad_own, back_prev, back_next, sums_out, agg_out, ga_out, pair_node, pair_edge,
):
    halo = jnp.concatenate([from_prev[...], from_next[...]], 0)
    table = dot(halo, w_in[:128, :]).astype(BF)
    blocks = range(EC // 128)
    src_rows = src[...]
    dst_rows = live_rows(dst[...], live[...])
    a = pre[...] + dot(pick(columns(src_rows - NC), blocks, 2 * SLOT), table)
    hidden, slope = activation(a)
    normed, inv = normed_of(hidden, w_outs[2])
    put_dst = put(dst_rows, blocks, NC)
    agg = dot(put_dst, normed.astype(BF)).astype(BF)
    agg_out[...] = agg
    a = pre_node[...] + dot(agg, w_node[128:, :])
    hidden_node, slope_node = activation(a)
    normed_node, inv_node = normed_of(hidden_node, w_outs[3])
    coarse_out[...] = (own[...].astype(F32) + normed_node).astype(BF)
    grad = grad_coarse[...].astype(F32)
    go = norm_back(grad, normed_node, inv_node)
    ga = (dot_nt(go, w_outs[3]) * slope_node).astype(BF)
    ga_out[...] = ga
    pair_node[0] = hidden_node
    pair_node[1] = go
    grad_total = grad + dot_nt(ga, w_node[:128, :])
    grad_agg = dot_nt(ga, w_node[128:, :]).astype(BF)
    grad = dot(pick(columns(dst_rows), blocks, NC), grad_agg)
    go = norm_back(grad, normed, inv)
    pair_edge[0] = hidden
    pair_edge[1] = go
    ga = (dot_nt(go, w_outs[2]) * slope).astype(BF)
    src_sums = dot(put(src_rows, blocks, NC + 2 * SLOT), ga).astype(BF)
    dst_sums = dot(put_dst, ga).astype(BF)
    sums_out[: NC + 2 * SLOT, :] = src_sums
    sums_out[NC + 2 * SLOT :, :] = dst_sums
    grad_ext = dot_nt(src_sums, w_in[:128, :])
    back_prev[...] = grad_ext[NC : NC + SLOT].astype(BF)
    back_next[...] = grad_ext[NC + SLOT :].astype(BF)
    grad_own[...] = grad_total + grad_ext[:NC] + dot_nt(dst_sums, w_in[128:, :])


def lift_kernel(
    own, cot, from_prev, from_next, coarse, sums, agg, ga, pair_node, pair_edge, refined, pool,
    w_outs, new_nodes, grads,
):
    part = 1.0 / 8.0
    rows = own[...]
    ext = jnp.concatenate([rows, from_prev[...], from_next[...]], 0)
    both = sums[...]
    lifted = dot(pick(columns(pool[...]), range(NF // 128), NC), coarse[...]).astype(BF)
    new_nodes[...] = (refined[...].astype(F32) + dot(lifted, w_outs[4])).astype(BF)
    grads[0:128, :] = (part * dot_tn(ext, both[: NC + 2 * SLOT])).astype(BF)
    grads[128:256, :] = (part * dot_tn(rows, both[NC + 2 * SLOT :])).astype(BF)
    grads[256:384, :] = (part * dot_tn(rows, ga[...])).astype(BF)
    grads[384:512, :] = (part * dot_tn(agg[...], ga[...])).astype(BF)
    grads[512:640, :] = (part * dot_tn(pair_edge[0], pair_edge[1])).astype(BF)
    grads[640:768, :] = (part * dot_tn(pair_node[0], pair_node[1])).astype(BF)
    grads[768:896, :] = (part * dot_tn(coarse[...], cot[...])).astype(BF)


def prep_kernel(
    act, act_node, w_outs, hidden_out, slope_out, normed_out, inv_out, hidden_node, slope_node,
    normed_node, inv_node,
):
    for c in range(EF // 128 // FINE_BLK):
        at = pl.ds(c * FINE_BLK * 128, FINE_BLK * 128)
        hidden, slope = activation(act[at, :])
        normed, inv = normed_of(hidden, w_outs[0])
        hidden_out[at, :] = hidden
        slope_out[at, :] = slope.astype(BF)
        normed_out[at, :] = normed.astype(BF)
        inv_out[at, :] = inv
    hidden, slope = activation(act_node[...])
    normed, inv = normed_of(hidden, w_outs[1])
    hidden_node[...] = hidden
    slope_node[...] = slope
    normed_node[...] = normed
    inv_node[...] = inv


def fine_back_kernel(
    live, counts, grad_own, divisor, ret_prev, ret_next, send, cot, pool, node, from_prev,
    from_next, agg, hidden, slope, normed, inv, hidden_node, slope_node, normed_node, inv_node,
    edge, cot_edges, src, dst, w_in, w_node, w_outs, coarse_grads,
    grad_edges_hbm, grad_node, back_prev, back_next, grads, grad_edges, sems,
):
    back = jnp.concatenate([ret_prev[...], ret_next[...]], 0)
    hot = put(live_slots(send[...], counts), (0, 1), NC)
    grad_pool = (grad_own[...] + dot(hot, back)).astype(BF).astype(F32) / divisor[...]
    pooled = dot(pick(columns(pool[...]), range(NF // 128), NC), grad_pool.astype(BF))
    grad_refined = (cot[...].astype(F32) + pooled).astype(BF).astype(F32)
    go = norm_back(grad_refined, normed_node[...], inv_node[...])
    ga = (dot_nt(go, w_outs[1]) * slope_node[...]).astype(BF)
    grad_agg = dot_nt(ga, w_node[128:, :]).astype(BF)
    rows = node[...]
    grads[384:512, :] = dot_tn(rows, ga).astype(BF)
    grads[512:640, :] = dot_tn(agg[...], ga).astype(BF)
    grads[1280:1408, :] = dot_tn(hidden_node[...], go).astype(BF)
    grad_node[...] = grad_refined + dot_nt(ga, w_node[:128, :])
    src_rows = src[...]
    dst_rows = live_rows(dst[...], live[...])
    dst_cols = columns(dst_rows)
    w_second = w_outs[0]
    first = jnp.zeros((L, L), F32)
    second = jnp.zeros((L, L), F32)
    sums = jnp.zeros((NF + 2 * SLOT + NF, L), F32)
    copies = []
    for c in range(EF // 128 // FINE_BLK):
        blocks = range(c * FINE_BLK, (c + 1) * FINE_BLK)
        at = pl.ds(c * FINE_BLK * 128, FINE_BLK * 128)
        gathered = dot(pick(dst_cols, blocks, NF), grad_agg)
        grad_new = (cot_edges[at, :].astype(F32) + gathered).astype(BF).astype(F32)
        here = lax.broadcasted_iota(I32, grad_new.shape, 0) + c * FINE_BLK * 128
        here = here < jnp.broadcast_to(live[...], grad_new.shape)
        go = norm_back(jnp.where(here, grad_new, 0.0), normed[at, :].astype(F32), inv[at, :])
        ga = (dot_nt(go, w_second) * slope[at, :].astype(F32)).astype(BF)
        grad_edges[at, :] = (grad_new + dot_nt(ga, w_in[:128, :])).astype(BF)
        copies.append(pltpu.make_async_copy(grad_edges.at[at], grad_edges_hbm.at[at], sems.at[c]))
        copies[-1].start()
        first += dot_tn(edge[at, :], ga)
        second += dot_tn(hidden[at, :], go)
        hot = jnp.concatenate(
            [put(src_rows, blocks, NF + 2 * SLOT), put(dst_rows, blocks, NF)], 0
        )
        sums += dot(hot, ga)
    sums = sums.astype(BF)
    grad_ext = dot_nt(sums[: NF + 2 * SLOT], w_in[128:256, :])
    grad_node[...] += grad_ext[:NF] + dot_nt(sums[NF + 2 * SLOT :], w_in[256:, :])
    back_prev[...] = grad_ext[NF : NF + SLOT].astype(BF)
    back_next[...] = grad_ext[NF + SLOT :].astype(BF)
    ext = jnp.concatenate([rows, from_prev[...], from_next[...]], 0)
    grads[0:128, :] = first.astype(BF)
    grads[128:256, :] = dot_tn(ext, sums[: NF + 2 * SLOT]).astype(BF)
    grads[256:384, :] = dot_tn(rows, sums[NF + 2 * SLOT :]).astype(BF)
    grads[640:1152, :] = coarse_grads[0:512, :]
    grads[1152:1280, :] = second.astype(BF)
    grads[1408:1792, :] = coarse_grads[512:896, :]
    for copy in copies:
        copy.wait()


def node_end_kernel(counts, grad_node, ret_prev, ret_next, send, out):
    back = jnp.concatenate([ret_prev[...], ret_next[...]], 0)
    hot = put(live_slots(send[...], counts), (0, 1), NF)
    out[...] = (grad_node[...] + dot(hot, back)).astype(BF)


def spread_kernel(parts, out):
    total = parts[0].astype(F32)
    for k in range(1, parts.shape[0]):
        total += parts[k].astype(F32)
    total = total.astype(BF)
    for k in range(out.shape[0]):
        out[k] = total


def end_kernel(rows, edge_in, node_in, cedge_in, cnode_in, outs):
    edge_in[...] = rows[ROWS_EDGE:ROWS_NODE, :].astype(F32)
    node_in[...] = rows[ROWS_NODE:ROWS_CEDGE, :].astype(F32)
    cedge_in[...] = rows[ROWS_CEDGE:ROWS_CNODE, :].astype(F32)
    cnode_in[...] = rows[ROWS_CNODE:ROWS_OUTS, :].astype(F32)
    for k in range(5):
        outs[k] = rows[ROWS_OUTS + k * 128 : ROWS_OUTS + (k + 1) * 128, :].astype(F32)


def shift(value, axes, step):
    count = lax.axis_size(axes)
    return lax.ppermute(
        value, axes, [(i, i + step) for i in range(count) if 0 <= i + step < count]
    )


def exchange(value, axes):
    return lax.all_to_all(value, axes, 0, 0)


def on_device(
    node, edge, src, dst, live, send, counts, pool, csrc, cdst, clive, csend, ccounts,
    w_edge, w_node, w_cedge, w_cnode, w_outs, cot, cot_edges,
):
    f32 = functools.partial(shape, dtype=F32)
    slots = (shape(SLOT, L), shape(SLOT, L))
    src, dst = src.reshape(EF // 128, 128), dst.reshape(EF // 128, 128)
    csrc, cdst = csrc.reshape(EC // 128, 128), cdst.reshape(EC // 128, 128)
    pool = pool.reshape(NF // 128, 128)
    send, csend = send.reshape(2, SLOT), csend.reshape(2, SLOT)
    live, clive = live.reshape(1, 1), clive.reshape(1, 1)
    edge_copies = (pltpu.VMEM((EF, L), BF), pltpu.SemaphoreType.DMA((EF // 128 // FINE_BLK,)))

    ins = (node, send, counts)
    to_prev, to_next = call(
        send_kernel, "send", slots, ins, 10**7, hbm_in=True, scratch=landing(ins)
    )
    from_prev, from_next = shift(to_next, EVERY, 1), shift(to_prev, EVERY, -1)
    ins = (node, w_edge, src, dst, edge, pool, cot)
    pre, side = call(
        pre_kernel, "pre", (f32(EF, L), shape(NC + CNT, L)), ins, hbm_in=True, scratch=landing(ins)
    )
    new_edges, act, agg, act_node, refined, payload = call(
        fine_kernel, "fine",
        (shape(EF, L), f32(EF, L), shape(NF, L), f32(NF, L), shape(NF, L), shape(2 * NC + CNT, L)),
        (live, pre, edge, node, from_prev, from_next, src, dst, w_edge, w_node, w_outs, pool, side),
        hbm_out=(0,), scratch=edge_copies,
    )
    pair = lax.all_gather(payload, "c", axis=0, tiled=False)
    total = call(pair_kernel, "pair", shape(2 * NC + CNT, L), (pair,), 10**6)
    others = tuple(
        lax.ppermute(total, "y", [(i, (i + k) % 4) for i in range(4)]) for k in (1, 2, 3)
    )
    prepared = call(
        prep_kernel, "prep",
        (shape(EF, L), shape(EF, L), shape(EF, L), f32(EF, 1),
         shape(NF, L), f32(NF, L), f32(NF, L), f32(NF, 1)),
        (act, act_node, w_outs),
    )
    own, pooled_cot, divisor, to_prev, to_next = call(
        pool_kernel, "pool", (shape(NC, L), shape(NC, L), f32(NC, L)) + slots,
        (total,) + others + (csend, ccounts), 10**7,
    )
    cfrom_prev, cfrom_next = shift(to_next, GROUP, 1), shift(to_prev, GROUP, -1)
    cpre, cpre_node, grad_coarse = call(
        coarse_pre_kernel, "coarse_pre", (f32(EC, L), f32(NC, L), shape(NC, L)),
        (own, pooled_cot, csrc, cdst, w_cedge, w_cnode, w_outs),
    )
    coarse, grad_own, back_prev, back_next, sums, cagg, cga, pair_node, pair_edge = call(
        coarse_kernel, "coarse",
        (shape(NC, L), f32(NC, L)) + slots
        + (shape(2 * NC + 2 * SLOT, L), shape(NC, L), shape(NC, L), shape(2, NC, L),
           shape(2, EC, L)),
        (clive, own, cpre, cpre_node, grad_coarse, cfrom_prev, cfrom_next, csrc, cdst,
         w_cedge, w_cnode, w_outs),
    )
    cret_prev, cret_next = shift(back_next, GROUP, 1), shift(back_prev, GROUP, -1)
    new_nodes, coarse_grads = call(
        lift_kernel, "lift", (shape(NF, L), shape(896, L)),
        (own, pooled_cot, cfrom_prev, cfrom_next, coarse, sums, cagg, cga, pair_node, pair_edge,
         refined, pool, w_outs),
    )
    grad_edges, grad_node, back_prev, back_next, grads = call(
        fine_back_kernel, "fine_back",
        (shape(EF, L), f32(NF, L)) + slots + (shape(GRADS, L),),
        (live, ccounts, grad_own, divisor, cret_prev, cret_next, csend, cot, pool, node,
         from_prev, from_next, agg) + tuple(prepared)
        + (edge, cot_edges, src, dst, w_edge, w_node, w_outs, coarse_grads),
        hbm_out=(0,), scratch=edge_copies,
    )
    ret_prev, ret_next = shift(back_next, EVERY, 1), shift(back_prev, EVERY, -1)
    parts = exchange(grads.reshape(32, GRADS // 32, L), PLANE)
    spread = call(spread_kernel, "sum_plane", shape(8, GRADS // 32, L), (parts,), 10**6)
    parts = exchange(spread, "z")
    spread = call(spread_kernel, "sum_z", shape(32, GRADS // 32, L), (parts,), 10**6)
    grad_nodes = call(
        node_end_kernel, "node_end", shape(NF, L), (counts, grad_node, ret_prev, ret_next, send),
        10**7,
    )
    rows = exchange(spread, PLANE).reshape(GRADS, L)
    weights = call(
        end_kernel, "end", (f32(384, L), f32(256, L), f32(256, L), f32(256, L), f32(5, L, L)),
        (rows,), 10**6,
    )
    return (new_nodes, new_edges, grad_nodes, grad_edges) + tuple(weights)


def solution(mesh):
    cube = Mesh(mesh.devices.reshape(8, 4, 4, 2), EVERY)
    fine, coarse = P(EVERY), P(GROUP)
    in_specs = (fine,) * 8 + (coarse,) * 5 + (P(),) * 5 + (fine,) * 2
    out_specs = (fine,) * 4 + (P(),) * 5
    return jax.shard_map(
        on_device, mesh=cube, in_specs=in_specs, out_specs=out_specs, check_vma=False
    )
```

```python
import functools

import jax
import jax.numpy as jnp
from jax import lax
from jax.experimental import pallas as pl
from jax.experimental.pallas import tpu as pltpu
from jax.sharding import Mesh
from jax.sharding import PartitionSpec as P

F32 = jnp.float32
BF = jnp.bfloat16
I32 = jnp.int32
EPS = 1e-05

L = 128
NF = 512
EF = 3072
NC = 256
EC = 1536
SLOT = 128
FINE_BLK = 8
COARSE_BLK = 12
CNT = 16
GRADS = 1792
ROWS_EDGE, ROWS_NODE, ROWS_CEDGE, ROWS_CNODE, ROWS_OUTS = 0, 384, 640, 896, 1152

EVERY = ("z", "x", "y", "c")
GROUP = ("z", "x")
PLANE = ("x", "y", "c")

VMEM = pl.BlockSpec(memory_space=pltpu.VMEM)
HBM = pl.BlockSpec(memory_space=pltpu.HBM)
SMEM = pl.BlockSpec(memory_space=pltpu.SMEM)


def call(kernel, name, out_shape, ins, flops=10**9, space=VMEM, hbm_out=(), scratch=()):
    size = sum(a.size * a.dtype.itemsize for a in ins)
    outs = out_shape if isinstance(out_shape, tuple) else (out_shape,)
    specs = tuple(HBM if k in hbm_out else VMEM for k in range(len(outs)))
    return pl.pallas_call(
        kernel,
        name=name,
        out_shape=out_shape,
        in_specs=[space] * len(ins),
        out_specs=specs if isinstance(out_shape, tuple) else specs[0],
        scratch_shapes=scratch,
        cost_estimate=pl.CostEstimate(flops=flops, bytes_accessed=size, transcendentals=0),
        compiler_params=pltpu.CompilerParams(vmem_limit_bytes=32 * 2**20),
    )(*ins)


def shape(*dims, dtype=BF):
    return jax.ShapeDtypeStruct(dims, dtype)


def dot(a, b):
    return jnp.dot(a, b, preferred_element_type=F32)


def dot_nt(a, b):
    return lax.dot_general(a, b, (((1,), (1,)), ((), ())), preferred_element_type=F32)


def dot_tn(a, b):
    return lax.dot_general(a, b, (((0,), (0,)), ((), ())), preferred_element_type=F32)


def mean(v):
    return jnp.mean(v, axis=-1, keepdims=True)


def columns(rows):
    pad = -rows.shape[0] % 8
    rows = rows.astype(F32)
    if pad:
        rows = jnp.concatenate([rows, jnp.zeros((pad, 128), F32)], 0)
    return rows.T.astype(I32)


def pick(cols, blocks, n):
    lane = lax.broadcasted_iota(I32, (128, n), 1)
    return jnp.concatenate(
        [jnp.where(lane == cols[:, j : j + 1], 1.0, 0.0).astype(BF) for j in blocks], 0
    )


def put(rows, blocks, n):
    line = lax.broadcasted_iota(I32, (n, 128), 0)
    return jnp.concatenate(
        [jnp.where(line == rows[j : j + 1, :], 1.0, 0.0).astype(BF) for j in blocks], 1
    )


def live_rows(rows, count):
    at = lax.broadcasted_iota(I32, rows.shape, 0) * 128 + lax.broadcasted_iota(I32, rows.shape, 1)
    return jnp.where(at < jnp.broadcast_to(count, rows.shape), rows, -1)


def live_slots(send, counts, axes):
    spot, last = 0, 1
    for axis in axes:
        spot = spot * lax.axis_size(axis) + lax.axis_index(axis)
        last = last * lax.axis_size(axis)
    there = ((spot > 0).astype(I32), (spot < last - 1).astype(I32))
    lane = lax.broadcasted_iota(I32, (1, SLOT), 1)
    return jnp.concatenate(
        [
            jnp.where(
                lane < jnp.broadcast_to(counts[0:1, s : s + 1], (1, SLOT)) * there[s],
                send[s : s + 1, :],
                -1,
            )
            for s in (0, 1)
        ],
        0,
    )


def sigmoid(a):
    return 1.0 / (1.0 + jnp.exp(-a))


def normed_of(hidden, w_second):
    outcome = dot(hidden, w_second)
    centred = outcome - mean(outcome)
    inv = lax.rsqrt(mean(centred * centred) + EPS)
    return centred * inv, inv


def activation(a):
    sig = sigmoid(a)
    return (a * sig).astype(BF), sig * (1.0 + a * (1.0 - sig))


def norm_back(grad, normed, inv):
    return (inv * (grad - mean(grad) - normed * mean(grad * normed))).astype(BF)


def forward(a, w_second):
    return normed_of((a * sigmoid(a)).astype(BF), w_second)[0]


def begin_kernel(live, clive, out):
    at = lax.broadcasted_iota(I32, out.shape, 0)
    out[...] = jnp.where(at == 0, live[0], jnp.where(at == 1, clive[0], 0))


def send_kernel(lives, node, send, counts, to_prev, to_next):
    cols = columns(live_slots(send[...] + lives[2:4, :], counts, EVERY))
    rows = node[...]
    to_prev[...] = dot(pick(cols, (0,), NF), rows).astype(BF)
    to_next[...] = dot(pick(cols, (1,), NF), rows).astype(BF)


def pre_kernel(node, w_in, src, dst, edge, pool, cot, pre, side):
    w = w_in[...]
    rows = node[...]
    table = jnp.concatenate([dot(rows, w[256:384]), dot(rows, w[128:256])], 0).astype(BF)
    src_cols, dst_cols = columns(src[...]), columns(dst[...])
    for c in range(EF // 128 // FINE_BLK):
        blocks = range(c * FINE_BLK, (c + 1) * FINE_BLK)
        at = pl.ds(c * FINE_BLK * 128, FINE_BLK * 128)
        hot = jnp.concatenate([pick(dst_cols, blocks, NF), pick(src_cols, blocks, NF)], 1)
        pre[at, :] = dot(edge[at, :], w[:128]) + dot(hot, table)
    pool_hot = put(pool[...], range(NF // 128), NC)
    side[0:NC, :] = dot(pool_hot, cot[...]).astype(BF)
    count = dot_nt(jnp.ones((8, NF), BF), pool_hot)
    high = jnp.floor(count * (1.0 / 16.0))
    low = count - 16.0 * high
    at = lax.broadcasted_iota(I32, (CNT, 128), 0)
    lines = jnp.zeros((CNT, 128), F32)
    for k, v in enumerate((high[0:1, :128], high[0:1, 128:], low[0:1, :128], low[0:1, 128:])):
        lines = jnp.where(at == k, v, lines)
    side[NC : NC + CNT, :] = lines.astype(BF)


def fine_kernel(
    live, pre, edge, node, from_prev, from_next, src, dst, w_in, w_node, w_outs, pool, side,
    new_edges_hbm, act, agg_out, act_node, refined, payload, new_edges, sems,
):
    halo = jnp.concatenate([from_prev[...], from_next[...]], 0)
    table = dot(halo, w_in[128:256, :]).astype(BF)
    src_cols = columns(src[...] - NF)
    dst_rows = live_rows(dst[...], live[0:1, 0:1])
    w_second = w_outs[0]
    total = jnp.zeros((NF, L), F32)
    copies = []
    for c in range(EF // 128 // FINE_BLK):
        blocks = range(c * FINE_BLK, (c + 1) * FINE_BLK)
        at = pl.ds(c * FINE_BLK * 128, FINE_BLK * 128)
        a = pre[at, :] + dot(pick(src_cols, blocks, 2 * SLOT), table)
        act[at, :] = a
        message = forward(a, w_second)
        here = lax.broadcasted_iota(I32, message.shape, 0) + c * FINE_BLK * 128
        here = here < jnp.broadcast_to(live[0:1, 0:1], message.shape)
        rows = (edge[at, :].astype(F32) + jnp.where(here, message, 0.0)).astype(BF)
        new_edges[at, :] = rows
        copies.append(pltpu.make_async_copy(new_edges.at[at], new_edges_hbm.at[at], sems.at[c]))
        copies[-1].start()
        total += dot(put(dst_rows, blocks, NF), rows)
    agg = total.astype(BF)
    agg_out[...] = agg
    a = dot(node[...], w_node[:128, :]) + dot(agg, w_node[128:, :])
    act_node[...] = a
    rows = (node[...].astype(F32) + forward(a, w_outs[1])).astype(BF)
    refined[...] = rows
    payload[0:NC, :] = dot(put(pool[...], range(NF // 128), NC), rows).astype(BF)
    payload[NC:, :] = side[...]
    for copy in copies:
        copy.wait()


def pair_kernel(pair, out):
    out[...] = (pair[0].astype(F32) + pair[1].astype(F32)).astype(BF)


def pool_kernel(a, b, c, d, send, counts, own_out, cot_out, divisor, to_prev, to_next):
    total = a[...].astype(F32) + b[...].astype(F32) + c[...].astype(F32) + d[...].astype(F32)
    lines = total[2 * NC :, :]
    count = 16.0 * lines[0:2, :] + lines[2:4, :]
    cols = jnp.concatenate([count, jnp.ones((6, 128), F32)], 0).T
    count = jnp.concatenate(
        [jnp.broadcast_to(cols[:, k : k + 1], (128, L)) for k in (0, 1)], 0
    )
    own = (total[:NC, :] / count).astype(BF)
    own_out[...] = own
    cot_out[...] = total[NC : 2 * NC, :].astype(BF)
    divisor[...] = count
    cols = columns(live_slots(send[...], counts, GROUP))
    to_prev[...] = dot(pick(cols, (0,), NC), own).astype(BF)
    to_next[...] = dot(pick(cols, (1,), NC), own).astype(BF)


def coarse_pre_kernel(own, cot, src, dst, w_in, w_node, w_outs, pre, pre_node, grad_coarse):
    rows = own[...]
    table = jnp.concatenate([dot(rows, w_in[128:, :]), dot(rows, w_in[:128, :])], 0).astype(BF)
    src_cols, dst_cols = columns(src[...]), columns(dst[...])
    for c in range(EC // 128 // COARSE_BLK):
        blocks = range(c * COARSE_BLK, (c + 1) * COARSE_BLK)
        hot = jnp.concatenate([pick(dst_cols, blocks, NC), pick(src_cols, blocks, NC)], 1)
        pre[pl.ds(c * COARSE_BLK * 128, COARSE_BLK * 128), :] = dot(hot, table)
    pre_node[...] = dot(rows, w_node[:128, :])
    grad_coarse[...] = dot_nt(cot[...], w_outs[4]).astype(BF)


def coarse_kernel(
    live, own, pre, pre_node, grad_coarse, from_prev, from_next, src, dst, w_in, w_node, w_outs,
    coarse_out, grad_own, back_prev, back_next, sums_out, agg_out, ga_out, pair_node, pair_edge,
):
    halo = jnp.concatenate([from_prev[...], from_next[...]], 0)
    table = dot(halo, w_in[:128, :]).astype(BF)
    blocks = range(EC // 128)
    src_rows = src[...]
    dst_rows = live_rows(dst[...], live[1:2, 0:1])
    a = pre[...] + dot(pick(columns(src_rows - NC), blocks, 2 * SLOT), table)
    hidden, slope = activation(a)
    normed, inv = normed_of(hidden, w_outs[2])
    put_dst = put(dst_rows, blocks, NC)
    agg = dot(put_dst, normed.astype(BF)).astype(BF)
    agg_out[...] = agg
    a = pre_node[...] + dot(agg, w_node[128:, :])
    hidden_node, slope_node = activation(a)
    normed_node, inv_node = normed_of(hidden_node, w_outs[3])
    coarse_out[...] = (own[...].astype(F32) + normed_node).astype(BF)
    grad = grad_coarse[...].astype(F32)
    go = norm_back(grad, normed_node, inv_node)
    ga = (dot_nt(go, w_outs[3]) * slope_node).astype(BF)
    ga_out[...] = ga
    pair_node[0] = hidden_node
    pair_node[1] = go
    grad_total = grad + dot_nt(ga, w_node[:128, :])
    grad_agg = dot_nt(ga, w_node[128:, :]).astype(BF)
    grad = dot(pick(columns(dst_rows), blocks, NC), grad_agg)
    go = norm_back(grad, normed, inv)
    pair_edge[0] = hidden
    pair_edge[1] = go
    ga = (dot_nt(go, w_outs[2]) * slope).astype(BF)
    src_sums = dot(put(src_rows, blocks, NC + 2 * SLOT), ga).astype(BF)
    dst_sums = dot(put_dst, ga).astype(BF)
    sums_out[: NC + 2 * SLOT, :] = src_sums
    sums_out[NC + 2 * SLOT :, :] = dst_sums
    grad_ext = dot_nt(src_sums, w_in[:128, :])
    back_prev[...] = grad_ext[NC : NC + SLOT].astype(BF)
    back_next[...] = grad_ext[NC + SLOT :].astype(BF)
    grad_own[...] = grad_total + grad_ext[:NC] + dot_nt(dst_sums, w_in[128:, :])


def lift_kernel(
    own, cot, from_prev, from_next, coarse, sums, agg, ga, pair_node, pair_edge, refined, pool,
    w_outs, new_nodes, grads,
):
    part = 1.0 / 8.0
    rows = own[...]
    ext = jnp.concatenate([rows, from_prev[...], from_next[...]], 0)
    both = sums[...]
    lifted = dot(pick(columns(pool[...]), range(NF // 128), NC), coarse[...]).astype(BF)
    new_nodes[...] = (refined[...].astype(F32) + dot(lifted, w_outs[4])).astype(BF)
    grads[0:128, :] = (part * dot_tn(ext, both[: NC + 2 * SLOT])).astype(BF)
    grads[128:256, :] = (part * dot_tn(rows, both[NC + 2 * SLOT :])).astype(BF)
    grads[256:384, :] = (part * dot_tn(rows, ga[...])).astype(BF)
    grads[384:512, :] = (part * dot_tn(agg[...], ga[...])).astype(BF)
    grads[512:640, :] = (part * dot_tn(pair_edge[0], pair_edge[1])).astype(BF)
    grads[640:768, :] = (part * dot_tn(pair_node[0], pair_node[1])).astype(BF)
    grads[768:896, :] = (part * dot_tn(coarse[...], cot[...])).astype(BF)


def prep_kernel(
    act, act_node, w_outs, hidden_out, slope_out, normed_out, inv_out, hidden_node, slope_node,
    normed_node, inv_node,
):
    for c in range(EF // 128 // FINE_BLK):
        at = pl.ds(c * FINE_BLK * 128, FINE_BLK * 128)
        hidden, slope = activation(act[at, :])
        normed, inv = normed_of(hidden, w_outs[0])
        hidden_out[at, :] = hidden
        slope_out[at, :] = slope.astype(BF)
        normed_out[at, :] = normed.astype(BF)
        inv_out[at, :] = inv
    hidden, slope = activation(act_node[...])
    normed, inv = normed_of(hidden, w_outs[1])
    hidden_node[...] = hidden
    slope_node[...] = slope
    normed_node[...] = normed
    inv_node[...] = inv


def fine_back_kernel(
    live, counts, grad_own, divisor, ret_prev, ret_next, send, cot, pool, node, from_prev,
    from_next, agg, hidden, slope, normed, inv, hidden_node, slope_node, normed_node, inv_node,
    edge, cot_edges, src, dst, w_in, w_node, w_outs, coarse_grads,
    grad_edges_hbm, grad_node, back_prev, back_next, grads, grad_edges, sems,
):
    back = jnp.concatenate([ret_prev[...], ret_next[...]], 0)
    hot = put(live_slots(send[...], counts, GROUP), (0, 1), NC)
    grad_pool = (grad_own[...] + dot(hot, back)).astype(BF).astype(F32) / divisor[...]
    pooled = dot(pick(columns(pool[...]), range(NF // 128), NC), grad_pool.astype(BF))
    grad_refined = (cot[...].astype(F32) + pooled).astype(BF).astype(F32)
    go = norm_back(grad_refined, normed_node[...], inv_node[...])
    ga = (dot_nt(go, w_outs[1]) * slope_node[...]).astype(BF)
    grad_agg = dot_nt(ga, w_node[128:, :]).astype(BF)
    rows = node[...]
    grads[384:512, :] = dot_tn(rows, ga).astype(BF)
    grads[512:640, :] = dot_tn(agg[...], ga).astype(BF)
    grads[1280:1408, :] = dot_tn(hidden_node[...], go).astype(BF)
    grad_node[...] = grad_refined + dot_nt(ga, w_node[:128, :])
    src_rows = src[...]
    dst_rows = live_rows(dst[...], live[0:1, 0:1])
    dst_cols = columns(dst_rows)
    w_second = w_outs[0]
    first = jnp.zeros((L, L), F32)
    second = jnp.zeros((L, L), F32)
    sums = jnp.zeros((NF + 2 * SLOT + NF, L), F32)
    copies = []
    for c in range(EF // 128 // FINE_BLK):
        blocks = range(c * FINE_BLK, (c + 1) * FINE_BLK)
        at = pl.ds(c * FINE_BLK * 128, FINE_BLK * 128)
        gathered = dot(pick(dst_cols, blocks, NF), grad_agg)
        grad_new = (cot_edges[at, :].astype(F32) + gathered).astype(BF).astype(F32)
        here = lax.broadcasted_iota(I32, grad_new.shape, 0) + c * FINE_BLK * 128
        here = here < jnp.broadcast_to(live[0:1, 0:1], grad_new.shape)
        go = norm_back(jnp.where(here, grad_new, 0.0), normed[at, :].astype(F32), inv[at, :])
        ga = (dot_nt(go, w_second) * slope[at, :].astype(F32)).astype(BF)
        grad_edges[at, :] = (grad_new + dot_nt(ga, w_in[:128, :])).astype(BF)
        copies.append(pltpu.make_async_copy(grad_edges.at[at], grad_edges_hbm.at[at], sems.at[c]))
        copies[-1].start()
        first += dot_tn(edge[at, :], ga)
        second += dot_tn(hidden[at, :], go)
        hot = jnp.concatenate(
            [put(src_rows, blocks, NF + 2 * SLOT), put(dst_rows, blocks, NF)], 0
        )
        sums += dot(hot, ga)
    sums = sums.astype(BF)
    grad_ext = dot_nt(sums[: NF + 2 * SLOT], w_in[128:256, :])
    grad_node[...] += grad_ext[:NF] + dot_nt(sums[NF + 2 * SLOT :], w_in[256:, :])
    back_prev[...] = grad_ext[NF : NF + SLOT].astype(BF)
    back_next[...] = grad_ext[NF + SLOT :].astype(BF)
    ext = jnp.concatenate([rows, from_prev[...], from_next[...]], 0)
    grads[0:128, :] = first.astype(BF)
    grads[128:256, :] = dot_tn(ext, sums[: NF + 2 * SLOT]).astype(BF)
    grads[256:384, :] = dot_tn(rows, sums[NF + 2 * SLOT :]).astype(BF)
    grads[640:1152, :] = coarse_grads[0:512, :]
    grads[1152:1280, :] = second.astype(BF)
    grads[1408:1792, :] = coarse_grads[512:896, :]
    for copy in copies:
        copy.wait()


def added(parts):
    total = parts[0].astype(F32)
    for k in range(1, parts.shape[0]):
        total += parts[k].astype(F32)
    return total.astype(BF)


def plane_kernel(parts, counts, grad_node, ret_prev, ret_next, send, out, grad_nodes):
    total = added(parts)
    for k in range(out.shape[0]):
        out[k] = total
    back = jnp.concatenate([ret_prev[...], ret_next[...]], 0)
    hot = put(live_slots(send[...], counts, EVERY), (0, 1), NF)
    grad_nodes[...] = (grad_node[...] + dot(hot, back)).astype(BF)


def spread_kernel(parts, out):
    total = added(parts)
    for k in range(out.shape[0]):
        out[k] = total


def end_kernel(rows, edge_in, node_in, cedge_in, cnode_in, outs):
    edge_in[...] = rows[ROWS_EDGE:ROWS_NODE, :].astype(F32)
    node_in[...] = rows[ROWS_NODE:ROWS_CEDGE, :].astype(F32)
    cedge_in[...] = rows[ROWS_CEDGE:ROWS_CNODE, :].astype(F32)
    cnode_in[...] = rows[ROWS_CNODE:ROWS_OUTS, :].astype(F32)
    for k in range(5):
        outs[k] = rows[ROWS_OUTS + k * 128 : ROWS_OUTS + (k + 1) * 128, :].astype(F32)


def shift(value, axes, step):
    count = lax.axis_size(axes)
    return lax.ppermute(value, axes, [(i, (i + step) % count) for i in range(count)])


def rounds(values, axis):
    return tuple(shift(v, axis, k + 1) for k, v in enumerate(values))


def exchange(value, axes):
    return lax.all_to_all(value, axes, 0, 0)


def on_device(
    node, edge, src, dst, live, send, counts, pool, csrc, cdst, clive, csend, ccounts,
    w_edge, w_node, w_cedge, w_cnode, w_outs, cot, cot_edges,
):
    f32 = functools.partial(shape, dtype=F32)
    slots = (shape(SLOT, L), shape(SLOT, L))
    src, dst = src.reshape(EF // 128, 128), dst.reshape(EF // 128, 128)
    csrc, cdst = csrc.reshape(EC // 128, 128), cdst.reshape(EC // 128, 128)
    pool = pool.reshape(NF // 128, 128)
    send, csend = send.reshape(2, SLOT), csend.reshape(2, SLOT)
    edge_copies = (pltpu.VMEM((EF, L), BF), pltpu.SemaphoreType.DMA((EF // 128 // FINE_BLK,)))

    lives = call(
        begin_kernel, "begin", shape(8, 128, dtype=I32), (live, clive), 10**10, space=SMEM
    )
    to_prev, to_next = call(send_kernel, "send", slots, (lives, node, send, counts), 10**10)
    from_prev, from_next = shift(to_next, EVERY, 1), shift(to_prev, EVERY, -1)
    pre, side = call(
        pre_kernel, "pre", (f32(EF, L), shape(NC + CNT, L)),
        (node, w_edge, src, dst, edge, pool, cot),
    )
    new_edges, act, agg, act_node, refined, payload = call(
        fine_kernel, "fine",
        (shape(EF, L), f32(EF, L), shape(NF, L), f32(NF, L), shape(NF, L), shape(2 * NC + CNT, L)),
        (lives, pre, edge, node, from_prev, from_next, src, dst, w_edge, w_node, w_outs, pool, side),
        hbm_out=(0,), scratch=edge_copies,
    )
    pair = lax.all_gather(payload, "c", axis=0, tiled=False)
    total = call(pair_kernel, "pair", shape(2 * NC + CNT, L), (pair,), 10**6)
    others = rounds((total,) * 3, "y")
    prepared = call(
        prep_kernel, "prep",
        (shape(EF, L), shape(EF, L), shape(EF, L), f32(EF, 1),
         shape(NF, L), f32(NF, L), f32(NF, L), f32(NF, 1)),
        (act, act_node, w_outs),
    )
    own, pooled_cot, divisor, to_prev, to_next = call(
        pool_kernel, "pool", (shape(NC, L), shape(NC, L), f32(NC, L)) + slots,
        (total,) + others + (csend, ccounts), 10**7,
    )
    cfrom_prev, cfrom_next = shift(to_next, GROUP, 1), shift(to_prev, GROUP, -1)
    cpre, cpre_node, grad_coarse = call(
        coarse_pre_kernel, "coarse_pre", (f32(EC, L), f32(NC, L), shape(NC, L)),
        (own, pooled_cot, csrc, cdst, w_cedge, w_cnode, w_outs),
    )
    coarse, grad_own, back_prev, back_next, sums, cagg, cga, pair_node, pair_edge = call(
        coarse_kernel, "coarse",
        (shape(NC, L), f32(NC, L)) + slots
        + (shape(2 * NC + 2 * SLOT, L), shape(NC, L), shape(NC, L), shape(2, NC, L),
           shape(2, EC, L)),
        (lives, own, cpre, cpre_node, grad_coarse, cfrom_prev, cfrom_next, csrc, cdst,
         w_cedge, w_cnode, w_outs),
    )
    cret_prev, cret_next = shift(back_next, GROUP, 1), shift(back_prev, GROUP, -1)
    new_nodes, coarse_grads = call(
        lift_kernel, "lift", (shape(NF, L), shape(896, L)),
        (own, pooled_cot, cfrom_prev, cfrom_next, coarse, sums, cagg, cga, pair_node, pair_edge,
         refined, pool, w_outs),
    )
    grad_edges, grad_node, back_prev, back_next, grads = call(
        fine_back_kernel, "fine_back",
        (shape(EF, L), f32(NF, L)) + slots + (shape(GRADS, L),),
        (lives, ccounts, grad_own, divisor, cret_prev, cret_next, csend, cot, pool, node,
         from_prev, from_next, agg) + tuple(prepared)
        + (edge, cot_edges, src, dst, w_edge, w_node, w_outs, coarse_grads),
        hbm_out=(0,), scratch=edge_copies,
    )
    ret_prev, ret_next = shift(back_next, EVERY, 1), shift(back_prev, EVERY, -1)
    parts = exchange(grads.reshape(32, GRADS // 32, L), PLANE)
    spread, grad_nodes = call(
        plane_kernel, "sum_plane", (shape(8, GRADS // 32, L), shape(NF, L)),
        (parts, counts, grad_node, ret_prev, ret_next, send), 10**6,
    )
    parts = exchange(spread, "z")
    spread = call(spread_kernel, "sum_z", shape(32, GRADS // 32, L), (parts,), 10**6)
    rows = exchange(spread, PLANE).reshape(GRADS, L)
    weights = call(
        end_kernel, "end", (f32(384, L), f32(256, L), f32(256, L), f32(256, L), f32(5, L, L)),
        (rows,), 10**6,
    )
    return (new_nodes, new_edges, grad_nodes, grad_edges) + tuple(weights)


def solution(mesh):
    cube = Mesh(mesh.devices.reshape(8, 4, 4, 2), EVERY)
    fine, coarse = P(EVERY), P(GROUP)
    in_specs = (fine,) * 8 + (coarse,) * 5 + (P(),) * 5 + (fine,) * 2
    out_specs = (fine,) * 4 + (P(),) * 5
    return jax.shard_map(
        on_device, mesh=cube, in_specs=in_specs, out_specs=out_specs, check_vma=False
    )
```

```python
import functools

import jax
import jax.numpy as jnp
from jax import lax
from jax.experimental import pallas as pl
from jax.experimental.pallas import tpu as pltpu
from jax.sharding import Mesh
from jax.sharding import PartitionSpec as P

F32 = jnp.float32
BF = jnp.bfloat16
I32 = jnp.int32
EPS = 1e-05

L = 128
NF = 512
EF = 3072
NC = 256
EC = 1536
SLOT = 128
FINE_BLK = 8
COARSE_BLK = 12
CNT = 16
GRADS = 1792
ROWS_EDGE, ROWS_NODE, ROWS_CEDGE, ROWS_CNODE, ROWS_OUTS = 0, 384, 640, 896, 1152

EVERY = ("z", "x", "y", "c")
GROUP = ("z", "x")
PLANE = ("x", "y", "c")

VMEM = pl.BlockSpec(memory_space=pltpu.VMEM)
HBM = pl.BlockSpec(memory_space=pltpu.HBM)
SMEM = pl.BlockSpec(memory_space=pltpu.SMEM)


def call(kernel, name, out_shape, ins, flops=10**9, space=VMEM, hbm_out=(), scratch=()):
    size = sum(a.size * a.dtype.itemsize for a in ins)
    outs = out_shape if isinstance(out_shape, tuple) else (out_shape,)
    specs = tuple(HBM if k in hbm_out else VMEM for k in range(len(outs)))
    return pl.pallas_call(
        kernel,
        name=name,
        out_shape=out_shape,
        in_specs=[space] * len(ins),
        out_specs=specs if isinstance(out_shape, tuple) else specs[0],
        scratch_shapes=scratch,
        cost_estimate=pl.CostEstimate(flops=flops, bytes_accessed=size, transcendentals=0),
        compiler_params=pltpu.CompilerParams(vmem_limit_bytes=32 * 2**20),
    )(*ins)


def shape(*dims, dtype=BF):
    return jax.ShapeDtypeStruct(dims, dtype)


def dot(a, b):
    return jnp.dot(a, b, preferred_element_type=F32)


def dot_nt(a, b):
    return lax.dot_general(a, b, (((1,), (1,)), ((), ())), preferred_element_type=F32)


def dot_tn(a, b):
    return lax.dot_general(a, b, (((0,), (0,)), ((), ())), preferred_element_type=F32)


def mean(v):
    return jnp.mean(v, axis=-1, keepdims=True)


def columns(rows):
    pad = -rows.shape[0] % 8
    rows = rows.astype(F32)
    if pad:
        rows = jnp.concatenate([rows, jnp.zeros((pad, 128), F32)], 0)
    return rows.T.astype(I32)


def pick(cols, blocks, n):
    lane = lax.broadcasted_iota(I32, (128, n), 1)
    return jnp.concatenate(
        [jnp.where(lane == cols[:, j : j + 1], 1.0, 0.0).astype(BF) for j in blocks], 0
    )


def put(rows, blocks, n):
    line = lax.broadcasted_iota(I32, (n, 128), 0)
    return jnp.concatenate(
        [jnp.where(line == rows[j : j + 1, :], 1.0, 0.0).astype(BF) for j in blocks], 1
    )


def live_rows(rows, count):
    at = lax.broadcasted_iota(I32, rows.shape, 0) * 128 + lax.broadcasted_iota(I32, rows.shape, 1)
    return jnp.where(at < jnp.broadcast_to(count, rows.shape), rows, -1)


def live_slots(send, counts, axes):
    spot, last = 0, 1
    for axis in axes:
        spot = spot * lax.axis_size(axis) + lax.axis_index(axis)
        last = last * lax.axis_size(axis)
    there = ((spot > 0).astype(I32), (spot < last - 1).astype(I32))
    lane = lax.broadcasted_iota(I32, (1, SLOT), 1)
    return jnp.concatenate(
        [
            jnp.where(
                lane < jnp.broadcast_to(counts[0:1, s : s + 1], (1, SLOT)) * there[s],
                send[s : s + 1, :],
                -1,
            )
            for s in (0, 1)
        ],
        0,
    )


def sigmoid(a):
    return 1.0 / (1.0 + jnp.exp(-a))


def normed_of(hidden, w_second):
    outcome = dot(hidden, w_second)
    centred = outcome - mean(outcome)
    inv = lax.rsqrt(mean(centred * centred) + EPS)
    return centred * inv, inv


def activation(a):
    sig = sigmoid(a)
    return (a * sig).astype(BF), sig * (1.0 + a * (1.0 - sig))


def norm_back(grad, normed, inv):
    return (inv * (grad - mean(grad) - normed * mean(grad * normed))).astype(BF)


def forward(a, w_second):
    return normed_of((a * sigmoid(a)).astype(BF), w_second)[0]


def begin_kernel(live, clive, out):
    at = lax.broadcasted_iota(I32, out.shape, 0)
    out[...] = jnp.where(at == 0, live[0], jnp.where(at == 1, clive[0], 0))


def send_kernel(lives, node, send, counts, to_prev, to_next):
    cols = columns(live_slots(send[...] + lives[2:4, :], counts, EVERY))
    rows = node[...]
    to_prev[...] = dot(pick(cols, (0,), NF), rows).astype(BF)
    to_next[...] = dot(pick(cols, (1,), NF), rows).astype(BF)


def pre_kernel(node, w_in, src, dst, edge, pool, cot, pre, side, src_rows, dst_rows):
    w = w_in[...]
    rows = node[...]
    src_table = jnp.concatenate([dot(rows, w[128:256]).astype(BF), rows], 1)
    dst_table = jnp.concatenate([dot(rows, w[256:384]).astype(BF), rows], 1)
    src_cols, dst_cols = columns(src[...]), columns(dst[...])
    for c in range(EF // 128 // FINE_BLK):
        blocks = range(c * FINE_BLK, (c + 1) * FINE_BLK)
        at = pl.ds(c * FINE_BLK * 128, FINE_BLK * 128)
        from_src = dot(pick(src_cols, blocks, NF), src_table)
        from_dst = dot(pick(dst_cols, blocks, NF), dst_table)
        pre[at, :] = dot(edge[at, :], w[:128]) + from_src[:, :L] + from_dst[:, :L]
        src_rows[at, :] = from_src[:, L:].astype(BF)
        dst_rows[at, :] = from_dst[:, L:].astype(BF)
    pool_hot = put(pool[...], range(NF // 128), NC)
    side[0:NC, :] = dot(pool_hot, cot[...]).astype(BF)
    count = dot_nt(jnp.ones((8, NF), BF), pool_hot)
    high = jnp.floor(count * (1.0 / 16.0))
    low = count - 16.0 * high
    at = lax.broadcasted_iota(I32, (CNT, 128), 0)
    lines = jnp.zeros((CNT, 128), F32)
    for k, v in enumerate((high[0:1, :128], high[0:1, 128:], low[0:1, :128], low[0:1, 128:])):
        lines = jnp.where(at == k, v, lines)
    side[NC : NC + CNT, :] = lines.astype(BF)


def fine_kernel(
    live, pre, edge, node, from_prev, from_next, src, dst, w_in, w_node, w_outs, pool, side,
    new_edges_hbm, act, agg_out, act_node, refined, payload, new_edges, sems,
):
    halo = jnp.concatenate([from_prev[...], from_next[...]], 0)
    table = dot(halo, w_in[128:256, :]).astype(BF)
    src_cols = columns(src[...] - NF)
    dst_rows = live_rows(dst[...], live[0:1, 0:1])
    w_second = w_outs[0]
    total = jnp.zeros((NF, L), F32)
    copies = []
    for c in range(EF // 128 // FINE_BLK):
        blocks = range(c * FINE_BLK, (c + 1) * FINE_BLK)
        at = pl.ds(c * FINE_BLK * 128, FINE_BLK * 128)
        a = pre[at, :] + dot(pick(src_cols, blocks, 2 * SLOT), table)
        act[at, :] = a
        message = forward(a, w_second)
        here = lax.broadcasted_iota(I32, message.shape, 0) + c * FINE_BLK * 128
        here = here < jnp.broadcast_to(live[0:1, 0:1], message.shape)
        rows = (edge[at, :].astype(F32) + jnp.where(here, message, 0.0)).astype(BF)
        new_edges[at, :] = rows
        copies.append(pltpu.make_async_copy(new_edges.at[at], new_edges_hbm.at[at], sems.at[c]))
        copies[-1].start()
        total += dot(put(dst_rows, blocks, NF), rows)
    agg = total.astype(BF)
    agg_out[...] = agg
    a = dot(node[...], w_node[:128, :]) + dot(agg, w_node[128:, :])
    act_node[...] = a
    rows = (node[...].astype(F32) + forward(a, w_outs[1])).astype(BF)
    refined[...] = rows
    payload[0:NC, :] = dot(put(pool[...], range(NF // 128), NC), rows).astype(BF)
    payload[NC:, :] = side[...]
    for copy in copies:
        copy.wait()


def pair_kernel(a, b, out):
    out[...] = (a[...].astype(F32) + b[...].astype(F32)).astype(BF)


def pool_kernel(a, b, c, d, send, counts, own_out, cot_out, divisor, to_prev, to_next):
    total = a[...].astype(F32) + b[...].astype(F32) + c[...].astype(F32) + d[...].astype(F32)
    lines = total[2 * NC :, :]
    count = 16.0 * lines[0:2, :] + lines[2:4, :]
    cols = jnp.concatenate([count, jnp.ones((6, 128), F32)], 0).T
    count = jnp.concatenate(
        [jnp.broadcast_to(cols[:, k : k + 1], (128, L)) for k in (0, 1)], 0
    )
    own = (total[:NC, :] / count).astype(BF)
    own_out[...] = own
    cot_out[...] = total[NC : 2 * NC, :].astype(BF)
    divisor[...] = count
    cols = columns(live_slots(send[...], counts, GROUP))
    to_prev[...] = dot(pick(cols, (0,), NC), own).astype(BF)
    to_next[...] = dot(pick(cols, (1,), NC), own).astype(BF)


def coarse_pre_kernel(own, cot, src, dst, w_in, w_node, w_outs, pre, pre_node, grad_coarse):
    rows = own[...]
    table = jnp.concatenate([dot(rows, w_in[128:, :]), dot(rows, w_in[:128, :])], 0).astype(BF)
    src_cols, dst_cols = columns(src[...]), columns(dst[...])
    for c in range(EC // 128 // COARSE_BLK):
        blocks = range(c * COARSE_BLK, (c + 1) * COARSE_BLK)
        hot = jnp.concatenate([pick(dst_cols, blocks, NC), pick(src_cols, blocks, NC)], 1)
        pre[pl.ds(c * COARSE_BLK * 128, COARSE_BLK * 128), :] = dot(hot, table)
    pre_node[...] = dot(rows, w_node[:128, :])
    grad_coarse[...] = dot_nt(cot[...], w_outs[4]).astype(BF)


def coarse_kernel(
    live, own, pre, pre_node, grad_coarse, from_prev, from_next, src, dst, w_in, w_node, w_outs,
    coarse_out, grad_own, back_prev, back_next, sums_out, agg_out, ga_out, pair_node, pair_edge, ga_edge,
):
    halo = jnp.concatenate([from_prev[...], from_next[...]], 0)
    table = dot(halo, w_in[:128, :]).astype(BF)
    blocks = range(EC // 128)
    src_rows = src[...]
    dst_rows = live_rows(dst[...], live[1:2, 0:1])
    a = pre[...] + dot(pick(columns(src_rows - NC), blocks, 2 * SLOT), table)
    hidden, slope = activation(a)
    normed, inv = normed_of(hidden, w_outs[2])
    put_dst = put(dst_rows, blocks, NC)
    agg = dot(put_dst, normed.astype(BF)).astype(BF)
    agg_out[...] = agg
    a = pre_node[...] + dot(agg, w_node[128:, :])
    hidden_node, slope_node = activation(a)
    normed_node, inv_node = normed_of(hidden_node, w_outs[3])
    coarse_out[...] = (own[...].astype(F32) + normed_node).astype(BF)
    grad = grad_coarse[...].astype(F32)
    go = norm_back(grad, normed_node, inv_node)
    ga = (dot_nt(go, w_outs[3]) * slope_node).astype(BF)
    ga_out[...] = ga
    pair_node[0] = hidden_node
    pair_node[1] = go
    grad_total = grad + dot_nt(ga, w_node[:128, :])
    grad_agg = dot_nt(ga, w_node[128:, :]).astype(BF)
    grad = dot(pick(columns(dst_rows), blocks, NC), grad_agg)
    go = norm_back(grad, normed, inv)
    pair_edge[0] = hidden
    pair_edge[1] = go
    ga = (dot_nt(go, w_outs[2]) * slope).astype(BF)
    src_sums = dot(put(src_rows, blocks, NC + 2 * SLOT), ga).astype(BF)
    sums_out[...] = src_sums
    ga_edge[...] = ga
    grad_ext = dot_nt(src_sums, w_in[:128, :])
    back_prev[...] = grad_ext[NC : NC + SLOT].astype(BF)
    back_next[...] = grad_ext[NC + SLOT :].astype(BF)
    grad_own[...] = grad_total + grad_ext[:NC]


def lift_kernel(
    own, cot, from_prev, from_next, coarse, grad_part, sums, agg, ga, pair_node, pair_edge,
    ga_edge, dst, w_in, refined, pool, w_outs, new_nodes, grads, grad_own,
):
    part = 1.0 / 8.0
    rows = own[...]
    ext = jnp.concatenate([rows, from_prev[...], from_next[...]], 0)
    dst_sums = dot(put(dst[...], range(EC // 128), NC), ga_edge[...]).astype(BF)
    grad_own[...] = grad_part[...] + dot_nt(dst_sums, w_in[128:, :])
    lifted = dot(pick(columns(pool[...]), range(NF // 128), NC), coarse[...]).astype(BF)
    new_nodes[...] = (refined[...].astype(F32) + dot(lifted, w_outs[4])).astype(BF)
    grads[0:128, :] = (part * dot_tn(ext, sums[...])).astype(BF)
    grads[128:256, :] = (part * dot_tn(rows, dst_sums)).astype(BF)
    grads[256:384, :] = (part * dot_tn(rows, ga[...])).astype(BF)
    grads[384:512, :] = (part * dot_tn(agg[...], ga[...])).astype(BF)
    grads[512:640, :] = (part * dot_tn(pair_edge[0], pair_edge[1])).astype(BF)
    grads[640:768, :] = (part * dot_tn(pair_node[0], pair_node[1])).astype(BF)
    grads[768:896, :] = (part * dot_tn(coarse[...], cot[...])).astype(BF)


def prep_kernel(
    act, act_node, w_outs, src, from_prev, from_next, src_part, src_rows, hidden_out, slope_out, normed_out, inv_out, hidden_node, slope_node,
    normed_node, inv_node,
):
    halo = jnp.concatenate([from_prev[...], from_next[...]], 0)
    src_cols = columns(src[...] - NF)
    for c in range(EF // 128 // FINE_BLK):
        at = pl.ds(c * FINE_BLK * 128, FINE_BLK * 128)
        blocks = range(c * FINE_BLK, (c + 1) * FINE_BLK)
        src_rows[at, :] = src_part[at, :] + dot(pick(src_cols, blocks, 2 * SLOT), halo).astype(BF)
        hidden, slope = activation(act[at, :])
        normed, inv = normed_of(hidden, w_outs[0])
        hidden_out[at, :] = hidden
        slope_out[at, :] = slope.astype(BF)
        normed_out[at, :] = normed.astype(BF)
        inv_out[at, :] = inv
    hidden, slope = activation(act_node[...])
    normed, inv = normed_of(hidden, w_outs[1])
    hidden_node[...] = hidden
    slope_node[...] = slope
    normed_node[...] = normed
    inv_node[...] = inv


def fine_back_kernel(
    lives, counts, grad_own, divisor, ret_prev, ret_next, send, cot, pool, node, agg, src_rows,
    hidden, slope, normed, inv, hidden_node, slope_node, normed_node, inv_node, dst_rows, edge,
    cot_edges, src, dst, w_in, w_node, w_outs, coarse_grads, grad_new, ga_out, grad_node, grads,
    back_prev, back_next,
):
    back = jnp.concatenate([ret_prev[...], ret_next[...]], 0)
    hot = put(live_slots(send[...], counts, GROUP), (0, 1), NC)
    grad_pool = (grad_own[...] + dot(hot, back)).astype(BF).astype(F32) / divisor[...]
    pooled = dot(pick(columns(pool[...]), range(NF // 128), NC), grad_pool.astype(BF))
    grad_refined = (cot[...].astype(F32) + pooled).astype(BF).astype(F32)
    go = norm_back(grad_refined, normed_node[...], inv_node[...])
    ga = (dot_nt(go, w_outs[1]) * slope_node[...]).astype(BF)
    grad_agg = dot_nt(ga, w_node[128:, :]).astype(BF)
    grads[384:512, :] = dot_tn(node[...], ga).astype(BF)
    grads[512:640, :] = dot_tn(agg[...], ga).astype(BF)
    grads[1280:1408, :] = dot_tn(hidden_node[...], go).astype(BF)
    grad_node[...] = grad_refined + dot_nt(ga, w_node[:128, :])
    dst_cols = columns(live_rows(dst[...], lives[0:1, 0:1]))
    slot_rows = src[...] - NF
    sums = jnp.zeros((2 * SLOT, L), F32)
    w_second = w_outs[0]
    totals = [jnp.zeros((L, L), F32) for _ in range(4)]
    for c in range(EF // 128 // FINE_BLK):
        blocks = range(c * FINE_BLK, (c + 1) * FINE_BLK)
        at = pl.ds(c * FINE_BLK * 128, FINE_BLK * 128)
        gathered = dot(pick(dst_cols, blocks, NF), grad_agg)
        total = (cot_edges[at, :].astype(F32) + gathered).astype(BF)
        grad_new[at, :] = total
        here = lax.broadcasted_iota(I32, total.shape, 0) + c * FINE_BLK * 128
        here = here < jnp.broadcast_to(lives[0:1, 0:1], total.shape)
        total = jnp.where(here, total.astype(F32), 0.0)
        go = norm_back(total, normed[at, :].astype(F32), inv[at, :])
        ga = (dot_nt(go, w_second) * slope[at, :].astype(F32)).astype(BF)
        ga_out[at, :] = ga
        sums += dot(put(slot_rows, blocks, 2 * SLOT), ga)
        for k, rows in enumerate((edge, src_rows, dst_rows)):
            totals[k] += dot_tn(rows[at, :], ga)
        totals[3] += dot_tn(hidden[at, :], go)
    sums = dot_nt(sums.astype(BF), w_in[128:256, :])
    back_prev[...] = sums[:SLOT].astype(BF)
    back_next[...] = sums[SLOT:].astype(BF)
    for k in range(3):
        grads[k * 128 : (k + 1) * 128, :] = totals[k].astype(BF)
    grads[640:1152, :] = coarse_grads[0:512, :]
    grads[1152:1280, :] = totals[3].astype(BF)
    grads[1408:1792, :] = coarse_grads[512:896, :]


def fine_rest_kernel(
    counts, grad_new, ga, grad_part, src, dst, w_in, ret_prev, ret_next, send, grad_edges_hbm,
    grad_nodes, grad_edges, sems,
):
    src_rows, dst_rows = src[...], dst[...]
    src_sums = jnp.zeros((NF, L), F32)
    dst_sums = jnp.zeros((NF, L), F32)
    copies = []
    for c in range(EF // 128 // FINE_BLK):
        blocks = range(c * FINE_BLK, (c + 1) * FINE_BLK)
        at = pl.ds(c * FINE_BLK * 128, FINE_BLK * 128)
        rows = ga[at, :]
        grad_edges[at, :] = (
            grad_new[at, :].astype(F32) + dot_nt(rows, w_in[:128, :])
        ).astype(BF)
        copies.append(pltpu.make_async_copy(grad_edges.at[at], grad_edges_hbm.at[at], sems.at[c]))
        copies[-1].start()
        src_sums += dot(put(src_rows, blocks, NF), rows)
        dst_sums += dot(put(dst_rows, blocks, NF), rows)
    back = jnp.concatenate([ret_prev[...], ret_next[...]], 0)
    hot = put(live_slots(send[...], counts, EVERY), (0, 1), NF)
    grad_nodes[...] = (
        grad_part[...]
        + dot_nt(src_sums.astype(BF), w_in[128:256, :])
        + dot_nt(dst_sums.astype(BF), w_in[256:, :])
        + dot(hot, back)
    ).astype(BF)
    for copy in copies:
        copy.wait()


def added(parts):
    total = parts[0].astype(F32)
    for k in range(1, parts.shape[0]):
        total += parts[k].astype(F32)
    return total.astype(BF)


def plane_kernel(parts, ret_prev, ret_next, out):
    total = added(parts)
    for k in range(out.shape[0]):
        out[k] = total


def spread_kernel(parts, out):
    total = added(parts)
    for k in range(out.shape[0]):
        out[k] = total


def end_kernel(rows, edge_in, node_in, cedge_in, cnode_in, outs):
    edge_in[...] = rows[ROWS_EDGE:ROWS_NODE, :].astype(F32)
    node_in[...] = rows[ROWS_NODE:ROWS_CEDGE, :].astype(F32)
    cedge_in[...] = rows[ROWS_CEDGE:ROWS_CNODE, :].astype(F32)
    cnode_in[...] = rows[ROWS_CNODE:ROWS_OUTS, :].astype(F32)
    for k in range(5):
        outs[k] = rows[ROWS_OUTS + k * 128 : ROWS_OUTS + (k + 1) * 128, :].astype(F32)


def shift(value, axes, step):
    count = lax.axis_size(axes)
    return lax.ppermute(value, axes, [(i, (i + step) % count) for i in range(count)])


def rounds(values, axis):
    return tuple(shift(v, axis, k + 1) for k, v in enumerate(values))


def exchange(value, axes):
    return lax.all_to_all(value, axes, 0, 0)


def on_device(
    node, edge, src, dst, live, send, counts, pool, csrc, cdst, clive, csend, ccounts,
    w_edge, w_node, w_cedge, w_cnode, w_outs, cot, cot_edges,
):
    f32 = functools.partial(shape, dtype=F32)
    slots = (shape(SLOT, L), shape(SLOT, L))
    src, dst = src.reshape(EF // 128, 128), dst.reshape(EF // 128, 128)
    csrc, cdst = csrc.reshape(EC // 128, 128), cdst.reshape(EC // 128, 128)
    pool = pool.reshape(NF // 128, 128)
    send, csend = send.reshape(2, SLOT), csend.reshape(2, SLOT)
    edge_copies = (pltpu.VMEM((EF, L), BF), pltpu.SemaphoreType.DMA((EF // 128 // FINE_BLK,)))

    lives = call(
        begin_kernel, "begin", shape(8, 128, dtype=I32), (live, clive), 10**10, space=SMEM
    )
    to_prev, to_next = call(send_kernel, "send", slots, (lives, node, send, counts), 10**10)
    from_prev, from_next = shift(to_next, EVERY, 1), shift(to_prev, EVERY, -1)
    pre, side, src_part, dst_rows = call(
        pre_kernel, "pre", (f32(EF, L), shape(NC + CNT, L), shape(EF, L), shape(EF, L)),
        (node, w_edge, src, dst, edge, pool, cot),
    )
    new_edges, act, agg, act_node, refined, payload = call(
        fine_kernel, "fine",
        (shape(EF, L), f32(EF, L), shape(NF, L), f32(NF, L), shape(NF, L), shape(2 * NC + CNT, L)),
        (lives, pre, edge, node, from_prev, from_next, src, dst, w_edge, w_node, w_outs, pool, side),
        hbm_out=(0,), scratch=edge_copies,
    )
    total = call(
        pair_kernel, "pair", shape(2 * NC + CNT, L), (payload, shift(payload, "c", 1)), 10**6
    )
    others = rounds((total,) * 3, "y")
    prepared = call(
        prep_kernel, "prep",
        (shape(EF, L), shape(EF, L), shape(EF, L), shape(EF, L), f32(EF, 1),
         shape(NF, L), f32(NF, L), f32(NF, L), f32(NF, 1)),
        (act, act_node, w_outs, src, from_prev, from_next, src_part),
    )
    own, pooled_cot, divisor, to_prev, to_next = call(
        pool_kernel, "pool", (shape(NC, L), shape(NC, L), f32(NC, L)) + slots,
        (total,) + others + (csend, ccounts), 10**7,
    )
    cfrom_prev, cfrom_next = shift(to_next, GROUP, 1), shift(to_prev, GROUP, -1)
    cpre, cpre_node, grad_coarse = call(
        coarse_pre_kernel, "coarse_pre", (f32(EC, L), f32(NC, L), shape(NC, L)),
        (own, pooled_cot, csrc, cdst, w_cedge, w_cnode, w_outs),
    )
    coarse, grad_part, back_prev, back_next, sums, cagg, cga, pair_node, pair_edge, cga_edge = call(
        coarse_kernel, "coarse",
        (shape(NC, L), f32(NC, L)) + slots
        + (shape(NC + 2 * SLOT, L), shape(NC, L), shape(NC, L), shape(2, NC, L),
           shape(2, EC, L), shape(EC, L)),
        (lives, own, cpre, cpre_node, grad_coarse, cfrom_prev, cfrom_next, csrc, cdst,
         w_cedge, w_cnode, w_outs),
    )
    cret_prev, cret_next = shift(back_next, GROUP, 1), shift(back_prev, GROUP, -1)
    new_nodes, coarse_grads, grad_own = call(
        lift_kernel, "lift", (shape(NF, L), shape(896, L), f32(NC, L)),
        (own, pooled_cot, cfrom_prev, cfrom_next, coarse, grad_part, sums, cagg, cga, pair_node,
         pair_edge, cga_edge, cdst, w_cedge, refined, pool, w_outs),
    )
    grad_new, ga, grad_part, grads, back_prev, back_next = call(
        fine_back_kernel, "fine_back",
        (shape(EF, L), shape(EF, L), f32(NF, L), shape(GRADS, L)) + slots,
        (lives, ccounts, grad_own, divisor, cret_prev, cret_next, csend, cot, pool, node, agg)
        + tuple(prepared)
        + (dst_rows, edge, cot_edges, src, dst, w_edge, w_node, w_outs, coarse_grads),
    )
    ret_prev, ret_next = shift(back_next, EVERY, 1), shift(back_prev, EVERY, -1)
    parts = exchange(grads.reshape(32, GRADS // 32, L), PLANE)
    spread = call(
        plane_kernel, "sum_plane", shape(8, GRADS // 32, L), (parts, ret_prev, ret_next), 10**6
    )
    grad_edges, grad_nodes = call(
        fine_rest_kernel, "fine_rest", (shape(EF, L), shape(NF, L)),
        (counts, grad_new, ga, grad_part, src, dst, w_edge, ret_prev, ret_next, send),
        hbm_out=(0,), scratch=edge_copies,
    )
    parts = exchange(spread, "z")
    spread = call(spread_kernel, "sum_z", shape(32, GRADS // 32, L), (parts,), 10**6)
    rows = exchange(spread, PLANE).reshape(GRADS, L)
    weights = call(
        end_kernel, "end", (f32(384, L), f32(256, L), f32(256, L), f32(256, L), f32(5, L, L)),
        (rows,), 10**6,
    )
    return (new_nodes, new_edges, grad_nodes, grad_edges) + tuple(weights)


def solution(mesh):
    cube = Mesh(mesh.devices.reshape(8, 4, 4, 2), EVERY)
    fine, coarse = P(EVERY), P(GROUP)
    in_specs = (fine,) * 8 + (coarse,) * 5 + (P(),) * 5 + (fine,) * 2
    out_specs = (fine,) * 4 + (P(),) * 5
    return jax.shard_map(
        on_device, mesh=cube, in_specs=in_specs, out_specs=out_specs, check_vma=False
    )
```

```python
import functools

import jax
import jax.numpy as jnp
from jax import lax
from jax.experimental import pallas as pl
from jax.experimental.pallas import tpu as pltpu
from jax.sharding import Mesh
from jax.sharding import PartitionSpec as P

F32 = jnp.float32
BF = jnp.bfloat16
I32 = jnp.int32
EPS = 1e-05

L = 128
NF = 512
EF = 3072
NC = 256
EC = 1536
SLOT = 128
FINE_BLK = 8
COARSE_BLK = 12
CNT = 16
PART = 272
GRADS = 1792
ROWS_EDGE, ROWS_NODE, ROWS_CEDGE, ROWS_CNODE, ROWS_OUTS = 0, 384, 640, 896, 1152

EVERY = ("z", "x", "y", "c")
GROUP = ("z", "x")
PLANE = ("x", "y", "c")

VMEM = pl.BlockSpec(memory_space=pltpu.VMEM)
HBM = pl.BlockSpec(memory_space=pltpu.HBM)
SMEM = pl.BlockSpec(memory_space=pltpu.SMEM)


def call(kernel, name, out_shape, ins, flops=10**9, space=VMEM, hbm_out=(), scratch=()):
    size = sum(a.size * a.dtype.itemsize for a in ins)
    outs = out_shape if isinstance(out_shape, tuple) else (out_shape,)
    specs = tuple(HBM if k in hbm_out else VMEM for k in range(len(outs)))
    return pl.pallas_call(
        kernel,
        name=name,
        out_shape=out_shape,
        in_specs=[space] * len(ins),
        out_specs=specs if isinstance(out_shape, tuple) else specs[0],
        scratch_shapes=scratch,
        cost_estimate=pl.CostEstimate(flops=flops, bytes_accessed=size, transcendentals=0),
        compiler_params=pltpu.CompilerParams(vmem_limit_bytes=32 * 2**20),
    )(*ins)


def shape(*dims, dtype=BF):
    return jax.ShapeDtypeStruct(dims, dtype)


def dot(a, b):
    return jnp.dot(a, b, preferred_element_type=F32)


def dot_nt(a, b):
    return lax.dot_general(a, b, (((1,), (1,)), ((), ())), preferred_element_type=F32)


def dot_tn(a, b):
    return lax.dot_general(a, b, (((0,), (0,)), ((), ())), preferred_element_type=F32)


def mean(v):
    return jnp.mean(v, axis=-1, keepdims=True)


def columns(rows):
    pad = -rows.shape[0] % 8
    rows = rows.astype(F32)
    if pad:
        rows = jnp.concatenate([rows, jnp.zeros((pad, 128), F32)], 0)
    return rows.T.astype(I32)


def pick(cols, blocks, n):
    lane = lax.broadcasted_iota(I32, (128, n), 1)
    return jnp.concatenate(
        [jnp.where(lane == cols[:, j : j + 1], 1.0, 0.0).astype(BF) for j in blocks], 0
    )


def put(rows, blocks, n):
    line = lax.broadcasted_iota(I32, (n, 128), 0)
    return jnp.concatenate(
        [jnp.where(line == rows[j : j + 1, :], 1.0, 0.0).astype(BF) for j in blocks], 1
    )


def live_rows(rows, count):
    at = lax.broadcasted_iota(I32, rows.shape, 0) * 128 + lax.broadcasted_iota(I32, rows.shape, 1)
    return jnp.where(at < jnp.broadcast_to(count, rows.shape), rows, -1)


def live_slots(send, counts, axes):
    spot, last = 0, 1
    for axis in axes:
        spot = spot * lax.axis_size(axis) + lax.axis_index(axis)
        last = last * lax.axis_size(axis)
    there = ((spot > 0).astype(I32), (spot < last - 1).astype(I32))
    lane = lax.broadcasted_iota(I32, (1, SLOT), 1)
    return jnp.concatenate(
        [
            jnp.where(
                lane < jnp.broadcast_to(counts[0:1, s : s + 1], (1, SLOT)) * there[s],
                send[s : s + 1, :],
                -1,
            )
            for s in (0, 1)
        ],
        0,
    )


def sigmoid(a):
    return 1.0 / (1.0 + jnp.exp(-a))


def normed_of(hidden, w_second):
    outcome = dot(hidden, w_second)
    centred = outcome - mean(outcome)
    inv = lax.rsqrt(mean(centred * centred) + EPS)
    return centred * inv, inv


def activation(a):
    sig = sigmoid(a)
    return (a * sig).astype(BF), sig * (1.0 + a * (1.0 - sig))


def norm_back(grad, normed, inv):
    return (inv * (grad - mean(grad) - normed * mean(grad * normed))).astype(BF)


def forward(a, w_second):
    return normed_of((a * sigmoid(a)).astype(BF), w_second)[0]


def begin_kernel(live, clive, out):
    at = lax.broadcasted_iota(I32, out.shape, 0)
    out[...] = jnp.where(at == 0, live[0], jnp.where(at == 1, clive[0], 0))


def send_kernel(lives, node, send, counts, to_prev, to_next):
    cols = columns(live_slots(send[...] + lives[2:4, :], counts, EVERY))
    rows = node[...]
    to_prev[...] = dot(pick(cols, (0,), NF), rows).astype(BF)
    to_next[...] = dot(pick(cols, (1,), NF), rows).astype(BF)


def pre_kernel(node, w_in, src, dst, edge, pool, cot, pre, side, src_rows, dst_rows):
    w = w_in[...]
    rows = node[...]
    src_table = jnp.concatenate([dot(rows, w[128:256]).astype(BF), rows], 1)
    dst_table = jnp.concatenate([dot(rows, w[256:384]).astype(BF), rows], 1)
    src_cols, dst_cols = columns(src[...]), columns(dst[...])
    for c in range(EF // 128 // FINE_BLK):
        blocks = range(c * FINE_BLK, (c + 1) * FINE_BLK)
        at = pl.ds(c * FINE_BLK * 128, FINE_BLK * 128)
        from_src = dot(pick(src_cols, blocks, NF), src_table)
        from_dst = dot(pick(dst_cols, blocks, NF), dst_table)
        pre[at, :] = dot(edge[at, :], w[:128]) + from_src[:, :L] + from_dst[:, :L]
        src_rows[at, :] = from_src[:, L:].astype(BF)
        dst_rows[at, :] = from_dst[:, L:].astype(BF)
    pool_hot = put(pool[...], range(NF // 128), NC)
    side[0:NC, :] = dot(pool_hot, cot[...]).astype(BF)
    count = dot_nt(jnp.ones((8, NF), BF), pool_hot)
    high = jnp.floor(count * (1.0 / 16.0))
    low = count - 16.0 * high
    at = lax.broadcasted_iota(I32, (CNT, 128), 0)
    lines = jnp.zeros((CNT, 128), F32)
    for k, v in enumerate((high[0:1, :128], high[0:1, 128:], low[0:1, :128], low[0:1, 128:])):
        lines = jnp.where(at == k, v, lines)
    side[NC : NC + CNT, :] = lines.astype(BF)


def fine_kernel(
    live, pre, edge, node, from_prev, from_next, src, dst, w_in, w_node, w_outs, pool, side,
    new_edges_hbm, act, agg_out, act_node, refined, payload, new_edges, sems,
):
    halo = jnp.concatenate([from_prev[...], from_next[...]], 0)
    table = dot(halo, w_in[128:256, :]).astype(BF)
    src_cols = columns(src[...] - NF)
    dst_rows = live_rows(dst[...], live[0:1, 0:1])
    w_second = w_outs[0]
    total = jnp.zeros((NF, L), F32)
    copies = []
    for c in range(EF // 128 // FINE_BLK):
        blocks = range(c * FINE_BLK, (c + 1) * FINE_BLK)
        at = pl.ds(c * FINE_BLK * 128, FINE_BLK * 128)
        a = pre[at, :] + dot(pick(src_cols, blocks, 2 * SLOT), table)
        act[at, :] = a
        message = forward(a, w_second)
        here = lax.broadcasted_iota(I32, message.shape, 0) + c * FINE_BLK * 128
        here = here < jnp.broadcast_to(live[0:1, 0:1], message.shape)
        rows = (edge[at, :].astype(F32) + jnp.where(here, message, 0.0)).astype(BF)
        new_edges[at, :] = rows
        copies.append(pltpu.make_async_copy(new_edges.at[at], new_edges_hbm.at[at], sems.at[c]))
        copies[-1].start()
        total += dot(put(dst_rows, blocks, NF), rows)
    agg = total.astype(BF)
    agg_out[...] = agg
    a = dot(node[...], w_node[:128, :]) + dot(agg, w_node[128:, :])
    act_node[...] = a
    rows = (node[...].astype(F32) + forward(a, w_outs[1])).astype(BF)
    refined[...] = rows
    payload[0:NC, :] = dot(put(pool[...], range(NF // 128), NC), rows).astype(BF)
    payload[NC:, :] = side[...]
    for copy in copies:
        copy.wait()


def pair_kernel(a, b, out, part):
    out[...] = (a[...].astype(F32) + b[...].astype(F32)).astype(BF)
    part[...] = out[pl.ds(pl.multiple_of(lax.axis_index("c") * NC, NC), PART), :]


def join_kernel(own, near, part, ahead, out, total):
    core = lax.axis_index("c")
    total[...] = near[...].astype(F32) + jnp.where(core == 0, own[...].astype(F32), 0.0)
    line = lax.broadcasted_iota(I32, (PART, L), 0)
    rows = jnp.where(line < NC + core * PART, part[...].astype(F32), 0.0)
    at = pl.ds(pl.multiple_of(core * NC, NC), PART)
    total[at, :] = total[at, :] + rows
    out[...] = total[...].astype(BF)


def pool_kernel(a, b, send, counts, own_out, cot_out, divisor, to_prev, to_next):
    total = a[...].astype(F32) + b[...].astype(F32)
    lines = total[2 * NC :, :]
    count = 16.0 * lines[0:2, :] + lines[2:4, :]
    cols = jnp.concatenate([count, jnp.ones((6, 128), F32)], 0).T
    count = jnp.concatenate(
        [jnp.broadcast_to(cols[:, k : k + 1], (128, L)) for k in (0, 1)], 0
    )
    own = (total[:NC, :] / count).astype(BF)
    own_out[...] = own
    cot_out[...] = total[NC : 2 * NC, :].astype(BF)
    divisor[...] = count
    cols = columns(live_slots(send[...], counts, GROUP))
    to_prev[...] = dot(pick(cols, (0,), NC), own).astype(BF)
    to_next[...] = dot(pick(cols, (1,), NC), own).astype(BF)


def coarse_pre_kernel(own, cot, src, dst, w_in, w_node, w_outs, pre, pre_node, grad_coarse):
    rows = own[...]
    table = jnp.concatenate([dot(rows, w_in[128:, :]), dot(rows, w_in[:128, :])], 0).astype(BF)
    src_cols, dst_cols = columns(src[...]), columns(dst[...])
    for c in range(EC // 128 // COARSE_BLK):
        blocks = range(c * COARSE_BLK, (c + 1) * COARSE_BLK)
        hot = jnp.concatenate([pick(dst_cols, blocks, NC), pick(src_cols, blocks, NC)], 1)
        pre[pl.ds(c * COARSE_BLK * 128, COARSE_BLK * 128), :] = dot(hot, table)
    pre_node[...] = dot(rows, w_node[:128, :])
    grad_coarse[...] = dot_nt(cot[...], w_outs[4]).astype(BF)


def coarse_kernel(
    live, own, pre, pre_node, grad_coarse, from_prev, from_next, src, dst, w_in, w_node, w_outs,
    coarse_out, grad_own, back_prev, back_next, sums_out, agg_out, ga_out, pair_node, pair_edge, ga_edge,
):
    halo = jnp.concatenate([from_prev[...], from_next[...]], 0)
    table = dot(halo, w_in[:128, :]).astype(BF)
    blocks = range(EC // 128)
    src_rows = src[...]
    dst_rows = live_rows(dst[...], live[1:2, 0:1])
    a = pre[...] + dot(pick(columns(src_rows - NC), blocks, 2 * SLOT), table)
    hidden, slope = activation(a)
    normed, inv = normed_of(hidden, w_outs[2])
    put_dst = put(dst_rows, blocks, NC)
    agg = dot(put_dst, normed.astype(BF)).astype(BF)
    agg_out[...] = agg
    a = pre_node[...] + dot(agg, w_node[128:, :])
    hidden_node, slope_node = activation(a)
    normed_node, inv_node = normed_of(hidden_node, w_outs[3])
    coarse_out[...] = (own[...].astype(F32) + normed_node).astype(BF)
    grad = grad_coarse[...].astype(F32)
    go = norm_back(grad, normed_node, inv_node)
    ga = (dot_nt(go, w_outs[3]) * slope_node).astype(BF)
    ga_out[...] = ga
    pair_node[0] = hidden_node
    pair_node[1] = go
    grad_total = grad + dot_nt(ga, w_node[:128, :])
    grad_agg = dot_nt(ga, w_node[128:, :]).astype(BF)
    grad = dot(pick(columns(dst_rows), blocks, NC), grad_agg)
    go = norm_back(grad, normed, inv)
    pair_edge[0] = hidden
    pair_edge[1] = go
    ga = (dot_nt(go, w_outs[2]) * slope).astype(BF)
    src_sums = dot(put(src_rows, blocks, NC + 2 * SLOT), ga).astype(BF)
    sums_out[...] = src_sums
    ga_edge[...] = ga
    grad_ext = dot_nt(src_sums, w_in[:128, :])
    back_prev[...] = grad_ext[NC : NC + SLOT].astype(BF)
    back_next[...] = grad_ext[NC + SLOT :].astype(BF)
    grad_own[...] = grad_total + grad_ext[:NC]


def lift_kernel(
    own, cot, from_prev, from_next, coarse, grad_part, sums, agg, ga, pair_node, pair_edge,
    ga_edge, dst, w_in, refined, pool, w_outs, new_nodes, grads, grad_own,
):
    part = 1.0 / 8.0
    rows = own[...]
    ext = jnp.concatenate([rows, from_prev[...], from_next[...]], 0)
    dst_sums = dot(put(dst[...], range(EC // 128), NC), ga_edge[...]).astype(BF)
    grad_own[...] = grad_part[...] + dot_nt(dst_sums, w_in[128:, :])
    lifted = dot(pick(columns(pool[...]), range(NF // 128), NC), coarse[...]).astype(BF)
    new_nodes[...] = (refined[...].astype(F32) + dot(lifted, w_outs[4])).astype(BF)
    grads[0:128, :] = (part * dot_tn(ext, sums[...])).astype(BF)
    grads[128:256, :] = (part * dot_tn(rows, dst_sums)).astype(BF)
    grads[256:384, :] = (part * dot_tn(rows, ga[...])).astype(BF)
    grads[384:512, :] = (part * dot_tn(agg[...], ga[...])).astype(BF)
    grads[512:640, :] = (part * dot_tn(pair_edge[0], pair_edge[1])).astype(BF)
    grads[640:768, :] = (part * dot_tn(pair_node[0], pair_node[1])).astype(BF)
    grads[768:896, :] = (part * dot_tn(coarse[...], cot[...])).astype(BF)


def prep_kernel(
    act, act_node, w_outs, src, from_prev, from_next, src_part, src_rows, hidden_out, slope_out, normed_out, inv_out, hidden_node, slope_node,
    normed_node, inv_node,
):
    halo = jnp.concatenate([from_prev[...], from_next[...]], 0)
    src_cols = columns(src[...] - NF)
    for c in range(EF // 128 // FINE_BLK):
        at = pl.ds(c * FINE_BLK * 128, FINE_BLK * 128)
        blocks = range(c * FINE_BLK, (c + 1) * FINE_BLK)
        src_rows[at, :] = src_part[at, :] + dot(pick(src_cols, blocks, 2 * SLOT), halo).astype(BF)
        hidden, slope = activation(act[at, :])
        normed, inv = normed_of(hidden, w_outs[0])
        hidden_out[at, :] = hidden
        slope_out[at, :] = slope.astype(BF)
        normed_out[at, :] = normed.astype(BF)
        inv_out[at, :] = inv
    hidden, slope = activation(act_node[...])
    normed, inv = normed_of(hidden, w_outs[1])
    hidden_node[...] = hidden
    slope_node[...] = slope
    normed_node[...] = normed
    inv_node[...] = inv


def fine_back_kernel(
    lives, counts, grad_own, divisor, ret_prev, ret_next, send, cot, pool, node, agg, src_rows,
    hidden, slope, normed, inv, hidden_node, slope_node, normed_node, inv_node, dst_rows, edge,
    cot_edges, src, dst, w_in, w_node, w_outs, coarse_grads, grad_new, ga_out, grad_node, grads,
    back_prev, back_next,
):
    back = jnp.concatenate([ret_prev[...], ret_next[...]], 0)
    hot = put(live_slots(send[...], counts, GROUP), (0, 1), NC)
    grad_pool = (grad_own[...] + dot(hot, back)).astype(BF).astype(F32) / divisor[...]
    pooled = dot(pick(columns(pool[...]), range(NF // 128), NC), grad_pool.astype(BF))
    grad_refined = (cot[...].astype(F32) + pooled).astype(BF).astype(F32)
    go = norm_back(grad_refined, normed_node[...], inv_node[...])
    ga = (dot_nt(go, w_outs[1]) * slope_node[...]).astype(BF)
    grad_agg = dot_nt(ga, w_node[128:, :]).astype(BF)
    grads[384:512, :] = dot_tn(node[...], ga).astype(BF)
    grads[512:640, :] = dot_tn(agg[...], ga).astype(BF)
    grads[1280:1408, :] = dot_tn(hidden_node[...], go).astype(BF)
    grad_node[...] = grad_refined + dot_nt(ga, w_node[:128, :])
    dst_cols = columns(live_rows(dst[...], lives[0:1, 0:1]))
    slot_rows = src[...] - NF
    sums = jnp.zeros((2 * SLOT, L), F32)
    w_second = w_outs[0]
    totals = [jnp.zeros((L, L), F32) for _ in range(4)]
    for c in range(EF // 128 // FINE_BLK):
        blocks = range(c * FINE_BLK, (c + 1) * FINE_BLK)
        at = pl.ds(c * FINE_BLK * 128, FINE_BLK * 128)
        gathered = dot(pick(dst_cols, blocks, NF), grad_agg)
        total = (cot_edges[at, :].astype(F32) + gathered).astype(BF)
        grad_new[at, :] = total
        here = lax.broadcasted_iota(I32, total.shape, 0) + c * FINE_BLK * 128
        here = here < jnp.broadcast_to(lives[0:1, 0:1], total.shape)
        total = jnp.where(here, total.astype(F32), 0.0)
        go = norm_back(total, normed[at, :].astype(F32), inv[at, :])
        ga = (dot_nt(go, w_second) * slope[at, :].astype(F32)).astype(BF)
        ga_out[at, :] = ga
        sums += dot(put(slot_rows, blocks, 2 * SLOT), ga)
        for k, rows in enumerate((edge, src_rows, dst_rows)):
            totals[k] += dot_tn(rows[at, :], ga)
        totals[3] += dot_tn(hidden[at, :], go)
    sums = dot_nt(sums.astype(BF), w_in[128:256, :])
    back_prev[...] = sums[:SLOT].astype(BF)
    back_next[...] = sums[SLOT:].astype(BF)
    for k in range(3):
        grads[k * 128 : (k + 1) * 128, :] = totals[k].astype(BF)
    grads[640:1152, :] = coarse_grads[0:512, :]
    grads[1152:1280, :] = totals[3].astype(BF)
    grads[1408:1792, :] = coarse_grads[512:896, :]


def fine_rest_kernel(
    counts, grad_new, ga, grad_part, src, dst, w_in, ret_prev, ret_next, send, grad_edges_hbm,
    grad_nodes, grad_edges, sems,
):
    src_rows, dst_rows = src[...], dst[...]
    src_sums = jnp.zeros((NF, L), F32)
    dst_sums = jnp.zeros((NF, L), F32)
    copies = []
    for c in range(EF // 128 // FINE_BLK):
        blocks = range(c * FINE_BLK, (c + 1) * FINE_BLK)
        at = pl.ds(c * FINE_BLK * 128, FINE_BLK * 128)
        rows = ga[at, :]
        grad_edges[at, :] = (
            grad_new[at, :].astype(F32) + dot_nt(rows, w_in[:128, :])
        ).astype(BF)
        copies.append(pltpu.make_async_copy(grad_edges.at[at], grad_edges_hbm.at[at], sems.at[c]))
        copies[-1].start()
        src_sums += dot(put(src_rows, blocks, NF), rows)
        dst_sums += dot(put(dst_rows, blocks, NF), rows)
    back = jnp.concatenate([ret_prev[...], ret_next[...]], 0)
    hot = put(live_slots(send[...], counts, EVERY), (0, 1), NF)
    grad_nodes[...] = (
        grad_part[...]
        + dot_nt(src_sums.astype(BF), w_in[128:256, :])
        + dot_nt(dst_sums.astype(BF), w_in[256:, :])
        + dot(hot, back)
    ).astype(BF)
    for copy in copies:
        copy.wait()


def added(parts):
    total = parts[0].astype(F32)
    for k in range(1, parts.shape[0]):
        total += parts[k].astype(F32)
    return total.astype(BF)


def plane_kernel(parts, ret_prev, ret_next, out):
    total = added(parts)
    for k in range(out.shape[0]):
        out[k] = total


def spread_kernel(parts, out):
    total = added(parts)
    for k in range(out.shape[0]):
        out[k] = total


def end_kernel(rows, edge_in, node_in, cedge_in, cnode_in, outs):
    edge_in[...] = rows[ROWS_EDGE:ROWS_NODE, :].astype(F32)
    node_in[...] = rows[ROWS_NODE:ROWS_CEDGE, :].astype(F32)
    cedge_in[...] = rows[ROWS_CEDGE:ROWS_CNODE, :].astype(F32)
    cnode_in[...] = rows[ROWS_CNODE:ROWS_OUTS, :].astype(F32)
    for k in range(5):
        outs[k] = rows[ROWS_OUTS + k * 128 : ROWS_OUTS + (k + 1) * 128, :].astype(F32)


def shift(value, axes, step):
    count = lax.axis_size(axes)
    return lax.ppermute(value, axes, [(i, (i + step) % count) for i in range(count)])


def cross(value):
    size = {axis: lax.axis_size(axis) for axis in EVERY}
    count = size["z"] * size["x"] * size["y"] * size["c"]
    pairs = []
    for i in range(count):
        core, y = i % size["c"], i // size["c"] % size["y"]
        to = (y + 1 - 2 * core) % size["y"]
        pairs.append((i, i + (to - y) * size["c"]))
    return lax.ppermute(value, EVERY, pairs)


def exchange(value, axes):
    return lax.all_to_all(value, axes, 0, 0)


def on_device(
    node, edge, src, dst, live, send, counts, pool, csrc, cdst, clive, csend, ccounts,
    w_edge, w_node, w_cedge, w_cnode, w_outs, cot, cot_edges,
):
    f32 = functools.partial(shape, dtype=F32)
    slots = (shape(SLOT, L), shape(SLOT, L))
    src, dst = src.reshape(EF // 128, 128), dst.reshape(EF // 128, 128)
    csrc, cdst = csrc.reshape(EC // 128, 128), cdst.reshape(EC // 128, 128)
    pool = pool.reshape(NF // 128, 128)
    send, csend = send.reshape(2, SLOT), csend.reshape(2, SLOT)
    edge_copies = (pltpu.VMEM((EF, L), BF), pltpu.SemaphoreType.DMA((EF // 128 // FINE_BLK,)))

    lives = call(
        begin_kernel, "begin", shape(8, 128, dtype=I32), (live, clive), 10**10, space=SMEM
    )
    to_prev, to_next = call(send_kernel, "send", slots, (lives, node, send, counts), 10**10)
    from_prev, from_next = shift(to_next, EVERY, 1), shift(to_prev, EVERY, -1)
    pre, side, src_part, dst_rows = call(
        pre_kernel, "pre", (f32(EF, L), shape(NC + CNT, L), shape(EF, L), shape(EF, L)),
        (node, w_edge, src, dst, edge, pool, cot),
    )
    new_edges, act, agg, act_node, refined, payload = call(
        fine_kernel, "fine",
        (shape(EF, L), f32(EF, L), shape(NF, L), f32(NF, L), shape(NF, L), shape(2 * NC + CNT, L)),
        (lives, pre, edge, node, from_prev, from_next, src, dst, w_edge, w_node, w_outs, pool, side),
        hbm_out=(0,), scratch=edge_copies,
    )
    total, part = call(
        pair_kernel, "pair", (shape(2 * NC + CNT, L), shape(PART, L)),
        (payload, shift(payload, "c", 1)), 10**6,
    )
    near, part = cross(total), shift(part, "y", 2)
    prepared = call(
        prep_kernel, "prep",
        (shape(EF, L), shape(EF, L), shape(EF, L), shape(EF, L), f32(EF, 1),
         shape(NF, L), f32(NF, L), f32(NF, L), f32(NF, 1)),
        (act, act_node, w_outs, src, from_prev, from_next, src_part),
    )
    joined = call(
        join_kernel, "join", shape(2 * NC + CNT, L), (total, near, part, prepared[-1]), 10**6,
        scratch=(pltpu.VMEM((2 * NC + CNT, L), F32),),
    )
    own, pooled_cot, divisor, to_prev, to_next = call(
        pool_kernel, "pool", (shape(NC, L), shape(NC, L), f32(NC, L)) + slots,
        (joined, shift(joined, "c", 1), csend, ccounts), 10**7,
    )
    cfrom_prev, cfrom_next = shift(to_next, GROUP, 1), shift(to_prev, GROUP, -1)
    cpre, cpre_node, grad_coarse = call(
        coarse_pre_kernel, "coarse_pre", (f32(EC, L), f32(NC, L), shape(NC, L)),
        (own, pooled_cot, csrc, cdst, w_cedge, w_cnode, w_outs),
    )
    coarse, grad_part, back_prev, back_next, sums, cagg, cga, pair_node, pair_edge, cga_edge = call(
        coarse_kernel, "coarse",
        (shape(NC, L), f32(NC, L)) + slots
        + (shape(NC + 2 * SLOT, L), shape(NC, L), shape(NC, L), shape(2, NC, L),
           shape(2, EC, L), shape(EC, L)),
        (lives, own, cpre, cpre_node, grad_coarse, cfrom_prev, cfrom_next, csrc, cdst,
         w_cedge, w_cnode, w_outs),
    )
    cret_prev, cret_next = shift(back_next, GROUP, 1), shift(back_prev, GROUP, -1)
    new_nodes, coarse_grads, grad_own = call(
        lift_kernel, "lift", (shape(NF, L), shape(896, L), f32(NC, L)),
        (own, pooled_cot, cfrom_prev, cfrom_next, coarse, grad_part, sums, cagg, cga, pair_node,
         pair_edge, cga_edge, cdst, w_cedge, refined, pool, w_outs),
    )
    grad_new, ga, grad_part, grads, back_prev, back_next = call(
        fine_back_kernel, "fine_back",
        (shape(EF, L), shape(EF, L), f32(NF, L), shape(GRADS, L)) + slots,
        (lives, ccounts, grad_own, divisor, cret_prev, cret_next, csend, cot, pool, node, agg)
        + tuple(prepared)
        + (dst_rows, edge, cot_edges, src, dst, w_edge, w_node, w_outs, coarse_grads),
    )
    ret_prev, ret_next = shift(back_next, EVERY, 1), shift(back_prev, EVERY, -1)
    parts = exchange(grads.reshape(32, GRADS // 32, L), PLANE)
    spread = call(
        plane_kernel, "sum_plane", shape(8, GRADS // 32, L), (parts, ret_prev, ret_next), 10**6
    )
    grad_edges, grad_nodes = call(
        fine_rest_kernel, "fine_rest", (shape(EF, L), shape(NF, L)),
        (counts, grad_new, ga, grad_part, src, dst, w_edge, ret_prev, ret_next, send),
        hbm_out=(0,), scratch=edge_copies,
    )
    parts = exchange(spread, "z")
    spread = call(spread_kernel, "sum_z", shape(32, GRADS // 32, L), (parts,), 10**6)
    rows = exchange(spread, PLANE).reshape(GRADS, L)
    weights = call(
        end_kernel, "end", (f32(384, L), f32(256, L), f32(256, L), f32(256, L), f32(5, L, L)),
        (rows,), 10**6,
    )
    return (new_nodes, new_edges, grad_nodes, grad_edges) + tuple(weights)


def solution(mesh):
    cube = Mesh(mesh.devices.reshape(8, 4, 4, 2), EVERY)
    fine, coarse = P(EVERY), P(GROUP)
    in_specs = (fine,) * 8 + (coarse,) * 5 + (P(),) * 5 + (fine,) * 2
    out_specs = (fine,) * 4 + (P(),) * 5
    return jax.shard_map(
        on_device, mesh=cube, in_specs=in_specs, out_specs=out_specs, check_vma=False
    )
```

```python
import functools

import jax
import jax.numpy as jnp
from jax import lax
from jax.experimental import pallas as pl
from jax.experimental.pallas import tpu as pltpu
from jax.sharding import Mesh
from jax.sharding import PartitionSpec as P

F32 = jnp.float32
BF = jnp.bfloat16
I32 = jnp.int32
EPS = 1e-05

L = 128
NF = 512
EF = 3072
NC = 256
EC = 1536
SLOT = 128
FINE_BLK = 8
COARSE_BLK = 12
CNT = 16
PART = 272
GRADS = 1792
ROWS_EDGE, ROWS_NODE, ROWS_CEDGE, ROWS_CNODE, ROWS_OUTS = 0, 384, 640, 896, 1152

EVERY = ("z", "x", "y", "c")
GROUP = ("z", "x")
PLANE = ("x", "y", "c")

VMEM = pl.BlockSpec(memory_space=pltpu.VMEM)
HBM = pl.BlockSpec(memory_space=pltpu.HBM)
SMEM = pl.BlockSpec(memory_space=pltpu.SMEM)


def call(kernel, name, out_shape, ins, flops=10**9, space=VMEM, hbm_out=(), scratch=()):
    size = sum(a.size * a.dtype.itemsize for a in ins)
    outs = out_shape if isinstance(out_shape, tuple) else (out_shape,)
    specs = tuple(HBM if k in hbm_out else VMEM for k in range(len(outs)))
    return pl.pallas_call(
        kernel,
        name=name,
        out_shape=out_shape,
        in_specs=[space] * len(ins),
        out_specs=specs if isinstance(out_shape, tuple) else specs[0],
        scratch_shapes=scratch,
        cost_estimate=pl.CostEstimate(flops=flops, bytes_accessed=size, transcendentals=0),
        compiler_params=pltpu.CompilerParams(vmem_limit_bytes=32 * 2**20),
    )(*ins)


def shape(*dims, dtype=BF):
    return jax.ShapeDtypeStruct(dims, dtype)


def dot(a, b):
    return jnp.dot(a, b, preferred_element_type=F32)


def dot_nt(a, b):
    return lax.dot_general(a, b, (((1,), (1,)), ((), ())), preferred_element_type=F32)


def dot_tn(a, b):
    return lax.dot_general(a, b, (((0,), (0,)), ((), ())), preferred_element_type=F32)


def mean(v):
    return jnp.mean(v, axis=-1, keepdims=True)


def columns(rows):
    pad = -rows.shape[0] % 8
    rows = rows.astype(F32)
    if pad:
        rows = jnp.concatenate([rows, jnp.zeros((pad, 128), F32)], 0)
    return rows.T.astype(I32)


def pick(cols, blocks, n):
    lane = lax.broadcasted_iota(I32, (128, n), 1)
    return jnp.concatenate(
        [jnp.where(lane == cols[:, j : j + 1], 1.0, 0.0).astype(BF) for j in blocks], 0
    )


def put(rows, blocks, n):
    line = lax.broadcasted_iota(I32, (n, 128), 0)
    return jnp.concatenate(
        [jnp.where(line == rows[j : j + 1, :], 1.0, 0.0).astype(BF) for j in blocks], 1
    )


def live_rows(rows, count):
    at = lax.broadcasted_iota(I32, rows.shape, 0) * 128 + lax.broadcasted_iota(I32, rows.shape, 1)
    return jnp.where(at < jnp.broadcast_to(count, rows.shape), rows, -1)


def live_slots(send, counts, axes):
    spot, last = 0, 1
    for axis in axes:
        spot = spot * lax.axis_size(axis) + lax.axis_index(axis)
        last = last * lax.axis_size(axis)
    there = ((spot > 0).astype(I32), (spot < last - 1).astype(I32))
    lane = lax.broadcasted_iota(I32, (1, SLOT), 1)
    return jnp.concatenate(
        [
            jnp.where(
                lane < jnp.broadcast_to(counts[0:1, s : s + 1], (1, SLOT)) * there[s],
                send[s : s + 1, :],
                -1,
            )
            for s in (0, 1)
        ],
        0,
    )


def sigmoid(a):
    return 1.0 / (1.0 + jnp.exp(-a))


def normed_of(hidden, w_second):
    outcome = dot(hidden, w_second)
    centred = outcome - mean(outcome)
    inv = lax.rsqrt(mean(centred * centred) + EPS)
    return centred * inv, inv


def activation(a):
    sig = sigmoid(a)
    return (a * sig).astype(BF), sig * (1.0 + a * (1.0 - sig))


def norm_back(grad, normed, inv):
    return (inv * (grad - mean(grad) - normed * mean(grad * normed))).astype(BF)


def forward(a, w_second):
    return normed_of((a * sigmoid(a)).astype(BF), w_second)[0]


def begin_kernel(live, clive, out):
    at = lax.broadcasted_iota(I32, out.shape, 0)
    out[...] = jnp.where(at == 0, live[0], jnp.where(at == 1, clive[0], 0))


def send_kernel(lives, node, send, counts, to_prev, to_next):
    cols = columns(live_slots(send[...] + lives[2:4, :], counts, EVERY))
    rows = node[...]
    to_prev[...] = dot(pick(cols, (0,), NF), rows).astype(BF)
    to_next[...] = dot(pick(cols, (1,), NF), rows).astype(BF)


def pre_kernel(node, w_in, src, dst, edge, pool, cot, pre, side, src_rows, dst_rows):
    w = w_in[...]
    rows = node[...]
    src_table = jnp.concatenate([dot(rows, w[128:256]).astype(BF), rows], 1)
    dst_table = jnp.concatenate([dot(rows, w[256:384]).astype(BF), rows], 1)
    src_cols, dst_cols = columns(src[...]), columns(dst[...])
    for c in range(EF // 128 // FINE_BLK):
        blocks = range(c * FINE_BLK, (c + 1) * FINE_BLK)
        at = pl.ds(c * FINE_BLK * 128, FINE_BLK * 128)
        from_src = dot(pick(src_cols, blocks, NF), src_table)
        from_dst = dot(pick(dst_cols, blocks, NF), dst_table)
        pre[at, :] = dot(edge[at, :], w[:128]) + from_src[:, :L] + from_dst[:, :L]
        src_rows[at, :] = from_src[:, L:].astype(BF)
        dst_rows[at, :] = from_dst[:, L:].astype(BF)
    pool_hot = put(pool[...], range(NF // 128), NC)
    side[0:NC, :] = dot(pool_hot, cot[...]).astype(BF)
    count = dot_nt(jnp.ones((8, NF), BF), pool_hot)
    high = jnp.floor(count * (1.0 / 16.0))
    low = count - 16.0 * high
    at = lax.broadcasted_iota(I32, (CNT, 128), 0)
    lines = jnp.zeros((CNT, 128), F32)
    for k, v in enumerate((high[0:1, :128], high[0:1, 128:], low[0:1, :128], low[0:1, 128:])):
        lines = jnp.where(at == k, v, lines)
    side[NC : NC + CNT, :] = lines.astype(BF)


def fine_kernel(
    live, pre, edge, node, from_prev, from_next, src, dst, w_in, w_node, w_outs, pool, side,
    new_edges_hbm, act, agg_out, act_node, refined, payload, new_edges, sems,
):
    halo = jnp.concatenate([from_prev[...], from_next[...]], 0)
    table = dot(halo, w_in[128:256, :]).astype(BF)
    src_cols = columns(src[...] - NF)
    dst_rows = live_rows(dst[...], live[0:1, 0:1])
    w_second = w_outs[0]
    total = jnp.zeros((NF, L), F32)
    copies = []
    for c in range(EF // 128 // FINE_BLK):
        blocks = range(c * FINE_BLK, (c + 1) * FINE_BLK)
        at = pl.ds(c * FINE_BLK * 128, FINE_BLK * 128)
        a = pre[at, :] + dot(pick(src_cols, blocks, 2 * SLOT), table)
        act[at, :] = a
        message = forward(a, w_second)
        here = lax.broadcasted_iota(I32, message.shape, 0) + c * FINE_BLK * 128
        here = here < jnp.broadcast_to(live[0:1, 0:1], message.shape)
        rows = (edge[at, :].astype(F32) + jnp.where(here, message, 0.0)).astype(BF)
        new_edges[at, :] = rows
        copies.append(pltpu.make_async_copy(new_edges.at[at], new_edges_hbm.at[at], sems.at[c]))
        copies[-1].start()
        total += dot(put(dst_rows, blocks, NF), rows)
    agg = total.astype(BF)
    agg_out[...] = agg
    a = dot(node[...], w_node[:128, :]) + dot(agg, w_node[128:, :])
    act_node[...] = a
    rows = (node[...].astype(F32) + forward(a, w_outs[1])).astype(BF)
    refined[...] = rows
    payload[0:NC, :] = dot(put(pool[...], range(NF // 128), NC), rows).astype(BF)
    payload[NC:, :] = side[...]
    for copy in copies:
        copy.wait()


def pair_kernel(a, b, out, part):
    out[...] = (a[...].astype(F32) + b[...].astype(F32)).astype(BF)
    part[...] = out[pl.ds(pl.multiple_of(lax.axis_index("c") * NC, NC), PART), :]


def join_kernel(own, near, part, ahead, out, total):
    core = lax.axis_index("c")
    total[...] = near[...].astype(F32) + jnp.where(core == 0, own[...].astype(F32), 0.0)
    line = lax.broadcasted_iota(I32, (PART, L), 0)
    rows = jnp.where(line < NC + core * PART, part[...].astype(F32), 0.0)
    at = pl.ds(pl.multiple_of(core * NC, NC), PART)
    total[at, :] = total[at, :] + rows
    out[...] = total[...].astype(BF)


def pool_kernel(a, b, send, counts, own_out, cot_out, divisor, to_prev, to_next):
    total = a[...].astype(F32) + b[...].astype(F32)
    lines = total[2 * NC :, :]
    count = 16.0 * lines[0:2, :] + lines[2:4, :]
    cols = jnp.concatenate([count, jnp.ones((6, 128), F32)], 0).T
    count = jnp.concatenate(
        [jnp.broadcast_to(cols[:, k : k + 1], (128, L)) for k in (0, 1)], 0
    )
    own = (total[:NC, :] / count).astype(BF)
    own_out[...] = own
    cot_out[...] = total[NC : 2 * NC, :].astype(BF)
    divisor[...] = count
    cols = columns(live_slots(send[...], counts, GROUP))
    to_prev[...] = dot(pick(cols, (0,), NC), own).astype(BF)
    to_next[...] = dot(pick(cols, (1,), NC), own).astype(BF)


def coarse_pre_kernel(own, cot, src, dst, w_in, w_node, w_outs, pre, pre_node, grad_coarse):
    rows = own[...]
    table = jnp.concatenate([dot(rows, w_in[128:, :]), dot(rows, w_in[:128, :])], 0).astype(BF)
    src_cols, dst_cols = columns(src[...]), columns(dst[...])
    for c in range(EC // 128 // COARSE_BLK):
        blocks = range(c * COARSE_BLK, (c + 1) * COARSE_BLK)
        hot = jnp.concatenate([pick(dst_cols, blocks, NC), pick(src_cols, blocks, NC)], 1)
        pre[pl.ds(c * COARSE_BLK * 128, COARSE_BLK * 128), :] = dot(hot, table)
    pre_node[...] = dot(rows, w_node[:128, :])
    grad_coarse[...] = dot_nt(cot[...], w_outs[4]).astype(BF)


def coarse_kernel(
    live, own, pre, pre_node, grad_coarse, from_prev, from_next, src, dst, w_in, w_node, w_outs,
    coarse_out, grad_own, back_prev, back_next, sums_out, agg_out, ga_out, pair_node, pair_edge, ga_edge,
):
    halo = jnp.concatenate([from_prev[...], from_next[...]], 0)
    table = dot(halo, w_in[:128, :]).astype(BF)
    blocks = range(EC // 128)
    src_rows = src[...]
    dst_rows = live_rows(dst[...], live[1:2, 0:1])
    a = pre[...] + dot(pick(columns(src_rows - NC), blocks, 2 * SLOT), table)
    hidden, slope = activation(a)
    normed, inv = normed_of(hidden, w_outs[2])
    put_dst = put(dst_rows, blocks, NC)
    agg = dot(put_dst, normed.astype(BF)).astype(BF)
    agg_out[...] = agg
    a = pre_node[...] + dot(agg, w_node[128:, :])
    hidden_node, slope_node = activation(a)
    normed_node, inv_node = normed_of(hidden_node, w_outs[3])
    coarse_out[...] = (own[...].astype(F32) + normed_node).astype(BF)
    grad = grad_coarse[...].astype(F32)
    go = norm_back(grad, normed_node, inv_node)
    ga = (dot_nt(go, w_outs[3]) * slope_node).astype(BF)
    ga_out[...] = ga
    pair_node[0] = hidden_node
    pair_node[1] = go
    grad_total = grad + dot_nt(ga, w_node[:128, :])
    grad_agg = dot_nt(ga, w_node[128:, :]).astype(BF)
    grad = dot(pick(columns(dst_rows), blocks, NC), grad_agg)
    go = norm_back(grad, normed, inv)
    pair_edge[0] = hidden
    pair_edge[1] = go
    ga = (dot_nt(go, w_outs[2]) * slope).astype(BF)
    src_sums = dot(put(src_rows - NC, blocks, 2 * SLOT), ga).astype(BF)
    sums_out[...] = src_sums
    ga_edge[...] = ga
    grad_ext = dot_nt(src_sums, w_in[:128, :])
    back_prev[...] = grad_ext[:SLOT].astype(BF)
    back_next[...] = grad_ext[SLOT:].astype(BF)
    grad_own[...] = grad_total


def lift_kernel(
    own, cot, from_prev, from_next, coarse, grad_part, sums, agg, ga, pair_node, pair_edge,
    ga_edge, src, dst, w_in, refined, pool, w_outs, new_nodes, grads, grad_own,
):
    part = 1.0 / 8.0
    rows = own[...]
    ext = jnp.concatenate([rows, from_prev[...], from_next[...]], 0)
    dst_sums = dot(put(dst[...], range(EC // 128), NC), ga_edge[...]).astype(BF)
    src_sums = dot(put(src[...], range(EC // 128), NC), ga_edge[...]).astype(BF)
    grad_own[...] = (
        grad_part[...] + dot_nt(src_sums, w_in[:128, :]) + dot_nt(dst_sums, w_in[128:, :])
    )
    src_sums = jnp.concatenate([src_sums, sums[...]], 0)
    lifted = dot(pick(columns(pool[...]), range(NF // 128), NC), coarse[...]).astype(BF)
    new_nodes[...] = (refined[...].astype(F32) + dot(lifted, w_outs[4])).astype(BF)
    grads[0:128, :] = (part * dot_tn(ext, src_sums)).astype(BF)
    grads[128:256, :] = (part * dot_tn(rows, dst_sums)).astype(BF)
    grads[256:384, :] = (part * dot_tn(rows, ga[...])).astype(BF)
    grads[384:512, :] = (part * dot_tn(agg[...], ga[...])).astype(BF)
    grads[512:640, :] = (part * dot_tn(pair_edge[0], pair_edge[1])).astype(BF)
    grads[640:768, :] = (part * dot_tn(pair_node[0], pair_node[1])).astype(BF)
    grads[768:896, :] = (part * dot_tn(coarse[...], cot[...])).astype(BF)


def prep_kernel(
    act, act_node, w_outs, src, from_prev, from_next, src_part, src_rows, hidden_out, slope_out, normed_out, inv_out, hidden_node, slope_node,
    normed_node, inv_node,
):
    halo = jnp.concatenate([from_prev[...], from_next[...]], 0)
    src_cols = columns(src[...] - NF)
    for c in range(EF // 128 // FINE_BLK):
        at = pl.ds(c * FINE_BLK * 128, FINE_BLK * 128)
        blocks = range(c * FINE_BLK, (c + 1) * FINE_BLK)
        src_rows[at, :] = src_part[at, :] + dot(pick(src_cols, blocks, 2 * SLOT), halo).astype(BF)
        hidden, slope = activation(act[at, :])
        normed, inv = normed_of(hidden, w_outs[0])
        hidden_out[at, :] = hidden
        slope_out[at, :] = slope.astype(BF)
        normed_out[at, :] = normed.astype(BF)
        inv_out[at, :] = inv
    hidden, slope = activation(act_node[...])
    normed, inv = normed_of(hidden, w_outs[1])
    hidden_node[...] = hidden
    slope_node[...] = slope
    normed_node[...] = normed
    inv_node[...] = inv


def fine_back_kernel(
    lives, counts, grad_own, divisor, ret_prev, ret_next, send, cot, pool, node, agg, src_rows,
    hidden, slope, normed, inv, hidden_node, slope_node, normed_node, inv_node, dst_rows, edge,
    cot_edges, src, dst, w_in, w_node, w_outs, coarse_grads, grad_new, ga_out, grad_node, ga_node,
    grads, back_prev, back_next,
):
    back = jnp.concatenate([ret_prev[...], ret_next[...]], 0)
    hot = put(live_slots(send[...], counts, GROUP), (0, 1), NC)
    grad_pool = (grad_own[...] + dot(hot, back)).astype(BF).astype(F32) / divisor[...]
    pooled = dot(pick(columns(pool[...]), range(NF // 128), NC), grad_pool.astype(BF))
    grad_refined = (cot[...].astype(F32) + pooled).astype(BF).astype(F32)
    go = norm_back(grad_refined, normed_node[...], inv_node[...])
    ga = (dot_nt(go, w_outs[1]) * slope_node[...]).astype(BF)
    grad_agg = dot_nt(ga, w_node[128:, :]).astype(BF)
    grads[384:512, :] = dot_tn(node[...], ga).astype(BF)
    grads[512:640, :] = dot_tn(agg[...], ga).astype(BF)
    grads[1280:1408, :] = dot_tn(hidden_node[...], go).astype(BF)
    grad_node[...] = grad_refined.astype(BF)
    ga_node[...] = ga
    dst_cols = columns(live_rows(dst[...], lives[0:1, 0:1]))
    slot_rows = src[...] - NF
    sums = jnp.zeros((2 * SLOT, L), F32)
    w_second = w_outs[0]
    totals = [jnp.zeros((L, L), F32) for _ in range(4)]
    for c in range(EF // 128 // FINE_BLK):
        blocks = range(c * FINE_BLK, (c + 1) * FINE_BLK)
        at = pl.ds(c * FINE_BLK * 128, FINE_BLK * 128)
        gathered = dot(pick(dst_cols, blocks, NF), grad_agg)
        total = (cot_edges[at, :].astype(F32) + gathered).astype(BF)
        grad_new[at, :] = total
        here = lax.broadcasted_iota(I32, total.shape, 0) + c * FINE_BLK * 128
        here = here < jnp.broadcast_to(lives[0:1, 0:1], total.shape)
        total = jnp.where(here, total.astype(F32), 0.0)
        go = norm_back(total, normed[at, :].astype(F32), inv[at, :])
        ga = (dot_nt(go, w_second) * slope[at, :].astype(F32)).astype(BF)
        ga_out[at, :] = ga
        sums += dot(put(slot_rows, blocks, 2 * SLOT), ga)
        for k, rows in enumerate((edge, src_rows, dst_rows)):
            totals[k] += dot_tn(rows[at, :], ga)
        totals[3] += dot_tn(hidden[at, :], go)
    sums = dot_nt(sums.astype(BF), w_in[128:256, :])
    back_prev[...] = sums[:SLOT].astype(BF)
    back_next[...] = sums[SLOT:].astype(BF)
    for k in range(3):
        grads[k * 128 : (k + 1) * 128, :] = totals[k].astype(BF)
    grads[640:1152, :] = coarse_grads[0:512, :]
    grads[1152:1280, :] = totals[3].astype(BF)
    grads[1408:1792, :] = coarse_grads[512:896, :]


def fine_rest_kernel(
    counts, grad_new, ga, grad_part, ga_node, src, dst, w_in, w_node, ret_prev, ret_next, send,
    grad_edges_hbm,
    grad_nodes, grad_edges, sems,
):
    src_rows, dst_rows = src[...], dst[...]
    src_sums = jnp.zeros((NF, L), F32)
    dst_sums = jnp.zeros((NF, L), F32)
    copies = []
    for c in range(EF // 128 // FINE_BLK):
        blocks = range(c * FINE_BLK, (c + 1) * FINE_BLK)
        at = pl.ds(c * FINE_BLK * 128, FINE_BLK * 128)
        rows = ga[at, :]
        grad_edges[at, :] = (
            grad_new[at, :].astype(F32) + dot_nt(rows, w_in[:128, :])
        ).astype(BF)
        copies.append(pltpu.make_async_copy(grad_edges.at[at], grad_edges_hbm.at[at], sems.at[c]))
        copies[-1].start()
        src_sums += dot(put(src_rows, blocks, NF), rows)
        dst_sums += dot(put(dst_rows, blocks, NF), rows)
    back = jnp.concatenate([ret_prev[...], ret_next[...]], 0)
    hot = put(live_slots(send[...], counts, EVERY), (0, 1), NF)
    grad_nodes[...] = (
        grad_part[...].astype(F32)
        + dot_nt(ga_node[...], w_node[:128, :])
        + dot_nt(src_sums.astype(BF), w_in[128:256, :])
        + dot_nt(dst_sums.astype(BF), w_in[256:, :])
        + dot(hot, back)
    ).astype(BF)
    for copy in copies:
        copy.wait()


def added(parts):
    total = parts[0].astype(F32)
    for k in range(1, parts.shape[0]):
        total += parts[k].astype(F32)
    return total.astype(BF)


def plane_kernel(parts, ret_prev, ret_next, out):
    total = added(parts)
    for k in range(out.shape[0]):
        out[k] = total


def spread_kernel(parts, out):
    total = added(parts)
    for k in range(out.shape[0]):
        out[k] = total


def end_kernel(rows, edge_in, node_in, cedge_in, cnode_in, outs):
    edge_in[...] = rows[ROWS_EDGE:ROWS_NODE, :].astype(F32)
    node_in[...] = rows[ROWS_NODE:ROWS_CEDGE, :].astype(F32)
    cedge_in[...] = rows[ROWS_CEDGE:ROWS_CNODE, :].astype(F32)
    cnode_in[...] = rows[ROWS_CNODE:ROWS_OUTS, :].astype(F32)
    for k in range(5):
        outs[k] = rows[ROWS_OUTS + k * 128 : ROWS_OUTS + (k + 1) * 128, :].astype(F32)


def shift(value, axes, step):
    count = lax.axis_size(axes)
    return lax.ppermute(value, axes, [(i, (i + step) % count) for i in range(count)])


def cross(value):
    size = {axis: lax.axis_size(axis) for axis in EVERY}
    count = size["z"] * size["x"] * size["y"] * size["c"]
    pairs = []
    for i in range(count):
        core, y = i % size["c"], i // size["c"] % size["y"]
        to = (y + 1 - 2 * core) % size["y"]
        pairs.append((i, i + (to - y) * size["c"]))
    return lax.ppermute(value, EVERY, pairs)


def exchange(value, axes):
    return lax.all_to_all(value, axes, 0, 0)


def on_device(
    node, edge, src, dst, live, send, counts, pool, csrc, cdst, clive, csend, ccounts,
    w_edge, w_node, w_cedge, w_cnode, w_outs, cot, cot_edges,
):
    f32 = functools.partial(shape, dtype=F32)
    slots = (shape(SLOT, L), shape(SLOT, L))
    src, dst = src.reshape(EF // 128, 128), dst.reshape(EF // 128, 128)
    csrc, cdst = csrc.reshape(EC // 128, 128), cdst.reshape(EC // 128, 128)
    pool = pool.reshape(NF // 128, 128)
    send, csend = send.reshape(2, SLOT), csend.reshape(2, SLOT)
    edge_copies = (pltpu.VMEM((EF, L), BF), pltpu.SemaphoreType.DMA((EF // 128 // FINE_BLK,)))

    lives = call(
        begin_kernel, "begin", shape(8, 128, dtype=I32), (live, clive), 10**10, space=SMEM
    )
    to_prev, to_next = call(send_kernel, "send", slots, (lives, node, send, counts), 10**10)
    from_prev, from_next = shift(to_next, EVERY, 1), shift(to_prev, EVERY, -1)
    pre, side, src_part, dst_rows = call(
        pre_kernel, "pre", (f32(EF, L), shape(NC + CNT, L), shape(EF, L), shape(EF, L)),
        (node, w_edge, src, dst, edge, pool, cot),
    )
    new_edges, act, agg, act_node, refined, payload = call(
        fine_kernel, "fine",
        (shape(EF, L), f32(EF, L), shape(NF, L), f32(NF, L), shape(NF, L), shape(2 * NC + CNT, L)),
        (lives, pre, edge, node, from_prev, from_next, src, dst, w_edge, w_node, w_outs, pool, side),
        hbm_out=(0,), scratch=edge_copies,
    )
    total, part = call(
        pair_kernel, "pair", (shape(2 * NC + CNT, L), shape(PART, L)),
        (payload, shift(payload, "c", 1)), 10**6,
    )
    near, part = cross(total), shift(part, "y", 2)
    prepared = call(
        prep_kernel, "prep",
        (shape(EF, L), shape(EF, L), shape(EF, L), shape(EF, L), f32(EF, 1),
         shape(NF, L), f32(NF, L), f32(NF, L), f32(NF, 1)),
        (act, act_node, w_outs, src, from_prev, from_next, src_part),
    )
    joined = call(
        join_kernel, "join", shape(2 * NC + CNT, L), (total, near, part, prepared[-1]), 10**6,
        scratch=(pltpu.VMEM((2 * NC + CNT, L), F32),),
    )
    own, pooled_cot, divisor, to_prev, to_next = call(
        pool_kernel, "pool", (shape(NC, L), shape(NC, L), f32(NC, L)) + slots,
        (joined, shift(joined, "c", 1), csend, ccounts), 10**7,
    )
    cfrom_prev, cfrom_next = shift(to_next, GROUP, 1), shift(to_prev, GROUP, -1)
    cpre, cpre_node, grad_coarse = call(
        coarse_pre_kernel, "coarse_pre", (f32(EC, L), f32(NC, L), shape(NC, L)),
        (own, pooled_cot, csrc, cdst, w_cedge, w_cnode, w_outs),
    )
    coarse, grad_part, back_prev, back_next, sums, cagg, cga, pair_node, pair_edge, cga_edge = call(
        coarse_kernel, "coarse",
        (shape(NC, L), f32(NC, L)) + slots
        + (shape(2 * SLOT, L), shape(NC, L), shape(NC, L), shape(2, NC, L),
           shape(2, EC, L), shape(EC, L)),
        (lives, own, cpre, cpre_node, grad_coarse, cfrom_prev, cfrom_next, csrc, cdst,
         w_cedge, w_cnode, w_outs),
    )
    cret_prev, cret_next = shift(back_next, GROUP, 1), shift(back_prev, GROUP, -1)
    new_nodes, coarse_grads, grad_own = call(
        lift_kernel, "lift", (shape(NF, L), shape(896, L), f32(NC, L)),
        (own, pooled_cot, cfrom_prev, cfrom_next, coarse, grad_part, sums, cagg, cga, pair_node,
         pair_edge, cga_edge, csrc, cdst, w_cedge, refined, pool, w_outs),
    )
    grad_new, ga, grad_part, ga_node, grads, back_prev, back_next = call(
        fine_back_kernel, "fine_back",
        (shape(EF, L), shape(EF, L), shape(NF, L), shape(NF, L), shape(GRADS, L)) + slots,
        (lives, ccounts, grad_own, divisor, cret_prev, cret_next, csend, cot, pool, node, agg)
        + tuple(prepared)
        + (dst_rows, edge, cot_edges, src, dst, w_edge, w_node, w_outs, coarse_grads),
    )
    ret_prev, ret_next = shift(back_next, EVERY, 1), shift(back_prev, EVERY, -1)
    parts = exchange(grads.reshape(32, GRADS // 32, L), PLANE)
    spread = call(
        plane_kernel, "sum_plane", shape(8, GRADS // 32, L), (parts, ret_prev, ret_next), 10**6
    )
    grad_edges, grad_nodes = call(
        fine_rest_kernel, "fine_rest", (shape(EF, L), shape(NF, L)),
        (counts, grad_new, ga, grad_part, ga_node, src, dst, w_edge, w_node, ret_prev, ret_next,
         send),
        hbm_out=(0,), scratch=edge_copies,
    )
    parts = exchange(spread, "z")
    spread = call(spread_kernel, "sum_z", shape(32, GRADS // 32, L), (parts,), 10**6)
    rows = exchange(spread, PLANE).reshape(GRADS, L)
    weights = call(
        end_kernel, "end", (f32(384, L), f32(256, L), f32(256, L), f32(256, L), f32(5, L, L)),
        (rows,), 10**6,
    )
    return (new_nodes, new_edges, grad_nodes, grad_edges) + tuple(weights)


def solution(mesh):
    cube = Mesh(mesh.devices.reshape(8, 4, 4, 2), EVERY)
    fine, coarse = P(EVERY), P(GROUP)
    in_specs = (fine,) * 8 + (coarse,) * 5 + (P(),) * 5 + (fine,) * 2
    out_specs = (fine,) * 4 + (P(),) * 5
    return jax.shard_map(
        on_device, mesh=cube, in_specs=in_specs, out_specs=out_specs, check_vma=False
    )
```

```python
import functools

import jax
import jax.numpy as jnp
from jax import lax
from jax.experimental import pallas as pl
from jax.experimental.pallas import tpu as pltpu
from jax.sharding import Mesh
from jax.sharding import PartitionSpec as P

F32 = jnp.float32
BF = jnp.bfloat16
I32 = jnp.int32
EPS = 1e-05

L = 128
NF = 512
EF = 3072
NC = 256
EC = 1536
SLOT = 128
FINE_BLK = 8
COARSE_BLK = 12
CNT = 16
PART = 272
GRADS = 1792
ROWS_EDGE, ROWS_NODE, ROWS_CEDGE, ROWS_CNODE, ROWS_OUTS = 0, 384, 640, 896, 1152

EVERY = ("z", "x", "y", "c")
GROUP = ("z", "x")
PLANE = ("x", "y", "c")

VMEM = pl.BlockSpec(memory_space=pltpu.VMEM)
HBM = pl.BlockSpec(memory_space=pltpu.HBM)
SMEM = pl.BlockSpec(memory_space=pltpu.SMEM)


def call(kernel, name, out_shape, ins, flops=10**9, space=VMEM, hbm_out=(), scratch=()):
    size = sum(a.size * a.dtype.itemsize for a in ins)
    outs = out_shape if isinstance(out_shape, tuple) else (out_shape,)
    specs = tuple(HBM if k in hbm_out else VMEM for k in range(len(outs)))
    return pl.pallas_call(
        kernel,
        name=name,
        out_shape=out_shape,
        in_specs=[space] * len(ins),
        out_specs=specs if isinstance(out_shape, tuple) else specs[0],
        scratch_shapes=scratch,
        cost_estimate=pl.CostEstimate(flops=flops, bytes_accessed=size, transcendentals=0),
        compiler_params=pltpu.CompilerParams(vmem_limit_bytes=32 * 2**20),
    )(*ins)


def shape(*dims, dtype=BF):
    return jax.ShapeDtypeStruct(dims, dtype)


def dot(a, b):
    return jnp.dot(a, b, preferred_element_type=F32)


def dot_nt(a, b):
    return lax.dot_general(a, b, (((1,), (1,)), ((), ())), preferred_element_type=F32)


def dot_tn(a, b):
    return lax.dot_general(a, b, (((0,), (0,)), ((), ())), preferred_element_type=F32)


def mean(v):
    return jnp.mean(v, axis=-1, keepdims=True)


def columns(rows):
    pad = -rows.shape[0] % 8
    rows = rows.astype(F32)
    if pad:
        rows = jnp.concatenate([rows, jnp.zeros((pad, 128), F32)], 0)
    return rows.T.astype(I32)


def pick(cols, blocks, n):
    lane = lax.broadcasted_iota(I32, (128, n), 1)
    return jnp.concatenate(
        [jnp.where(lane == cols[:, j : j + 1], 1.0, 0.0).astype(BF) for j in blocks], 0
    )


def put(rows, blocks, n):
    line = lax.broadcasted_iota(I32, (n, 128), 0)
    return jnp.concatenate(
        [jnp.where(line == rows[j : j + 1, :], 1.0, 0.0).astype(BF) for j in blocks], 1
    )


def live_rows(rows, count):
    at = lax.broadcasted_iota(I32, rows.shape, 0) * 128 + lax.broadcasted_iota(I32, rows.shape, 1)
    return jnp.where(at < jnp.broadcast_to(count, rows.shape), rows, -1)


def live_slots(send, counts, axes):
    spot, last = 0, 1
    for axis in axes:
        spot = spot * lax.axis_size(axis) + lax.axis_index(axis)
        last = last * lax.axis_size(axis)
    there = ((spot > 0).astype(I32), (spot < last - 1).astype(I32))
    lane = lax.broadcasted_iota(I32, (1, SLOT), 1)
    return jnp.concatenate(
        [
            jnp.where(
                lane < jnp.broadcast_to(counts[0:1, s : s + 1], (1, SLOT)) * there[s],
                send[s : s + 1, :],
                -1,
            )
            for s in (0, 1)
        ],
        0,
    )


def even(axes):
    return lax.rem(lax.axis_index(axes[-1]), 2) == 0


def to_mates(prev, following, axes):
    here = even(axes)
    return (
        jnp.where(here, following, prev).astype(BF), jnp.where(here, prev, following).astype(BF)
    )


def by_side(first, second, axes):
    first, second, here = first[...].astype(F32), second[...].astype(F32), even(axes)
    return jnp.concatenate(
        [jnp.where(here, second, first), jnp.where(here, first, second)], 0
    ).astype(BF)


def sigmoid(a):
    return 1.0 / (1.0 + jnp.exp(-a))


def normed_of(hidden, w_second):
    outcome = dot(hidden, w_second)
    centred = outcome - mean(outcome)
    inv = lax.rsqrt(mean(centred * centred) + EPS)
    return centred * inv, inv


def activation(a):
    sig = sigmoid(a)
    return (a * sig).astype(BF), sig * (1.0 + a * (1.0 - sig))


def norm_back(grad, normed, inv):
    return (inv * (grad - mean(grad) - normed * mean(grad * normed))).astype(BF)


def forward(a, w_second):
    return normed_of((a * sigmoid(a)).astype(BF), w_second)[0]


def begin_kernel(live, clive, out):
    at = lax.broadcasted_iota(I32, out.shape, 0)
    out[...] = jnp.where(at == 0, live[0], jnp.where(at == 1, clive[0], 0))


def send_kernel(lives, node, send, counts, first, second):
    cols = columns(live_slots(send[...] + lives[2:4, :], counts, EVERY))
    rows = node[...]
    to_prev, to_next = dot(pick(cols, (0,), NF), rows), dot(pick(cols, (1,), NF), rows)
    first[...], second[...] = to_mates(to_prev, to_next, EVERY)


def pre_kernel(node, w_in, src, dst, edge, pool, cot, pre, side, src_rows, dst_rows):
    w = w_in[...]
    rows = node[...]
    src_table = jnp.concatenate([dot(rows, w[128:256]).astype(BF), rows], 1)
    dst_table = jnp.concatenate([dot(rows, w[256:384]).astype(BF), rows], 1)
    src_cols, dst_cols = columns(src[...]), columns(dst[...])
    for c in range(EF // 128 // FINE_BLK):
        blocks = range(c * FINE_BLK, (c + 1) * FINE_BLK)
        at = pl.ds(c * FINE_BLK * 128, FINE_BLK * 128)
        from_src = dot(pick(src_cols, blocks, NF), src_table)
        from_dst = dot(pick(dst_cols, blocks, NF), dst_table)
        pre[at, :] = dot(edge[at, :], w[:128]) + from_src[:, :L] + from_dst[:, :L]
        src_rows[at, :] = from_src[:, L:].astype(BF)
        dst_rows[at, :] = from_dst[:, L:].astype(BF)
    pool_hot = put(pool[...], range(NF // 128), NC)
    side[0:NC, :] = dot(pool_hot, cot[...]).astype(BF)
    count = dot_nt(jnp.ones((8, NF), BF), pool_hot)
    high = jnp.floor(count * (1.0 / 16.0))
    low = count - 16.0 * high
    at = lax.broadcasted_iota(I32, (CNT, 128), 0)
    lines = jnp.zeros((CNT, 128), F32)
    for k, v in enumerate((high[0:1, :128], high[0:1, 128:], low[0:1, :128], low[0:1, 128:])):
        lines = jnp.where(at == k, v, lines)
    side[NC : NC + CNT, :] = lines.astype(BF)


def fine_kernel(
    live, pre, edge, node, from_first, from_second, src, dst, w_in, w_node, w_outs, pool, side,
    new_edges_hbm, act, agg_out, act_node, refined, payload, new_edges, sems,
):
    halo = by_side(from_first, from_second, EVERY)
    table = dot(halo, w_in[128:256, :]).astype(BF)
    src_cols = columns(src[...] - NF)
    dst_rows = live_rows(dst[...], live[0:1, 0:1])
    w_second = w_outs[0]
    total = jnp.zeros((NF, L), F32)
    copies = []
    for c in range(EF // 128 // FINE_BLK):
        blocks = range(c * FINE_BLK, (c + 1) * FINE_BLK)
        at = pl.ds(c * FINE_BLK * 128, FINE_BLK * 128)
        a = pre[at, :] + dot(pick(src_cols, blocks, 2 * SLOT), table)
        act[at, :] = a
        message = forward(a, w_second)
        here = lax.broadcasted_iota(I32, message.shape, 0) + c * FINE_BLK * 128
        here = here < jnp.broadcast_to(live[0:1, 0:1], message.shape)
        rows = (edge[at, :].astype(F32) + jnp.where(here, message, 0.0)).astype(BF)
        new_edges[at, :] = rows
        copies.append(pltpu.make_async_copy(new_edges.at[at], new_edges_hbm.at[at], sems.at[c]))
        copies[-1].start()
        total += dot(put(dst_rows, blocks, NF), rows)
    agg = total.astype(BF)
    agg_out[...] = agg
    a = dot(node[...], w_node[:128, :]) + dot(agg, w_node[128:, :])
    act_node[...] = a
    rows = (node[...].astype(F32) + forward(a, w_outs[1])).astype(BF)
    refined[...] = rows
    payload[0:NC, :] = dot(put(pool[...], range(NF // 128), NC), rows).astype(BF)
    payload[NC:, :] = side[...]
    for copy in copies:
        copy.wait()


def pair_kernel(a, b, out, part):
    out[...] = (a[...].astype(F32) + b[...].astype(F32)).astype(BF)
    part[...] = out[pl.ds(pl.multiple_of(lax.axis_index("c") * NC, NC), PART), :]


def join_kernel(own, near, part, ahead, out, total):
    core = lax.axis_index("c")
    total[...] = near[...].astype(F32) + jnp.where(core == 0, own[...].astype(F32), 0.0)
    line = lax.broadcasted_iota(I32, (PART, L), 0)
    rows = jnp.where(line < NC + core * PART, part[...].astype(F32), 0.0)
    at = pl.ds(pl.multiple_of(core * NC, NC), PART)
    total[at, :] = total[at, :] + rows
    out[...] = total[...].astype(BF)


def pool_kernel(a, b, send, counts, own_out, cot_out, divisor, first, second):
    total = a[...].astype(F32) + b[...].astype(F32)
    lines = total[2 * NC :, :]
    count = 16.0 * lines[0:2, :] + lines[2:4, :]
    cols = jnp.concatenate([count, jnp.ones((6, 128), F32)], 0).T
    count = jnp.concatenate(
        [jnp.broadcast_to(cols[:, k : k + 1], (128, L)) for k in (0, 1)], 0
    )
    own = (total[:NC, :] / count).astype(BF)
    own_out[...] = own
    cot_out[...] = total[NC : 2 * NC, :].astype(BF)
    divisor[...] = count
    cols = columns(live_slots(send[...], counts, GROUP))
    to_prev, to_next = dot(pick(cols, (0,), NC), own), dot(pick(cols, (1,), NC), own)
    first[...], second[...] = to_mates(to_prev, to_next, GROUP)


def coarse_pre_kernel(own, cot, src, dst, w_in, w_node, w_outs, pre, pre_node, grad_coarse):
    rows = own[...]
    table = jnp.concatenate([dot(rows, w_in[128:, :]), dot(rows, w_in[:128, :])], 0).astype(BF)
    src_cols, dst_cols = columns(src[...]), columns(dst[...])
    for c in range(EC // 128 // COARSE_BLK):
        blocks = range(c * COARSE_BLK, (c + 1) * COARSE_BLK)
        hot = jnp.concatenate([pick(dst_cols, blocks, NC), pick(src_cols, blocks, NC)], 1)
        pre[pl.ds(c * COARSE_BLK * 128, COARSE_BLK * 128), :] = dot(hot, table)
    pre_node[...] = dot(rows, w_node[:128, :])
    grad_coarse[...] = dot_nt(cot[...], w_outs[4]).astype(BF)


def coarse_kernel(
    live, own, pre, pre_node, grad_coarse, from_first, from_second, src, dst, w_in, w_node, w_outs,
    coarse_out, grad_own, back_first, back_second, sums_out, agg_out, ga_out, pair_node, pair_edge, ga_edge,
):
    halo = by_side(from_first, from_second, GROUP)
    table = dot(halo, w_in[:128, :]).astype(BF)
    blocks = range(EC // 128)
    src_rows = src[...]
    dst_rows = live_rows(dst[...], live[1:2, 0:1])
    a = pre[...] + dot(pick(columns(src_rows - NC), blocks, 2 * SLOT), table)
    hidden, slope = activation(a)
    normed, inv = normed_of(hidden, w_outs[2])
    put_dst = put(dst_rows, blocks, NC)
    agg = dot(put_dst, normed.astype(BF)).astype(BF)
    agg_out[...] = agg
    a = pre_node[...] + dot(agg, w_node[128:, :])
    hidden_node, slope_node = activation(a)
    normed_node, inv_node = normed_of(hidden_node, w_outs[3])
    coarse_out[...] = (own[...].astype(F32) + normed_node).astype(BF)
    grad = grad_coarse[...].astype(F32)
    go = norm_back(grad, normed_node, inv_node)
    ga = (dot_nt(go, w_outs[3]) * slope_node).astype(BF)
    ga_out[...] = ga
    pair_node[0] = hidden_node
    pair_node[1] = go
    grad_total = grad + dot_nt(ga, w_node[:128, :])
    grad_agg = dot_nt(ga, w_node[128:, :]).astype(BF)
    grad = dot(pick(columns(dst_rows), blocks, NC), grad_agg)
    go = norm_back(grad, normed, inv)
    pair_edge[0] = hidden
    pair_edge[1] = go
    ga = (dot_nt(go, w_outs[2]) * slope).astype(BF)
    src_sums = dot(put(src_rows - NC, blocks, 2 * SLOT), ga).astype(BF)
    sums_out[...] = src_sums
    ga_edge[...] = ga
    grad_ext = dot_nt(src_sums, w_in[:128, :])
    back_first[...], back_second[...] = to_mates(grad_ext[:SLOT], grad_ext[SLOT:], GROUP)
    grad_own[...] = grad_total


def lift_kernel(
    own, cot, from_first, from_second, coarse, grad_part, sums, agg, ga, pair_node, pair_edge,
    ga_edge, src, dst, w_in, refined, pool, w_outs, new_nodes, grads, grad_own,
):
    part = 1.0 / 8.0
    rows = own[...]
    ext = jnp.concatenate([rows, by_side(from_first, from_second, GROUP)], 0)
    dst_sums = dot(put(dst[...], range(EC // 128), NC), ga_edge[...]).astype(BF)
    src_sums = dot(put(src[...], range(EC // 128), NC), ga_edge[...]).astype(BF)
    grad_own[...] = (
        grad_part[...] + dot_nt(src_sums, w_in[:128, :]) + dot_nt(dst_sums, w_in[128:, :])
    )
    src_sums = jnp.concatenate([src_sums, sums[...]], 0)
    lifted = dot(pick(columns(pool[...]), range(NF // 128), NC), coarse[...]).astype(BF)
    new_nodes[...] = (refined[...].astype(F32) + dot(lifted, w_outs[4])).astype(BF)
    grads[0:128, :] = (part * dot_tn(ext, src_sums)).astype(BF)
    grads[128:256, :] = (part * dot_tn(rows, dst_sums)).astype(BF)
    grads[256:384, :] = (part * dot_tn(rows, ga[...])).astype(BF)
    grads[384:512, :] = (part * dot_tn(agg[...], ga[...])).astype(BF)
    grads[512:640, :] = (part * dot_tn(pair_edge[0], pair_edge[1])).astype(BF)
    grads[640:768, :] = (part * dot_tn(pair_node[0], pair_node[1])).astype(BF)
    grads[768:896, :] = (part * dot_tn(coarse[...], cot[...])).astype(BF)


def prep_kernel(
    act, act_node, w_outs, src, from_first, from_second, src_part, src_rows, hidden_out, slope_out, normed_out, inv_out, hidden_node, slope_node,
    normed_node, inv_node,
):
    halo = by_side(from_first, from_second, EVERY)
    src_cols = columns(src[...] - NF)
    for c in range(EF // 128 // FINE_BLK):
        at = pl.ds(c * FINE_BLK * 128, FINE_BLK * 128)
        blocks = range(c * FINE_BLK, (c + 1) * FINE_BLK)
        src_rows[at, :] = src_part[at, :] + dot(pick(src_cols, blocks, 2 * SLOT), halo).astype(BF)
        hidden, slope = activation(act[at, :])
        normed, inv = normed_of(hidden, w_outs[0])
        hidden_out[at, :] = hidden
        slope_out[at, :] = slope.astype(BF)
        normed_out[at, :] = normed.astype(BF)
        inv_out[at, :] = inv
    hidden, slope = activation(act_node[...])
    normed, inv = normed_of(hidden, w_outs[1])
    hidden_node[...] = hidden
    slope_node[...] = slope
    normed_node[...] = normed
    inv_node[...] = inv


def fine_back_kernel(
    lives, counts, grad_own, divisor, ret_first, ret_second, send, cot, pool, node, agg, src_rows,
    hidden, slope, normed, inv, hidden_node, slope_node, normed_node, inv_node, dst_rows, edge,
    cot_edges, src, dst, w_in, w_node, w_outs, coarse_grads, grad_new, ga_out, grad_node, ga_node,
    grads_hbm, back_first, back_second, grads, sems,
):
    back = by_side(ret_first, ret_second, GROUP)
    hot = put(live_slots(send[...], counts, GROUP), (0, 1), NC)
    grad_pool = (grad_own[...] + dot(hot, back)).astype(BF).astype(F32) / divisor[...]
    pooled = dot(pick(columns(pool[...]), range(NF // 128), NC), grad_pool.astype(BF))
    grad_refined = (cot[...].astype(F32) + pooled).astype(BF).astype(F32)
    go = norm_back(grad_refined, normed_node[...], inv_node[...])
    ga = (dot_nt(go, w_outs[1]) * slope_node[...]).astype(BF)
    grad_agg = dot_nt(ga, w_node[128:, :]).astype(BF)
    grads[384:512, :] = dot_tn(node[...], ga).astype(BF)
    grads[512:640, :] = dot_tn(agg[...], ga).astype(BF)
    grads[1280:1408, :] = dot_tn(hidden_node[...], go).astype(BF)
    grad_node[...] = grad_refined.astype(BF)
    ga_node[...] = ga
    grads[640:1152, :] = coarse_grads[0:512, :]
    grads[1408:1792, :] = coarse_grads[512:896, :]
    copies = [
        pltpu.make_async_copy(grads.at[pl.ds(a, n)], grads_hbm.at[pl.ds(a, n)], sems.at[k])
        for k, (a, n) in enumerate(((384, 768), (1280, 512), (0, 384), (1152, 128)))
    ]
    copies[0].start()
    copies[1].start()
    dst_cols = columns(live_rows(dst[...], lives[0:1, 0:1]))
    slot_rows = src[...] - NF
    sums = jnp.zeros((2 * SLOT, L), F32)
    w_second = w_outs[0]
    totals = [jnp.zeros((L, L), F32) for _ in range(4)]
    for c in range(EF // 128 // FINE_BLK):
        blocks = range(c * FINE_BLK, (c + 1) * FINE_BLK)
        at = pl.ds(c * FINE_BLK * 128, FINE_BLK * 128)
        gathered = dot(pick(dst_cols, blocks, NF), grad_agg)
        total = (cot_edges[at, :].astype(F32) + gathered).astype(BF)
        grad_new[at, :] = total
        here = lax.broadcasted_iota(I32, total.shape, 0) + c * FINE_BLK * 128
        here = here < jnp.broadcast_to(lives[0:1, 0:1], total.shape)
        total = jnp.where(here, total.astype(F32), 0.0)
        go = norm_back(total, normed[at, :].astype(F32), inv[at, :])
        ga = (dot_nt(go, w_second) * slope[at, :].astype(F32)).astype(BF)
        ga_out[at, :] = ga
        for k, rows in enumerate((edge, src_rows, dst_rows)):
            totals[k] += dot_tn(rows[at, :], ga)
        totals[3] += dot_tn(hidden[at, :], go)
    for k in range(3):
        grads[k * 128 : (k + 1) * 128, :] = totals[k].astype(BF)
    grads[1152:1280, :] = totals[3].astype(BF)
    copies[2].start()
    copies[3].start()
    for c in range(EF // 128 // FINE_BLK):
        blocks = range(c * FINE_BLK, (c + 1) * FINE_BLK)
        at = pl.ds(c * FINE_BLK * 128, FINE_BLK * 128)
        sums += dot(put(slot_rows, blocks, 2 * SLOT), ga_out[at, :])
    sums = dot_nt(sums.astype(BF), w_in[128:256, :])
    back_first[...], back_second[...] = to_mates(sums[:SLOT], sums[SLOT:], EVERY)
    for copy in copies:
        copy.wait()


def fine_rest_kernel(
    counts, grad_new, ga, grad_part, ga_node, src, dst, w_in, w_node, ret_first, ret_second, send,
    grad_edges_hbm,
    grad_nodes, grad_edges, sems,
):
    src_rows, dst_rows = src[...], dst[...]
    src_sums = jnp.zeros((NF, L), F32)
    dst_sums = jnp.zeros((NF, L), F32)
    copies = []
    for c in range(EF // 128 // FINE_BLK):
        blocks = range(c * FINE_BLK, (c + 1) * FINE_BLK)
        at = pl.ds(c * FINE_BLK * 128, FINE_BLK * 128)
        rows = ga[at, :]
        grad_edges[at, :] = (
            grad_new[at, :].astype(F32) + dot_nt(rows, w_in[:128, :])
        ).astype(BF)
        copies.append(pltpu.make_async_copy(grad_edges.at[at], grad_edges_hbm.at[at], sems.at[c]))
        copies[-1].start()
        src_sums += dot(put(src_rows, blocks, NF), rows)
        dst_sums += dot(put(dst_rows, blocks, NF), rows)
    back = by_side(ret_first, ret_second, EVERY)
    hot = put(live_slots(send[...], counts, EVERY), (0, 1), NF)
    grad_nodes[...] = (
        grad_part[...].astype(F32)
        + dot_nt(ga_node[...], w_node[:128, :])
        + dot_nt(src_sums.astype(BF), w_in[128:256, :])
        + dot_nt(dst_sums.astype(BF), w_in[256:, :])
        + dot(hot, back)
    ).astype(BF)
    for copy in copies:
        copy.wait()


def added(parts):
    total = parts[0].astype(F32)
    for k in range(1, parts.shape[0]):
        total += parts[k].astype(F32)
    return total.astype(BF)


def plane_kernel(parts, ret_first, ret_second, out):
    total = added(parts)
    for k in range(out.shape[0]):
        out[k] = total


def spread_kernel(parts, out):
    total = added(parts)
    for k in range(out.shape[0]):
        out[k] = total


def end_kernel(rows, edge_in, node_in, cedge_in, cnode_in, outs):
    edge_in[...] = rows[ROWS_EDGE:ROWS_NODE, :].astype(F32)
    node_in[...] = rows[ROWS_NODE:ROWS_CEDGE, :].astype(F32)
    cedge_in[...] = rows[ROWS_CEDGE:ROWS_CNODE, :].astype(F32)
    cnode_in[...] = rows[ROWS_CNODE:ROWS_OUTS, :].astype(F32)
    for k in range(5):
        outs[k] = rows[ROWS_OUTS + k * 128 : ROWS_OUTS + (k + 1) * 128, :].astype(F32)


def shift(value, axes, step):
    count = lax.axis_size(axes)
    return lax.ppermute(value, axes, [(i, (i + step) % count) for i in range(count)])


def swap_mates(first, second, axes):
    count = lax.axis_size(axes)
    step = [1 - 2 * (i % 2) for i in range(count)]
    return (
        lax.ppermute(first, axes, [(i, i + step[i]) for i in range(count)]),
        lax.ppermute(second, axes, [(i, (i - step[i]) % count) for i in range(count)]),
    )


def cross(value):
    size = {axis: lax.axis_size(axis) for axis in EVERY}
    count = size["z"] * size["x"] * size["y"] * size["c"]
    pairs = []
    for i in range(count):
        core, y = i % size["c"], i // size["c"] % size["y"]
        to = (y + 1 - 2 * core) % size["y"]
        pairs.append((i, i + (to - y) * size["c"]))
    return lax.ppermute(value, EVERY, pairs)


def exchange(value, axes):
    return lax.all_to_all(value, axes, 0, 0)


def on_device(
    node, edge, src, dst, live, send, counts, pool, csrc, cdst, clive, csend, ccounts,
    w_edge, w_node, w_cedge, w_cnode, w_outs, cot, cot_edges,
):
    f32 = functools.partial(shape, dtype=F32)
    slots = (shape(SLOT, L), shape(SLOT, L))
    src, dst = src.reshape(EF // 128, 128), dst.reshape(EF // 128, 128)
    csrc, cdst = csrc.reshape(EC // 128, 128), cdst.reshape(EC // 128, 128)
    pool = pool.reshape(NF // 128, 128)
    send, csend = send.reshape(2, SLOT), csend.reshape(2, SLOT)
    edge_copies = (pltpu.VMEM((EF, L), BF), pltpu.SemaphoreType.DMA((EF // 128 // FINE_BLK,)))

    lives = call(
        begin_kernel, "begin", shape(8, 128, dtype=I32), (live, clive), 10**10, space=SMEM
    )
    to_first, to_second = call(send_kernel, "send", slots, (lives, node, send, counts), 10**10)
    from_first, from_second = swap_mates(to_first, to_second, EVERY)
    pre, side, src_part, dst_rows = call(
        pre_kernel, "pre", (f32(EF, L), shape(NC + CNT, L), shape(EF, L), shape(EF, L)),
        (node, w_edge, src, dst, edge, pool, cot),
    )
    new_edges, act, agg, act_node, refined, payload = call(
        fine_kernel, "fine",
        (shape(EF, L), f32(EF, L), shape(NF, L), f32(NF, L), shape(NF, L), shape(2 * NC + CNT, L)),
        (lives, pre, edge, node, from_first, from_second, src, dst, w_edge, w_node, w_outs, pool, side),
        hbm_out=(0,), scratch=edge_copies,
    )
    total, part = call(
        pair_kernel, "pair", (shape(2 * NC + CNT, L), shape(PART, L)),
        (payload, shift(payload, "c", 1)), 10**6,
    )
    near, part = cross(total), shift(part, "y", 2)
    prepared = call(
        prep_kernel, "prep",
        (shape(EF, L), shape(EF, L), shape(EF, L), shape(EF, L), f32(EF, 1),
         shape(NF, L), f32(NF, L), f32(NF, L), f32(NF, 1)),
        (act, act_node, w_outs, src, from_first, from_second, src_part),
    )
    joined = call(
        join_kernel, "join", shape(2 * NC + CNT, L), (total, near, part, prepared[-1]), 10**6,
        scratch=(pltpu.VMEM((2 * NC + CNT, L), F32),),
    )
    own, pooled_cot, divisor, to_first, to_second = call(
        pool_kernel, "pool", (shape(NC, L), shape(NC, L), f32(NC, L)) + slots,
        (joined, shift(joined, "c", 1), csend, ccounts), 10**7,
    )
    cfrom_first, cfrom_second = swap_mates(to_first, to_second, GROUP)
    cpre, cpre_node, grad_coarse = call(
        coarse_pre_kernel, "coarse_pre", (f32(EC, L), f32(NC, L), shape(NC, L)),
        (own, pooled_cot, csrc, cdst, w_cedge, w_cnode, w_outs),
    )
    coarse, grad_part, back_first, back_second, sums, cagg, cga, pair_node, pair_edge, cga_edge = call(
        coarse_kernel, "coarse",
        (shape(NC, L), f32(NC, L)) + slots
        + (shape(2 * SLOT, L), shape(NC, L), shape(NC, L), shape(2, NC, L),
           shape(2, EC, L), shape(EC, L)),
        (lives, own, cpre, cpre_node, grad_coarse, cfrom_first, cfrom_second, csrc, cdst,
         w_cedge, w_cnode, w_outs),
    )
    cret_first, cret_second = swap_mates(back_first, back_second, GROUP)
    new_nodes, coarse_grads, grad_own = call(
        lift_kernel, "lift", (shape(NF, L), shape(896, L), f32(NC, L)),
        (own, pooled_cot, cfrom_first, cfrom_second, coarse, grad_part, sums, cagg, cga, pair_node,
         pair_edge, cga_edge, csrc, cdst, w_cedge, refined, pool, w_outs),
    )
    grad_new, ga, grad_part, ga_node, grads, back_first, back_second = call(
        fine_back_kernel, "fine_back",
        (shape(EF, L), shape(EF, L), shape(NF, L), shape(NF, L), shape(GRADS, L)) + slots,
        (lives, ccounts, grad_own, divisor, cret_first, cret_second, csend, cot, pool, node, agg)
        + tuple(prepared)
        + (dst_rows, edge, cot_edges, src, dst, w_edge, w_node, w_outs, coarse_grads),
        hbm_out=(4,), scratch=(pltpu.VMEM((GRADS, L), BF), pltpu.SemaphoreType.DMA((4,))),
    )
    ret_first, ret_second = swap_mates(back_first, back_second, EVERY)
    parts = exchange(grads.reshape(32, GRADS // 32, L), PLANE)
    spread = call(
        plane_kernel, "sum_plane", shape(8, GRADS // 32, L), (parts, ret_first, ret_second), 10**6
    )
    grad_edges, grad_nodes = call(
        fine_rest_kernel, "fine_rest", (shape(EF, L), shape(NF, L)),
        (counts, grad_new, ga, grad_part, ga_node, src, dst, w_edge, w_node, ret_first, ret_second,
         send),
        hbm_out=(0,), scratch=edge_copies,
    )
    parts = exchange(spread, "z")
    spread = call(spread_kernel, "sum_z", shape(32, GRADS // 32, L), (parts,), 10**6)
    rows = exchange(spread, PLANE).reshape(GRADS, L)
    weights = call(
        end_kernel, "end", (f32(384, L), f32(256, L), f32(256, L), f32(256, L), f32(5, L, L)),
        (rows,), 10**6,
    )
    return (new_nodes, new_edges, grad_nodes, grad_edges) + tuple(weights)


def solution(mesh):
    cube = Mesh(mesh.devices.reshape(8, 4, 4, 2), EVERY)
    fine, coarse = P(EVERY), P(GROUP)
    in_specs = (fine,) * 8 + (coarse,) * 5 + (P(),) * 5 + (fine,) * 2
    out_specs = (fine,) * 4 + (P(),) * 5
    return jax.shard_map(
        on_device, mesh=cube, in_specs=in_specs, out_specs=out_specs, check_vma=False
    )
```
